128 devices in a mesh: seq: 8 (over z_lo, x), batch: 16 (over y, z_hi, core).
Axes of the slice: x: 4, y: 4, z: 4 (z_hi: 2, z_lo: 2; z = z_hi * 2 + z_lo), core: 2. Of those that a mesh axis runs over, the one named last changes fastest.
Arguments:
- tokens: bfloat16 [16, 1024, 768], P('batch', 'seq'), may hold values from -6 to 6
- seg_lengths: int32 [16, 5], P('batch'), may hold values from 16 to 960, as said below
- cotangent: bfloat16 [16, 1024, 768], P('batch', 'seq'), may hold values from -6 to 6
- norm_attn: float32 [2, 768], replicated, may hold values from 0.5 to 1.5
- w_query: bfloat16 [2, 768, 768], replicated, may hold values from -0.21875 to 0.21875
- w_key: bfloat16 [2, 768, 768], replicated, may hold values from -0.21875 to 0.21875
- w_value: bfloat16 [2, 768, 768], replicated, may hold values from -0.21875 to 0.21875
- w_out: bfloat16 [2, 768, 768], replicated, may hold values from -1.75 to 1.75
- norm_ffn: float32 [2, 768], replicated, may hold values from 0.5 to 1.5
- w_gate: bfloat16 [2, 768, 2048], replicated, may hold values from -0.21875 to 0.21875
- w_up: bfloat16 [2, 768, 2048], replicated, may hold values from -0.21875 to 0.21875
- w_down: bfloat16 [2, 2048, 768], replicated, may hold values from -0.125 to 0.125
Outputs:
- activations: bfloat16 [16, 1024, 768], P('batch', 'seq')
- grad_tokens: float32 [16, 1024, 768], P('batch', 'seq')
- grad_norm_attn: float32 [2, 768], P(None, ('seq', 'batch'))
- grad_query: float32 [2, 768, 768], P(None, ('seq', 'batch'))
- grad_key: float32 [2, 768, 768], P(None, ('seq', 'batch'))
- grad_value: float32 [2, 768, 768], P(None, ('seq', 'batch'))
- grad_out: float32 [2, 768, 768], P(None, ('seq', 'batch'))
- grad_norm_ffn: float32 [2, 768], P(None, ('seq', 'batch'))
- grad_gate: float32 [2, 768, 2048], P(None, ('seq', 'batch'))
- grad_up: float32 [2, 768, 2048], P(None, ('seq', 'batch'))
- grad_down: float32 [2, 2048, 768], P(None, ('seq', 'batch'))
The draws below stay inside these ranges and needn't reach their ends.
Inputs may be any that keep to these rules, and one draw needn't show every extreme that they name: `seg_lengths`: each row's 5 lengths sum to 1024; in every row exactly one segment, at a place drawn per row, begins within the row's first 128 tokens and ends within its last 128; every other one is shorter than 32.
All inputs are finite; a program needn't handle non-finite values.
Results may differ from the reference program's by a relative error of at most 0.02.
Values may be sent and summed in bfloat16 or wider, within the bound.
No kernel may reach another device: no remote copies, remote signals or barrier semaphores. Data moves between devices by JAX's collectives and lax.ppermute only.
A program may use at most 320 MiB of HBM per device.

```python
import math
import jax
import jax.numpy as jnp
from jax import lax

D = 768
HEADS = 12
HEAD_DIM = 64
FF = 2048
TOK_DEV = 128
LAYERS = 2
SEGS = 5
GRID = 16
ROW_LEN = 1024
ROWS = 16


def draw_seg_lengths(key, part):
    key = jax.random.fold_in(key, 7)
    key_short, key_slot = jax.random.split(key)
    shorts = jax.random.randint(key_short, (ROWS, SEGS - 1), TOK_DEV // 8, TOK_DEV // 4)
    shorts = shorts.at[:, 0].set(TOK_DEV // 8)
    first_row = jnp.arange(ROWS)[:, None] == 0
    shorts = jnp.where(first_row, TOK_DEV // 8, shorts)
    slot = jax.random.randint(key_slot, (ROWS, 1), 0, SEGS)
    longest = ROW_LEN - jnp.sum(shorts, axis=1, keepdims=True)
    column = jnp.arange(SEGS)[None, :]
    picked = jnp.clip(jnp.where(column < slot, column, column - 1), 0, SEGS - 2)
    taken = jnp.take_along_axis(shorts, jnp.broadcast_to(picked, (ROWS, SEGS)), axis=1)
    return jnp.where(column == slot, longest, taken).astype(jnp.int32)


def block_scale(rng, dims, cuts, least, high):
    level = 1.0
    for dim, blocks in cuts:
        draws = jax.random.uniform(jax.random.fold_in(jax.random.fold_in(rng, 6), dim), (blocks,), jnp.float32, least / len(cuts), high / len(cuts))
        level = level * jnp.repeat(jnp.exp(draws), dims[dim] // blocks).reshape((-1,) + (1,) * (len(dims) - 1 - dim))
    return level


def normal_values(rng, extent, spread, reach, shards=(), kind=jnp.bfloat16):
    values = spread * jax.random.normal(rng, extent, jnp.float32)
    if shards:
        values = values * block_scale(rng, extent, shards, -0.22, 0.18)
    return jnp.clip(values, -reach, reach).astype(kind)


def setup_inputs(seed: int = 0) -> dict:
    streams_of = jax.random.split(jax.random.key(seed), 13)
    return {
        "tokens": normal_values(streams_of[0], (ROWS, ROW_LEN, D), 1.0, 6.0, ((0, 16), (1, 8))),
        "seg_lengths": draw_seg_lengths(jax.random.fold_in(streams_of[12], 71), 0),
        "cotangent": normal_values(streams_of[2], (ROWS, ROW_LEN, D), 1.0, 6.0, ((0, 16), (1, 8))),
        "norm_attn": jnp.clip(1.0 + 0.1 * jax.random.normal(streams_of[3], (LAYERS, D), jnp.float32), 0.5, 1.5),
        "w_query": normal_values(streams_of[4], (LAYERS, D, D), D ** -0.5, 0.21875),
        "w_key": normal_values(streams_of[5], (LAYERS, D, D), D ** -0.5, 0.21875),
        "w_value": normal_values(streams_of[6], (LAYERS, D, D), D ** -0.5, 0.21875),
        "w_out": normal_values(streams_of[7], (LAYERS, D, D), (D // 64) ** -0.5, 1.75),
        "norm_ffn": jnp.clip(1.0 + 0.1 * jax.random.normal(streams_of[8], (LAYERS, D), jnp.float32), 0.5, 1.5),
        "w_gate": normal_values(streams_of[9], (LAYERS, D, FF), D ** -0.5, 0.21875),
        "w_up": normal_values(streams_of[10], (LAYERS, D, FF), D ** -0.5, 0.21875),
        "w_down": normal_values(streams_of[11], (LAYERS, FF, D), FF ** -0.5, 0.125),
    }


EPS = 1e-05
score_scale = 0.125
HIGH = lax.Precision.HIGHEST

@jax.custom_vjp
def low(v):
    return lax.optimization_barrier(v.astype(jnp.bfloat16)).astype(jnp.float32)

@jax.custom_vjp
def low_back(v):
    return v

def low_keep(v):
    return (low(v), None)

def low_pass(kept, grad):
    return (grad,)

def back_keep(v):
    return (v, None)

def back_low(kept, grad):
    return (low(grad),)
low.defvjp(low_keep, low_pass)
low_back.defvjp(back_keep, back_low)

def matmul(left, right):
    return jnp.dot(left, right, precision=HIGH, preferred_element_type=jnp.float32)

def layout(seg_lengths, first, count):
    ends = jnp.cumsum(seg_lengths).astype(jnp.int32)
    starts = (ends - seg_lengths).astype(jnp.int32)
    places = (first + jnp.arange(count, dtype=jnp.int32)).astype(jnp.int32)
    member = (places[:, None] >= starts[None, :]) & (places[:, None] < ends[None, :])
    numbers = jnp.arange(seg_lengths.shape[0], dtype=jnp.int32)
    segment = lax.optimization_barrier(jnp.sum(jnp.where(member, numbers[None, :], 0), axis=1)).astype(jnp.int32)
    inside = (places - lax.optimization_barrier(jnp.sum(jnp.where(member, starts[None, :], 0), axis=1))).astype(jnp.int32)
    return (segment, inside, places)

def rope_tables(inside):
    offset = jnp.maximum(inside - 1, 0).astype(jnp.int32)
    grid_rows = (offset // GRID).astype(jnp.float32)
    grid_cols = (offset % GRID).astype(jnp.float32)
    live = (inside > 0).astype(jnp.float32)
    freqs = 10000.0 ** (-4.0 * jnp.arange(HEAD_DIM // 4, dtype=jnp.float32) / HEAD_DIM)
    angles = jnp.concatenate([grid_rows[:, None] * freqs[None, :], grid_cols[:, None] * freqs[None, :]], axis=1)
    angles = angles * live[:, None]
    return (jnp.cos(angles), jnp.sin(angles))

def rotate(values, cosine, sine):
    count = values.shape[0]
    pairs = values.reshape(count, HEADS, HEAD_DIM // 2, 2)
    former = pairs[..., 0]
    latter = pairs[..., 1]
    cos_part = cosine[:, None, :]
    sin_part = sine[:, None, :]
    turned = jnp.stack([former * cos_part - latter * sin_part, former * sin_part + latter * cos_part], axis=-1)
    return turned.reshape(count, HEADS * HEAD_DIM)

def normalize(values, gain):
    return values * lax.rsqrt(lax.optimization_barrier(jnp.mean(values * values, axis=-1, keepdims=True)) + EPS) * gain

def attention(query, key, value, segment, places):
    count = query.shape[0]
    block = math.gcd(count, 512)
    heads_k = key.reshape(count, HEADS, HEAD_DIM)
    heads_v = value.reshape(count, HEADS, HEAD_DIM)

    def one_block(pieces):
        heads_q, block_segment, block_places = pieces
        raw = jnp.einsum('qhd,khd->hqk', heads_q, heads_k, precision=HIGH) * score_scale
        raw = low_back(raw)
        allowed = (block_segment[:, None] == segment[None, :]) & (places[None, :] <= block_places[:, None])
        masked = jnp.where(allowed[None], raw, -1e+30)
        top = lax.optimization_barrier(jnp.max(masked, axis=-1, keepdims=True))
        expd = jnp.exp(masked - top)
        probs = low(expd / lax.optimization_barrier(jnp.sum(expd, axis=-1, keepdims=True)))
        return jnp.einsum('hqk,khd->qhd', probs, heads_v, precision=HIGH)
    outputs = lax.map(jax.checkpoint(one_block), (query.reshape(count // block, block, HEADS, HEAD_DIM), segment.reshape(count // block, block), places.reshape(count // block, block)))
    return outputs.reshape(count, HEADS * HEAD_DIM)

def layer(current, weights, cosine, sine, segment, places):
    gain_attn, wq, wk, wv, wo, gain_ffn, wg, wu, wd = weights
    normed = low(normalize(current, gain_attn))
    query = low(rotate(low_back(matmul(normed, wq)), cosine, sine))
    key = low(rotate(low_back(matmul(normed, wk)), cosine, sine))
    value = low(low_back(matmul(normed, wv)))
    mixed = low_back(low(attention(query, key, value, segment, places)))
    middle = current + low_back(matmul(mixed, wo))
    normed2 = low(normalize(middle, gain_ffn))
    gate = low_back(matmul(normed2, wg))
    upper = low_back(matmul(normed2, wu))
    hidden = low(gate / (1.0 + jnp.exp(-gate)) * upper)
    return middle + low_back(matmul(hidden, wd))

def reference(tokens, seg_lengths, cotangent, norm_attn, w_query, w_key, w_value, w_out, norm_ffn, w_gate, w_up, w_down):
    params = tuple((p.astype(jnp.float32) for p in (norm_attn, w_query, w_key, w_value, w_out, norm_ffn, w_gate, w_up, w_down)))
    zeros = tuple((jnp.zeros_like(p) for p in params))

    def one_row(totals, row):
        row_tokens, row_lengths, row_cotangent = row
        segment, inside, places = layout(row_lengths, 0, ROW_LEN)
        cosine, sine = rope_tables(inside)

        def run(values, weights):
            for depth in range(LAYERS):
                values = layer(values, tuple((w[depth] for w in weights)), cosine, sine, segment, places)
            return values
        result, pull = jax.vjp(run, row_tokens.astype(jnp.float32), params)
        grad_input, grad_params = pull(row_cotangent.astype(jnp.float32))
        totals = tuple((total + piece for total, piece in zip(totals, grad_params)))
        return (totals, (result.astype(jnp.bfloat16), grad_input))
    totals, (results, grad_inputs) = lax.scan(one_row, zeros, (tokens, seg_lengths, cotangent))
    return (results, grad_inputs, totals[0], totals[1], totals[2], totals[3], totals[4], totals[5], totals[6], totals[7], totals[8])
```

```python
import jax
import jax.numpy as jnp
import numpy as np
from jax import lax
from jax.experimental import pallas as pl
from jax.experimental.pallas import tpu as pltpu
from jax.sharding import PartitionSpec as P

D = 768
HEADS = 12
HEAD_DIM = 64
FF = 2048
TOK = 128
ROW = 1024
GRID = 16
GROUP = 3 * HEAD_DIM
OFF = {"k": 0, "v": GROUP, "q": 2 * GROUP}
EPS = 1e-05
AXES = ("seq", "batch")
BF = jnp.bfloat16
F32 = jnp.float32
MIB = 1 << 20


def place(flat):
    seq, batch = divmod(flat, 16)
    z_lo, x = divmod(seq, 4)
    y, rest = divmod(batch, 4)
    z_hi, core = divmod(rest, 2)
    return dict(x=x, y=y, z=z_hi * 2 + z_lo, c=core)


def flat_of(p):
    z_hi, z_lo = divmod(p["z"], 2)
    return (z_lo * 4 + p["x"]) * 16 + p["y"] * 4 + z_hi * 2 + p["c"]


def permutation(move):
    pairs = []
    for flat in range(128):
        p = place(flat)
        move(p)
        pairs.append((flat, flat_of(p)))
    return pairs


def move_relocate(p):
    z_hi, z_lo = divmod(p["z"], 2)
    core = p["c"]
    p["z"] = z_hi * 2 + core
    p["c"] = z_lo ^ (1 if p["x"] >= 2 else 0)


RELOCATE = permutation(move_relocate)
RESTORE = sorted((dst, src) for src, dst in RELOCATE)


def move_core(p):
    p["c"] ^= 1


CORE = permutation(move_core)


def shift_x(by):
    def move(p):
        p["x"] = (p["x"] + by) % 4

    return permutation(move)


SHIFT_X = {d: shift_x(d) for d in (1, 2, 3)}


def pair_step(axis, step):
    def move(p):
        at = p[axis]
        p[axis] = at ^ 1 if (p["c"] == 0) == (step == 0) else 3 - at

    return permutation(move)


PAIR = {(axis, step): pair_step(axis, step) for axis in "xyz" for step in (0, 1)}


def send(value, pairs):
    return lax.ppermute(value, AXES, pairs)


RING_ORDER = {0: (0, 3, 1, 2), 1: (0, 1, 2, 3)}


def block_order(axes):
    order = []
    for core in (0, 1):
        ring = RING_ORDER[core]
        for a in ring:
            for b in ring:
                for c in ring:
                    order.append(flat_of({axes[0]: a, axes[1]: b, axes[2]: c, "c": core}))
    return np.array(order)


def row_order(axes, rows):
    return (block_order(axes)[:, None] * rows + np.arange(rows)[None, :]).reshape(-1)


def one_hot(axes):
    order = row_order(axes, 6)
    return jnp.asarray(np.eye(D, dtype=np.float32)[order], dtype=BF)


def mm(left, right):
    return jnp.dot(left, right, preferred_element_type=F32)


def mm_rt(left, right):
    return lax.dot_general(left, right, (((1,), (1,)), ((), ())), preferred_element_type=F32)


def mm_lt(left, right):
    return lax.dot_general(left, right, (((0,), (0,)), ((), ())), preferred_element_type=F32)


VMEM = pl.BlockSpec(memory_space=pltpu.VMEM)
SMEM = pl.BlockSpec(memory_space=pltpu.SMEM)
HBM = pl.BlockSpec(memory_space=pltpu.HBM)


def pinned(*weights):
    return tuple(pltpu.with_memory_space_constraint(w, pltpu.HBM) for w in weights)


def sds(shape, kind):
    return jax.ShapeDtypeStruct(shape, kind)


def turn(values, cos, sin):
    lane = lax.broadcasted_iota(jnp.int32, (TOK, 128), 1)
    even = lane % 2 == 0
    parts = []
    for t in range(6):
        v = values[:, 128 * t : 128 * t + 128]
        swapped = jnp.where(even, pltpu.roll(v, 127, 1), pltpu.roll(v, 1, 1))
        parts.append(v * cos + swapped * sin)
    return jnp.concatenate(parts, axis=1)


def norm_factor(values):
    return lax.rsqrt(jnp.mean(values * values, axis=-1, keepdims=True) + EPS)


def project_kernel(depth, me, x, gain, cos, sin, wq, wk, wv, o0, o1, o2, o3, normed_ref, wbuf, groups, sems):
    copies = [
        pltpu.make_async_copy(w.at[depth], wbuf.at[i], sems.at[i]) for i, w in enumerate((wk, wv, wq))
    ]
    for copy in copies:
        copy.start()
    values = x[...]
    normed = (values * norm_factor(values) * gain[...]).astype(BF)
    normed_ref[...] = normed
    for i in range(3):
        copies[i].wait()
        y = mm(normed, wbuf[i])
        if i != 1:
            y = turn(y, cos[...], sin[...])
        y = y.astype(BF)
        for g in range(4):
            groups[g, :, GROUP * i : GROUP * i + GROUP] = y[:, GROUP * g : GROUP * g + GROUP]
    mine = me[0]
    for d, o in enumerate((o0, o1, o2, o3)):
        o[...] = groups[lax.rem(mine + d, 4)]


def project(depth, me, x, gain, cos, sin, wq, wk, wv):
    return pl.pallas_call(
        lambda *refs: project_kernel(depth, *refs),
        out_shape=[sds((TOK, 3 * GROUP), BF)] * 4 + [sds((TOK, D), BF)],
        in_specs=[SMEM, VMEM, VMEM, VMEM, VMEM, HBM, HBM, HBM],
        out_specs=[VMEM] * 5,
        scratch_shapes=[
            pltpu.VMEM((3, D, D), BF),
            pltpu.VMEM((4, TOK, 3 * GROUP), BF),
            pltpu.SemaphoreType.DMA((3,)),
        ],
        compiler_params=pltpu.CompilerParams(vmem_limit_bytes=24 * MIB),
        cost_estimate=pl.CostEstimate(flops=2 * TOK * D * D * 3, bytes_accessed=3 * D * D * 2, transcendentals=0),
        name="project",
    )(me, x, gain, cos, sin, *pinned(wq, wk, wv))


def arrange_kernel(me, b0, b1, b2, b3, kv):
    mine = me[0]
    for d, b in enumerate((b0, b1, b2, b3)):
        rows = pl.ds(pl.multiple_of(lax.rem(mine - d + 4, 4) * TOK, TOK), TOK)
        kv[rows, :] = b[:, : 2 * GROUP]


def arrange(me, blocks):
    return pl.pallas_call(
        arrange_kernel,
        out_shape=sds((4 * TOK, 2 * GROUP), BF),
        in_specs=[SMEM] + [VMEM] * 4,
        out_specs=VMEM,
        cost_estimate=pl.CostEstimate(flops=0, bytes_accessed=1 << 20, transcendentals=0),
        name="arrange",
    )(me, *blocks)


def tile_scores(q, k, start, place0, n):
    raw = mm_rt(k, q)
    keys = lax.broadcasted_iota(jnp.int32, (n, 256), 0)
    asks = lax.broadcasted_iota(jnp.int32, (n, 256), 1) + place0
    return jnp.where((keys <= asks) & (keys >= start), raw, -1e30)


def attend_kernel(me, core, b0, b1, b2, b3, own, sib, starts, m0, m1, m2, m3, q, kv, lse, mixed):
    mine = me[0]
    for d, b in enumerate((b0, b1, b2, b3)):
        rows = pl.ds(pl.multiple_of(lax.rem(mine - d + 4, 4) * TOK, TOK), TOK)
        q[rows, :] = b[:, 2 * GROUP :]

    def tile(which, pos):
        n = 256 * (pos + 1)
        outs = []
        start = starts[which : which + 1, :]
        for h in range(3):
            qs = q[256 * which : 256 * which + 256, 64 * h : 64 * h + 64] * jnp.asarray(0.125, BF)
            s = tile_scores(qs, kv[0:n, 64 * h : 64 * h + 64], start, 256 * pos, n)
            top = jnp.max(s, axis=0, keepdims=True)
            e = jnp.exp(s - top)
            total = jnp.sum(e, axis=0, keepdims=True)
            probs = (e * (1.0 / total)).astype(BF)
            lse[3 * which + h : 3 * which + h + 1, :] = top + jnp.log(total)
            outs.append(mm_lt(kv[0:n, GROUP + 64 * h : GROUP + 64 * h + 64], probs))
        out = jnp.concatenate(outs, axis=0).T.astype(BF)
        mixed[2 * which] = out[:TOK]
        mixed[2 * which + 1] = out[TOK:]

    @pl.when(core[0] == 0)
    def _():
        kv[0:256, :] = own[0:256, :]
        kv[256:512, :] = sib[256:512, :]
        kv[512:768, :] = sib[0:256, :]
        kv[768:1024, :] = own[256:512, :]
        tile(0, 0)
        tile(1, 3)

    @pl.when(core[0] == 1)
    def _():
        kv[0:256, :] = sib[0:256, :]
        kv[256:512, :] = own[256:512, :]
        kv[512:768, :] = own[0:256, :]
        kv[768:1024, :] = sib[256:512, :]
        tile(0, 2)
        tile(1, 1)

    for d, m in enumerate((m0, m1, m2, m3)):
        m[...] = mixed[lax.rem(mine + d, 4)]


def attend(me, core, blocks, own, sib, starts):
    return pl.pallas_call(
        attend_kernel,
        out_shape=[sds((TOK, GROUP), BF)] * 4
        + [sds((4 * TOK, GROUP), BF), sds((ROW, 2 * GROUP), BF), sds((8, 256), F32)],
        in_specs=[SMEM, SMEM] + [VMEM] * 7,
        out_specs=[VMEM] * 7,
        scratch_shapes=[pltpu.VMEM((4, TOK, GROUP), BF)],
        compiler_params=pltpu.CompilerParams(vmem_limit_bytes=24 * MIB),
        cost_estimate=pl.CostEstimate(flops=4 * 5 * 3 * 256 * 256 * 64, bytes_accessed=3 << 20, transcendentals=5 * 3 * 65536),
        name="attend",
    )(me, core, *blocks, own, sib, starts)


def feed_kernel(
    depth, me, x, gain, b0, b1, b2, b3, wo, wg, wu, wd,
    result, mixed_ref, middle_ref, normed2_ref, gate_ref, up_ref, hidden_ref,
    groups, wob, wgb, wub, wdb, sems,
):
    copies = [
        pltpu.make_async_copy(w.at[depth], buf, sems.at[i])
        for i, (w, buf) in enumerate(((wo, wob), (wg, wgb), (wu, wub), (wd, wdb)))
    ]
    for copy in copies:
        copy.start()
    mine = me[0]
    for d, b in enumerate((b0, b1, b2, b3)):
        groups[lax.rem(mine - d + 4, 4)] = b[...]
    mixed = jnp.concatenate([groups[g] for g in range(4)], axis=1)
    mixed_ref[...] = mixed
    copies[0].wait()
    middle = x[...] + mm(mixed, wob[...])
    middle_ref[...] = middle
    normed2 = (middle * norm_factor(middle) * gain[...]).astype(BF)
    normed2_ref[...] = normed2
    copies[1].wait()
    gate = mm(normed2, wgb[...])
    gate_ref[...] = gate
    copies[2].wait()
    up = mm(normed2, wub[...])
    up_ref[...] = up
    hidden = (gate / (1.0 + jnp.exp(-gate)) * up).astype(BF)
    hidden_ref[...] = hidden
    copies[3].wait()
    result[...] = middle + mm(hidden, wdb[...])


def feed(depth, me, x, gain, blocks, wo, wg, wu, wd):
    return pl.pallas_call(
        lambda *refs: feed_kernel(depth, *refs),
        out_shape=[
            sds((TOK, D), F32), sds((TOK, D), BF), sds((TOK, D), F32), sds((TOK, D), BF),
            sds((TOK, FF), F32), sds((TOK, FF), F32), sds((TOK, FF), BF),
        ],
        in_specs=[SMEM] + [VMEM] * 6 + [HBM] * 4,
        out_specs=[VMEM] * 7,
        scratch_shapes=[
            pltpu.VMEM((4, TOK, GROUP), BF),
            pltpu.VMEM((D, D), BF),
            pltpu.VMEM((D, FF), BF),
            pltpu.VMEM((D, FF), BF),
            pltpu.VMEM((FF, D), BF),
            pltpu.SemaphoreType.DMA((4,)),
        ],
        compiler_params=pltpu.CompilerParams(vmem_limit_bytes=32 * MIB),
        cost_estimate=pl.CostEstimate(flops=2 * TOK * D * (D + 3 * FF), bytes_accessed=2 * D * (D + 3 * FF), transcendentals=TOK * FF),
        name="feed",
    )(me, x, gain, *blocks, *pinned(wo, wg, wu, wd))


def feed_back_kernel(
    depth, me, grad, middle, gate_ref, up_ref, gain, wd, wg, wu, wo,
    right_ref, dmid_ref, gnorm_ref, o0, o1, o2, o3,
    groups, wdb, wgb, wub, wob, sems,
):
    copies = [
        pltpu.make_async_copy(w.at[depth], buf, sems.at[i])
        for i, (w, buf) in enumerate(((wd, wdb), (wg, wgb), (wu, wub), (wo, wob)))
    ]
    for copy in copies:
        copy.start()
    g = grad[...]
    gb = g.astype(BF)
    right_ref[:, 2 * FF : 2 * FF + D] = gb
    copies[0].wait()
    dhidden = mm_rt(gb, wdb[...])
    gate = gate_ref[...]
    sigma = 1.0 / (1.0 + jnp.exp(-gate))
    dgate = (dhidden * up_ref[...] * sigma * (1.0 + gate * (1.0 - sigma))).astype(BF)
    dup = (dhidden * gate * sigma).astype(BF)
    right_ref[:, :FF] = dgate
    right_ref[:, FF : 2 * FF] = dup
    copies[1].wait()
    dn = mm_rt(dgate, wgb[...])
    copies[2].wait()
    dn = dn + mm_rt(dup, wub[...])
    mid = middle[...]
    factor = norm_factor(mid)
    s = mid * factor
    gnorm_ref[...] = jnp.sum(dn * s, axis=0, keepdims=True)
    inner = dn * gain[...]
    dmid = g + factor * (inner - s * jnp.mean(inner * s, axis=-1, keepdims=True))
    dmid_ref[...] = dmid
    dmb = dmid.astype(BF)
    right_ref[:, 2 * FF + D :] = dmb
    copies[3].wait()
    dmixed = mm_rt(dmb, wob[...]).astype(BF)
    for j in range(4):
        groups[j] = dmixed[:, GROUP * j : GROUP * j + GROUP]
    mine = me[0]
    for d, o in enumerate((o0, o1, o2, o3)):
        o[...] = groups[lax.rem(mine + d, 4)]


def feed_back(depth, me, grad, middle, gate, up, gain, wd, wg, wu, wo):
    return pl.pallas_call(
        lambda *refs: feed_back_kernel(depth, *refs),
        out_shape=[sds((TOK, 2 * FF + 2 * D), BF), sds((TOK, D), F32), sds((1, D), F32)]
        + [sds((TOK, GROUP), BF)] * 4,
        in_specs=[SMEM] + [VMEM] * 5 + [HBM] * 4,
        out_specs=[VMEM] * 7,
        scratch_shapes=[
            pltpu.VMEM((4, TOK, GROUP), BF),
            pltpu.VMEM((FF, D), BF),
            pltpu.VMEM((D, FF), BF),
            pltpu.VMEM((D, FF), BF),
            pltpu.VMEM((D, D), BF),
            pltpu.SemaphoreType.DMA((4,)),
        ],
        compiler_params=pltpu.CompilerParams(vmem_limit_bytes=32 * MIB),
        cost_estimate=pl.CostEstimate(flops=2 * TOK * D * (D + 3 * FF), bytes_accessed=2 * D * (D + 3 * FF), transcendentals=TOK * FF),
        name="feed_back",
    )(me, grad, middle, gate, up, gain, *pinned(wd, wg, wu, wo))


def attend_back_kernel(me, core, q, kv, starts, lse, b0, b1, b2, b3, dq, own, sib, dout, dk, dv):
    mine = me[0]
    for d, b in enumerate((b0, b1, b2, b3)):
        rows = pl.ds(pl.multiple_of(lax.rem(mine - d + 4, 4) * TOK, TOK), TOK)
        dout[rows, :] = b[...]

    def tile(which, pos, first):
        n = 256 * (pos + 1)
        start = starts[which : which + 1, :]
        dqs = []
        for h in range(3):
            lanes = slice(64 * h, 64 * h + 64)
            qs = q[256 * which : 256 * which + 256, lanes] * jnp.asarray(0.125, BF)
            do = dout[256 * which : 256 * which + 256, lanes]
            k = kv[0:n, lanes]
            v = kv[0:n, GROUP + 64 * h : GROUP + 64 * h + 64]
            s = tile_scores(qs, k, start, 256 * pos, n)
            p = jnp.exp(s - lse[3 * which + h : 3 * which + h + 1, :])
            dp = mm_rt(v, do)
            delta = jnp.sum(p * dp, axis=0, keepdims=True)
            ds = (p * (dp - delta)).astype(BF)
            dk_h = mm(ds, qs)
            dv_h = mm(p.astype(BF), do)
            if first:
                dk[0:n, lanes] = dk_h
                dv[0:n, lanes] = dv_h
            else:
                dk[0:n, lanes] += dk_h
                dv[0:n, lanes] += dv_h
            dqs.append(mm_lt(k, ds))
        out = jnp.concatenate(dqs, axis=0).T * 0.125
        dq[256 * which : 256 * which + 256, :] = out.astype(BF)

    def put(target, rows, tile_no):
        target[rows : rows + 256, :GROUP] = dk[256 * tile_no : 256 * tile_no + 256, :].astype(target.dtype)
        target[rows : rows + 256, GROUP:] = dv[256 * tile_no : 256 * tile_no + 256, :].astype(target.dtype)

    @pl.when(core[0] == 0)
    def _():
        tile(1, 3, True)
        tile(0, 0, False)
        put(own, 0, 0)
        put(sib, 256, 1)
        put(sib, 0, 2)
        put(own, 256, 3)

    @pl.when(core[0] == 1)
    def _():
        tile(0, 2, True)
        tile(1, 1, False)
        dk[768:1024, :] = jnp.zeros((256, GROUP), F32)
        dv[768:1024, :] = jnp.zeros((256, GROUP), F32)
        put(sib, 0, 0)
        put(own, 256, 1)
        put(own, 0, 2)
        put(sib, 256, 3)


def attend_back(me, core, q, kv, starts, lse, blocks):
    return pl.pallas_call(
        attend_back_kernel,
        out_shape=[sds((4 * TOK, GROUP), BF), sds((4 * TOK, 2 * GROUP), F32), sds((4 * TOK, 2 * GROUP), BF)],
        in_specs=[SMEM, SMEM] + [VMEM] * 8,
        out_specs=[VMEM] * 3,
        scratch_shapes=[
            pltpu.VMEM((4 * TOK, GROUP), BF),
            pltpu.VMEM((ROW, GROUP), F32),
            pltpu.VMEM((ROW, GROUP), F32),
        ],
        compiler_params=pltpu.CompilerParams(vmem_limit_bytes=32 * MIB),
        cost_estimate=pl.CostEstimate(flops=10 * 5 * 3 * 256 * 256 * 64, bytes_accessed=4 << 20, transcendentals=5 * 3 * 65536),
        name="attend_back",
    )(me, core, q, kv, starts, lse, *blocks)


def spread_kernel(me, dq, own, got, o0, o1, o2, o3):
    mine = me[0]
    for d, o in enumerate((o0, o1, o2, o3)):
        rows = pl.ds(pl.multiple_of(lax.rem(mine + d, 4) * TOK, TOK), TOK)
        o[:, 2 * GROUP :] = dq[rows, :]
        o[:, : 2 * GROUP] = (own[rows, :] + got[rows, :].astype(F32)).astype(BF)


def spread(me, dq, own, got):
    return pl.pallas_call(
        spread_kernel,
        out_shape=[sds((TOK, 3 * GROUP), BF)] * 4,
        in_specs=[SMEM] + [VMEM] * 3,
        out_specs=[VMEM] * 4,
        cost_estimate=pl.CostEstimate(flops=1 << 18, bytes_accessed=2 << 20, transcendentals=0),
        name="spread",
    )(me, dq, own, got)


def project_back_kernel(
    depth, me, dmid, x, gain, cos, sin, gains, b0, b1, b2, b3, wq, wk, wv,
    grad_ref, right_ref, gains_ref, groups, wbuf, sems,
):
    copies = [
        pltpu.make_async_copy(w.at[depth], wbuf.at[i], sems.at[i]) for i, w in enumerate((wq, wk, wv))
    ]
    for copy in copies:
        copy.start()
    mine = me[0]
    for d, b in enumerate((b0, b1, b2, b3)):
        groups[lax.rem(mine - d + 4, 4)] = b[...]
    da = jnp.zeros((TOK, D), F32)
    for i, name in enumerate("qkv"):
        y = jnp.concatenate([groups[g, :, OFF[name] : OFF[name] + GROUP] for g in range(4)], axis=1)
        if i < 2:
            y = turn(y.astype(F32), cos[...], -sin[...]).astype(BF)
        right_ref[:TOK, D * i : D * i + D] = y
        copies[i].wait()
        da = da + mm_rt(y, wbuf[i])
    values = x[...]
    factor = norm_factor(values)
    s = values * factor
    rows = jnp.concatenate(
        [gains[0:3, :], jnp.sum(da * s, axis=0, keepdims=True), jnp.zeros((12, D), F32)], axis=0
    )
    gains_ref[...] = rows[:8]
    right_ref[TOK:, :D] = rows.astype(BF)
    right_ref[TOK:, D:] = jnp.zeros((16, 2 * D), BF)
    inner = da * gain[...]
    grad_ref[...] = dmid[...] + factor * (inner - s * jnp.mean(inner * s, axis=-1, keepdims=True))


def project_back(depth, me, dmid, x, gain, cos, sin, gains, blocks, wq, wk, wv):
    return pl.pallas_call(
        lambda *refs: project_back_kernel(depth, *refs),
        out_shape=[sds((TOK, D), F32), sds((TOK + 16, 3 * D), BF), sds((8, D), F32)],
        in_specs=[SMEM] + [VMEM] * 10 + [HBM] * 3,
        out_specs=[VMEM] * 3,
        scratch_shapes=[
            pltpu.VMEM((4, TOK, 3 * GROUP), BF),
            pltpu.VMEM((3, D, D), BF),
            pltpu.SemaphoreType.DMA((3,)),
        ],
        compiler_params=pltpu.CompilerParams(vmem_limit_bytes=24 * MIB),
        cost_estimate=pl.CostEstimate(flops=2 * TOK * D * D * 3, bytes_accessed=3 * D * D * 2, transcendentals=0),
        name="project_back",
    )(me, dmid, x, gain, cos, sin, gains, *blocks, *pinned(wq, wk, wv))


def exchange_x(blocks):
    return (blocks[0],) + tuple(send(blocks[d], SHIFT_X[d]) for d in (1, 2, 3))


def left_kernel(jobs, core, *refs):
    ins, (keep, away), turned = refs[:-3], refs[-3:-1], refs[-1]
    mine = core[0]
    row = 0
    for source, hot in jobs:
        if hot is None:
            turned[...] = ins[source][...].T.reshape(2 * FF // 32, 16, TOK)
            half = block_order("zxy").reshape(2, 64)
            for i in range(64):
                for out, take in ((keep, mine == 0), (away, mine != 0)):
                    block = jnp.where(take, int(half[0, i]), int(half[1, i]))
                    out[row + 16 * i : row + 16 * i + 16, :] = turned[block]
            row += FF // 2
        else:
            for out, start in ((keep, mine * (D // 2)), (away, (1 - mine) * (D // 2))):
                hot_rows = ins[hot][pl.ds(pl.multiple_of(start, D // 2), D // 2), :]
                out[row : row + D // 2, :] = mm_rt(hot_rows, ins[source][...]).astype(BF)
            row += D // 2


def left_sides(core, sources, hots, jobs):
    rows = sum(FF // 2 if hot is None else D // 2 for _, hot in jobs)
    return pl.pallas_call(
        lambda *refs: left_kernel(jobs, *refs),
        out_shape=[sds((rows, TOK), BF)] * 2,
        in_specs=[SMEM] + [VMEM] * (len(sources) + len(hots)),
        out_specs=[VMEM] * 2,
        scratch_shapes=[pltpu.VMEM((FF // 16, 16, TOK), BF)],
        compiler_params=pltpu.CompilerParams(vmem_limit_bytes=16 * MIB),
        cost_estimate=pl.CostEstimate(flops=len(jobs) * 2 * D * D * TOK, bytes_accessed=4 << 20, transcendentals=0),
        name="left_sides",
    )(core, *sources, *hots)


def weights_kernel(jobs, bits, left, left_sib, right, right_sib, hot, core, *outs):
    for i, (row, rows, columns, bit, with_gains) in enumerate(jobs):
        half = rows // 2
        for out, side in ((outs[2 * i], 1 - bits[bit]), (outs[2 * i + 1], bits[bit])):
            pick = pl.ds(pl.multiple_of(row + side * half, 64), half)
            lhs = jnp.concatenate([left[pick, :], left_sib[pick, :]], axis=1)
            at = 0
            for first, last in columns:
                for col in range(first, last, 256):
                    rhs = jnp.concatenate(
                        [right[:TOK, col : col + 256], right_sib[:TOK, col : col + 256]], axis=0
                    )
                    out[:, at : at + 256] = mm(lhs, rhs).astype(BF)
                    at += 256
            if with_gains:
                total = right[TOK:, :D].astype(F32) + right_sib[TOK:, :D].astype(F32)
                columns_t = jnp.concatenate([total, jnp.zeros((TOK - 16, D), F32)], axis=0).astype(BF)
                hot_pick = pl.ds(pl.multiple_of(core[0] * (D // 2) + side * half, 64), half)
                out[:, at : at + TOK] = mm_rt(hot[hot_pick, :], columns_t).astype(BF)


def weights(bits, core, left, left_sib, right, right_sib, hot, jobs):
    shapes = []
    flops = 0
    for _, rows, columns, _, with_gains in jobs:
        width = sum(last - first for first, last in columns) + (TOK if with_gains else 0)
        shapes += [sds((rows // 2, width), BF)] * 2
        flops += 4 * rows * width * TOK
    outs = pl.pallas_call(
        lambda *refs: weights_kernel(jobs, *refs),
        out_shape=shapes,
        in_specs=[SMEM] + [VMEM] * 5 + [SMEM],
        out_specs=[VMEM] * len(shapes),
        compiler_params=pltpu.CompilerParams(vmem_limit_bytes=32 * MIB),
        cost_estimate=pl.CostEstimate(flops=2 * flops, bytes_accessed=8 << 20, transcendentals=0),
        name="weights",
    )(bits, left, left_sib, right, right_sib, hot, core)
    return [(outs[2 * i], outs[2 * i + 1]) for i in range(len(jobs))]


def halves(value, got, bit, half):
    if half % 16 == 0:
        for side in (1 - bit, bit):
            pick = pl.ds(pl.multiple_of(side * half, 16), half)
            yield value[pick, :].astype(F32) + got[pick, :].astype(F32)
    else:
        total = value[...].astype(F32) + got[...].astype(F32)
        low, high = total[:half], total[half:]
        yield jnp.where(bit == 0, high, low)
        yield jnp.where(bit == 0, low, high)


def round_kernel(groups, bits, *refs):
    count = 2 * sum(n for _, n in groups)
    ins, outs = refs[:count], refs[count:]
    for bit, n in groups:
        out, keep = outs[0], outs[1]
        at = 0
        for i in range(n):
            value, got = ins[0], ins[1]
            width = value.shape[1]
            sent, kept = halves(value, got, bits[bit], value.shape[0] // 2)
            out[:, at : at + width] = sent.astype(BF)
            keep[:, at : at + width] = kept.astype(BF)
            at += width
            ins = ins[2:]
        outs = outs[2:]


def round_step(bits, groups):
    shapes, args = [], []
    for _, members in groups:
        width = sum(value.shape[1] for value, _ in members)
        shapes += [sds((members[0][0].shape[0] // 2, width), BF)] * 2
        for value, got in members:
            args += [value, got]
    plan = [(bit, len(members)) for bit, members in groups]
    outs = pl.pallas_call(
        lambda *refs: round_kernel(plan, *refs),
        out_shape=shapes,
        in_specs=[SMEM] + [VMEM] * len(args),
        out_specs=[VMEM] * len(shapes),
        compiler_params=pltpu.CompilerParams(vmem_limit_bytes=16 * MIB),
        cost_estimate=pl.CostEstimate(
            flops=sum(a.size for a in args), bytes_accessed=4 * sum(a.size for a in args), transcendentals=0
        ),
        name="round_step",
    )(bits, *args)
    return [(outs[2 * i], outs[2 * i + 1]) for i in range(len(groups))]


def finish_kernel(plan, *refs):
    pairs = len(plan)
    ins, outs = refs[: 2 * pairs], refs[2 * pairs :]
    for i, places in enumerate(plan):
        total = ins[2 * i][...].astype(F32) + ins[2 * i + 1][...].astype(F32)
        for first, last, output, layer in places:
            if layer is None:
                outs[output][...] = total[:, first:last]
            else:
                outs[output][layer] = total[:, first:last]


def finish(pairs, plan, shapes):
    args = [a for pair in pairs for a in pair]
    return pl.pallas_call(
        lambda *refs: finish_kernel(plan, *refs),
        out_shape=[sds(shape, F32) for shape in shapes],
        in_specs=[VMEM] * len(args),
        out_specs=[VMEM] * len(shapes),
        compiler_params=pltpu.CompilerParams(vmem_limit_bytes=16 * MIB),
        cost_estimate=pl.CostEstimate(flops=1 << 18, bytes_accessed=2 << 20, transcendentals=0),
        name="finish",
    )(*args)


def tie(value, *others):
    return lax.optimization_barrier((value,) + others)[0]


BIT = {(axis, step): 2 * i + step for i, axis in enumerate("xyz") for step in (0, 1)}


def all_bits(spot):
    bits = []
    for axis in "xyz":
        at = spot[axis]
        rank = jnp.where(spot["c"] == 0, jnp.array([0, 2, 3, 1], jnp.int32)[at], at)
        bits += [rank // 2, rank % 2]
    return jnp.stack(bits).astype(jnp.int32)


def exchange(axis, step, pair):
    return (pair[1], send(pair[0], PAIR[axis, step]))


def rope_tables(inside):
    offset = jnp.maximum(inside - 1, 0)
    grid_rows = (offset // GRID).astype(F32)
    grid_cols = (offset % GRID).astype(F32)
    live = (inside > 0).astype(F32)
    freqs = 10000.0 ** (-4.0 * jnp.arange(HEAD_DIM // 4, dtype=F32) / HEAD_DIM)
    angles = jnp.concatenate([grid_rows[:, None] * freqs[None, :], grid_cols[:, None] * freqs[None, :]], axis=1)
    angles = angles * live[:, None]
    cos = jnp.tile(jnp.repeat(jnp.cos(angles), 2, axis=1), (1, 2))
    signs = jnp.tile(jnp.array([-1.0, 1.0], F32), 64)
    sin = jnp.tile(jnp.repeat(jnp.sin(angles), 2, axis=1), (1, 2)) * signs[None, :]
    return cos, sin


def segment_starts(lengths, places):
    ends = jnp.cumsum(lengths)
    starts = ends - lengths
    member = (places[:, None] >= starts[None, :]) & (places[:, None] < ends[None, :])
    return jnp.sum(jnp.where(member, starts[None, :], 0), axis=1)


def per_device(
    tokens, seg_lengths, cotangent, norm_attn, w_query, w_key, w_value, w_out, norm_ffn, w_gate, w_up, w_down
):
    seq = lax.axis_index("seq")
    batch = lax.axis_index("batch")
    spot = {
        "x": seq % 4,
        "y": batch // 4,
        "z": (batch // 2) % 2 * 2 + seq // 4,
        "c": batch % 2,
    }
    me = spot["x"].astype(jnp.int32).reshape(1)
    core = spot["c"].astype(jnp.int32).reshape(1)

    with jax.named_scope("S_setup"):
        moved = send(tokens[0], RELOCATE)
        lengths = send(seg_lengths[0], RELOCATE)
        cot = send(cotangent[0], RELOCATE)
        first = jnp.where(spot["c"] == 0, jnp.array([0, 1, 6, 7], jnp.int32), jnp.array([4, 5, 2, 3], jnp.int32))
        own_places = first[spot["x"]] * TOK + jnp.arange(TOK, dtype=jnp.int32)
        cos, sin = rope_tables(own_places - segment_starts(lengths, own_places))
        ask_places = (first[:, None] * TOK + jnp.arange(TOK, dtype=jnp.int32)[None, :]).reshape(-1)
        starts = segment_starts(lengths, ask_places).reshape(2, 256)

    layers = w_query.shape[0]
    bits = all_bits(spot)
    hots = {axes: one_hot(axes) for axes in ("xyz", "yzx", "zxy")}
    x = moved.astype(F32)
    kept = []
    lefts = []
    for depth in range(layers):
        with jax.named_scope(f"S_ahead{depth}"):
            gain = norm_attn[depth][None]
            gain2 = norm_ffn[depth][None]
            *blocks, normed = project(depth, me, x, gain, cos, sin, w_query, w_key, w_value)
            blocks = exchange_x(blocks)
            own = arrange(me, blocks)
            sib = send(own, CORE)
            *blocks, q, kv, lse = attend(me, core, blocks, own, sib, starts)
            result, mixed, middle, normed2, gate, up, hidden = feed(
                depth, me, x, gain2, exchange_x(blocks), w_out, w_gate, w_up, w_down
            )
            kept.append((x, gain, gain2, q, kv, lse, middle, gate, up))
            sources = [normed, mixed, normed2, hidden]
            if depth == 0:
                jobs = [(0, 4), (0, 5), (0, 6), (1, 6), (2, 5), (3, None)]
                left = left_sides(core, sources, [hots["xyz"], hots["yzx"], hots["zxy"]], jobs)
            else:
                jobs = [(0, 5), (1, 5), (2, 4), (3, None)]
                left = left_sides(core, sources, [hots["yzx"], hots["zxy"]], jobs)
            lefts.append((left[0], send(left[1], CORE)))
            x = result
    activations = send(x.astype(BF), RESTORE)[None]

    half = D // 2
    gu_cols, gb_cols, dmb_cols = (0, 2 * FF), (2 * FF, 2 * FF + D), (2 * FF + D, 2 * FF + 2 * D)

    x, gain, gain2, q, kv, lse, middle, gate, up = kept[1]
    with jax.named_scope("S_back1"):
        right1, dmid, gnorm_ffn1, *blocks = feed_back(
            1, me, cot.astype(F32), middle, gate, up, gain2, w_down, w_gate, w_up, w_out
        )
        right1_sib = send(right1, CORE)
        dq, own, sib = attend_back(me, core, q, kv, starts, lse, exchange_x(blocks))
        got = send(sib, CORE)
    with jax.named_scope("S_sum1"):
        left, left_sib = lefts[1]
        gu1, down1 = weights(
            bits, core, tie(left, dq), left_sib, right1, right1_sib, hots["xyz"],
            [
                (2 * half, D // 2, [gu_cols], BIT["y", 0], False),
                (3 * half, FF // 2, [gb_cols], BIT["z", 0], False),
            ],
        )
        gu1, down1 = exchange("y", 0, gu1), exchange("z", 0, down1)
    with jax.named_scope("S_back1"):
        blocks = spread(me, tie(dq, gu1[0]), own, got)
        gains = jnp.concatenate([gnorm_ffn1, jnp.zeros((7, D), F32)], axis=0)
        grad, right1b, gains = project_back(
            1, me, dmid, x, gain, cos, sin, gains, exchange_x(blocks), w_query, w_key, w_value
        )
        right1b_sib = send(right1b, CORE)

    x, gain, gain2, q, kv, lse, middle, gate, up = kept[0]
    with jax.named_scope("S_back0"):
        right0, dmid, gnorm_ffn0, *blocks = feed_back(
            0, me, grad, middle, gate, up, gain2, w_down, w_gate, w_up, w_out
        )
        right0_sib = send(right0, CORE)
        blocks = exchange_x(blocks)
    with jax.named_scope("S_sum1"):
        gu1, down1 = round_step(
            bits, [(BIT["y", 1], [(tie(gu1[0], dmid), gu1[1])]), (BIT["z", 1], [down1])]
        )
        gu1, down1 = exchange("y", 1, gu1), exchange("z", 1, down1)
        (out1,) = weights(
            bits, core, tie(left, dmid), left_sib, right1[:, 2 * FF + D :], right1_sib[:, 2 * FF + D :], hots["xyz"],
            [(half, D // 2, [(0, D)], BIT["z", 0], False)],
        )
        (qkv1,) = weights(
            bits, core, left, left_sib, right1b, right1b_sib, hots["xyz"],
            [(0, D // 2, [(0, 3 * D)], BIT["z", 0], False)],
        )
        out1, qkv1 = exchange("z", 0, out1), exchange("z", 0, qkv1)
    with jax.named_scope("S_back0"):
        blocks = (tie(blocks[0], qkv1[0], out1[0], gu1[0]),) + tuple(blocks[1:])
        dq, own, sib = attend_back(me, core, q, kv, starts, lse, blocks)
        got = send(sib, CORE)
    with jax.named_scope("S_sum0"):
        left, left_sib = lefts[0]
        gu0, down0, out0 = weights(
            bits, core, tie(left, dq), left_sib, right0, right0_sib, hots["xyz"],
            [
                (4 * half, D // 2, [gu_cols], BIT["y", 0], False),
                (5 * half, FF // 2, [gb_cols], BIT["z", 0], False),
                (3 * half, D // 2, [dmb_cols], BIT["z", 0], False),
            ],
        )
        gu0, down0, out0 = exchange("y", 0, gu0), exchange("z", 0, down0), exchange("z", 0, out0)
    with jax.named_scope("S_back0"):
        blocks = exchange_x(spread(me, tie(dq, gu0[0]), own, got))
    with jax.named_scope("S_sum1"):
        (ov1,) = round_step(bits, [(BIT["z", 1], [(tie(out1[0], blocks[0]), out1[1]), qkv1])])
        ov1 = exchange("z", 1, ov1)
    with jax.named_scope("S_back0"):
        blocks = (tie(blocks[0], ov1[0]),) + tuple(blocks[1:])
        gains = jnp.concatenate([gnorm_ffn1, gains[3:4], gnorm_ffn0, jnp.zeros((5, D), F32)], axis=0)
        grad, right0b, _ = project_back(
            0, me, dmid, x, gain, cos, sin, gains, blocks, w_query, w_key, w_value
        )
        right0b_sib = send(right0b, CORE)
        grad_tokens = send(grad.astype(BF), RESTORE).astype(F32)[None]

    with jax.named_scope("S_sum0"):
        gu0, down0, out0 = round_step(
            bits,
            [(BIT["y", 1], [(tie(gu0[0], right0b), gu0[1])]), (BIT["z", 1], [down0]), (BIT["z", 1], [out0])],
        )
        gu0, down0, out0 = exchange("y", 1, gu0), exchange("z", 1, down0), exchange("z", 1, out0)
        q0, k0, v0 = weights(
            bits, core, left, left_sib, right0b, right0b_sib, hots["xyz"],
            [
                (0, D // 2, [(0, D)], BIT["x", 0], True),
                (half, D // 2, [(D, 2 * D)], BIT["y", 0], False),
                (2 * half, D // 2, [(2 * D, 3 * D)], BIT["z", 0], False),
            ],
        )
        q0, k0, v0 = exchange("x", 0, q0), exchange("y", 0, k0), exchange("z", 0, v0)
        q0, k0, v0 = round_step(bits, [(BIT["x", 1], [q0]), (BIT["y", 1], [k0]), (BIT["z", 1], [v0])])
        q0, k0, v0 = exchange("x", 1, q0), exchange("y", 1, k0), exchange("z", 1, v0)
        group_q, group_g, group_o, group_d = [q0], [gu1, gu0, k0], [ov1, out0, v0], [down1, down0]
        for i in range(4):
            axes = ["yz"[i // 2], "zx"[i // 2], "xy"[i // 2], "xy"[i // 2]]
            step = i % 2
            outs = round_step(
                bits,
                [(BIT[axis, step], group) for axis, group in zip(axes, (group_q, group_g, group_o, group_d))],
            )
            group_q, group_g, group_o, group_d = (
                [exchange(axis, step, out)] for axis, out in zip(axes, outs)
            )
        plan = [
            [(0, D, 0, 0), (D, D + TOK, 7, None)],
            [(0, FF, 4, 1), (FF, 2 * FF, 5, 1), (2 * FF, 3 * FF, 4, 0), (3 * FF, 4 * FF, 5, 0), (4 * FF, 4 * FF + D, 1, 0)],
            [(0, D, 3, 1), (D, 2 * D, 0, 1), (2 * D, 3 * D, 1, 1), (3 * D, 4 * D, 2, 1), (4 * D, 5 * D, 3, 0), (5 * D, 6 * D, 2, 0)],
            [(0, D, 6, 1), (D, 2 * D, 6, 0)],
        ]
        grad_q, grad_k, grad_v, grad_o, grad_gate, grad_up, grad_down, gains = finish(
            [group_q[0], group_g[0], group_o[0], group_d[0]],
            plan,
            [(2, 6, D)] * 4 + [(2, 6, FF)] * 2 + [(2, 16, D), (6, TOK)],
        )
    return (
        activations,
        grad_tokens,
        jnp.stack([gains[:, 3], gains[:, 1]]),
        grad_q,
        grad_k,
        grad_v,
        grad_o,
        jnp.stack([gains[:, 2], gains[:, 0]]),
        grad_gate,
        grad_up,
        grad_down,
    )


def solution(mesh):
    rows = P("batch", "seq", None)
    split = P(None, AXES)
    split3 = P(None, AXES, None)
    return jax.shard_map(
        per_device,
        mesh=mesh,
        in_specs=(rows, P("batch", None), rows) + (P(),) * 9,
        out_specs=(rows, rows, split, split3, split3, split3, split3, split, split3, split3, split3),
        check_vma=False,
    )
```

```python
import jax
import jax.numpy as jnp
import numpy as np
from jax import lax
from jax.experimental import pallas as pl
from jax.experimental.pallas import tpu as pltpu
from jax.sharding import PartitionSpec as P

D = 768
HEADS = 12
HEAD_DIM = 64
FF = 2048
TOK = 128
ROW = 1024
GRID = 16
GROUP = 3 * HEAD_DIM
OFF = {"k": 0, "v": GROUP, "q": 2 * GROUP}
EPS = 1e-05
AXES = ("seq", "batch")
BF = jnp.bfloat16
F32 = jnp.float32
MIB = 1 << 20


def place(flat):
    seq, batch = divmod(flat, 16)
    z_lo, x = divmod(seq, 4)
    y, rest = divmod(batch, 4)
    z_hi, core = divmod(rest, 2)
    return dict(x=x, y=y, z=z_hi * 2 + z_lo, c=core)


def flat_of(p):
    z_hi, z_lo = divmod(p["z"], 2)
    return (z_lo * 4 + p["x"]) * 16 + p["y"] * 4 + z_hi * 2 + p["c"]


def permutation(move):
    pairs = []
    for flat in range(128):
        p = place(flat)
        move(p)
        pairs.append((flat, flat_of(p)))
    return pairs


def move_relocate(p):
    z_hi, z_lo = divmod(p["z"], 2)
    core = p["c"]
    p["z"] = z_hi * 2 + core
    p["c"] = z_lo ^ (1 if p["x"] >= 2 else 0)


RELOCATE = permutation(move_relocate)
RESTORE = sorted((dst, src) for src, dst in RELOCATE)


def move_core(p):
    p["c"] ^= 1


CORE = permutation(move_core)


def shift_x(by):
    def move(p):
        p["x"] = (p["x"] + by) % 4

    return permutation(move)


SHIFT_X = {d: shift_x(d) for d in (1, 2, 3)}


def pair_step(axis, step):
    def move(p):
        at = p[axis]
        p[axis] = at ^ 1 if (p["c"] == 0) == (step == 0) else 3 - at

    return permutation(move)


PAIR = {(axis, step): pair_step(axis, step) for axis in "xyz" for step in (0, 1)}


def send(value, pairs):
    return lax.ppermute(value, AXES, pairs)


RING_ORDER = {0: (0, 3, 1, 2), 1: (0, 1, 2, 3)}


def block_order(axes):
    order = []
    for core in (0, 1):
        ring = RING_ORDER[core]
        for a in ring:
            for b in ring:
                for c in ring:
                    order.append(flat_of({axes[0]: a, axes[1]: b, axes[2]: c, "c": core}))
    return np.array(order)


def one_hot(axes, core, swapped=False):
    row = lax.broadcasted_iota(jnp.int32, (D // 2, 1), 0)
    block = (row * 10923) >> 16
    within = row - 6 * block
    places = {}
    for i, axis in enumerate(axes):
        at = (block >> (4 - 2 * i)) & 3
        ring = jnp.where(at == 0, 0, jnp.where(at == 1, 3, at - 1))
        places[axis] = jnp.where(core == (1 if swapped else 0), ring, at)
    z = places["z"]
    flat = ((z & 1) * 4 + places["x"]) * 16 + places["y"] * 4 + (z >> 1) * 2 + core
    lane = lax.broadcasted_iota(jnp.int32, (D // 2, D), 1)
    return jnp.where(lane == flat * 6 + within, 1.0, 0.0).astype(BF)


def mm(left, right):
    return jnp.dot(left, right, preferred_element_type=F32)


def mm_rt(left, right):
    return lax.dot_general(left, right, (((1,), (1,)), ((), ())), preferred_element_type=F32)


def mm_lt(left, right):
    return lax.dot_general(left, right, (((0,), (0,)), ((), ())), preferred_element_type=F32)


VMEM = pl.BlockSpec(memory_space=pltpu.VMEM)
SMEM = pl.BlockSpec(memory_space=pltpu.SMEM)
HBM = pl.BlockSpec(memory_space=pltpu.HBM)


def pinned(*weights):
    return tuple(pltpu.with_memory_space_constraint(w, pltpu.VMEM) for w in weights)


def at_rest(value):
    return pltpu.with_memory_space_constraint(value, pltpu.HBM)


def stored(shape, kind):
    return pltpu.HBM(shape, kind)


def sds(shape, kind):
    return jax.ShapeDtypeStruct(shape, kind)


def turn(values, cos, sin):
    lane = lax.broadcasted_iota(jnp.int32, (TOK, 128), 1)
    even = lane % 2 == 0
    parts = []
    for t in range(6):
        v = values[:, 128 * t : 128 * t + 128]
        swapped = jnp.where(even, pltpu.roll(v, 127, 1), pltpu.roll(v, 1, 1))
        parts.append(v * cos + swapped * sin)
    return jnp.concatenate(parts, axis=1)


def norm_factor(values):
    return lax.rsqrt(jnp.mean(values * values, axis=-1, keepdims=True) + EPS)


def project_kernel(depth, me, x, gain, cos, sin, wq, wk, wv, o0, o1, o2, o3, normed_ref, groups):
    values = x[...]
    normed = (values * norm_factor(values) * gain[...]).astype(BF)
    normed_ref[...] = normed
    for i, w in enumerate((wk, wv, wq)):
        y = mm(normed, w[depth])
        if i != 1:
            mine_rows = pl.ds(pl.multiple_of(me[0] * TOK, TOK), TOK)
            y = turn(y, cos[mine_rows, :], sin[mine_rows, :])
        y = y.astype(BF)
        for g in range(4):
            groups[g, :, GROUP * i : GROUP * i + GROUP] = y[:, GROUP * g : GROUP * g + GROUP]
    mine = me[0]
    for d, o in enumerate((o0, o1, o2, o3)):
        o[...] = groups[lax.rem(mine + d, 4)]


def project(depth, me, x, gain, cos, sin, wq, wk, wv):
    return pl.pallas_call(
        lambda *refs: project_kernel(depth, *refs),
        out_shape=[sds((TOK, 3 * GROUP), BF)] * 4 + [stored((TOK, D), BF)],
        in_specs=[SMEM] + [VMEM] * 7,
        out_specs=[VMEM] * 5,
        scratch_shapes=[pltpu.VMEM((4, TOK, 3 * GROUP), BF)],
        compiler_params=pltpu.CompilerParams(vmem_limit_bytes=16 * MIB),
        cost_estimate=pl.CostEstimate(flops=2 * TOK * D * D * 3, bytes_accessed=3 * D * D * 2, transcendentals=0),
        name="project",
    )(me, x, gain, cos, sin, *pinned(wq, wk, wv))


def arrange_kernel(me, b0, b1, b2, b3, kv):
    mine = me[0]
    for d, b in enumerate((b0, b1, b2, b3)):
        rows = pl.ds(pl.multiple_of(lax.rem(mine - d + 4, 4) * TOK, TOK), TOK)
        kv[rows, :] = b[:, : 2 * GROUP]


def arrange(me, blocks):
    return pl.pallas_call(
        arrange_kernel,
        out_shape=sds((4 * TOK, 2 * GROUP), BF),
        in_specs=[SMEM] + [VMEM] * 4,
        out_specs=VMEM,
        compiler_params=pltpu.CompilerParams(vmem_limit_bytes=4 * MIB),
        cost_estimate=pl.CostEstimate(flops=0, bytes_accessed=1 << 20, transcendentals=0),
        name="arrange",
    )(me, *blocks)


def tile_scores(q, k, start, place0, n):
    raw = mm_rt(k, q)
    keys = lax.broadcasted_iota(jnp.int32, (n, 256), 0)
    asks = lax.broadcasted_iota(jnp.int32, (n, 256), 1) + place0
    return jnp.where((keys <= asks) & (keys >= start), raw, -1e30)


def attend_kernel(me, core, b0, b1, b2, b3, own, sib, starts, m0, m1, m2, m3, q_out, kv_out, lse_out, q, kv, lse, mixed, sems):
    mine = me[0]
    for d, b in enumerate((b0, b1, b2, b3)):
        rows = pl.ds(pl.multiple_of(lax.rem(mine - d + 4, 4) * TOK, TOK), TOK)
        q[rows, :] = b[:, 2 * GROUP :]
    stores = [
        pltpu.make_async_copy(source, out, sems.at[i])
        for i, (source, out) in enumerate(((q, q_out), (kv, kv_out), (lse, lse_out)))
    ]
    stores[0].start()

    @pl.when(core[0] == 0)
    def _():
        kv[0:256, :] = own[0:256, :]
        kv[256:512, :] = sib[256:512, :]
        kv[512:768, :] = sib[0:256, :]
        kv[768:1024, :] = own[256:512, :]

    @pl.when(core[0] == 1)
    def _():
        kv[0:256, :] = sib[0:256, :]
        kv[256:512, :] = own[256:512, :]
        kv[512:768, :] = own[0:256, :]
        kv[768:1024, :] = sib[256:512, :]

    stores[1].start()

    def tile(which, pos):
        n = 256 * (pos + 1)
        outs = []
        start = starts[which : which + 1, :]
        for h in range(3):
            qs = q[256 * which : 256 * which + 256, 64 * h : 64 * h + 64] * jnp.asarray(0.125, BF)
            s = tile_scores(qs, kv[0:n, 64 * h : 64 * h + 64], start, 256 * pos, n)
            top = jnp.max(s, axis=0, keepdims=True)
            e = jnp.exp(s - top)
            total = jnp.sum(e, axis=0, keepdims=True)
            probs = (e * (1.0 / total)).astype(BF)
            lse[3 * which + h : 3 * which + h + 1, :] = top + jnp.log(total)
            outs.append(mm_lt(kv[0:n, GROUP + 64 * h : GROUP + 64 * h + 64], probs))
        out = jnp.concatenate(outs, axis=0).T.astype(BF)
        mixed[2 * which] = out[:TOK]
        mixed[2 * which + 1] = out[TOK:]

    @pl.when(core[0] == 0)
    def _():
        tile(0, 0)
        tile(1, 3)

    @pl.when(core[0] == 1)
    def _():
        tile(0, 2)
        tile(1, 1)

    stores[2].start()
    for d, m in enumerate((m0, m1, m2, m3)):
        m[...] = mixed[lax.rem(mine + d, 4)]
    for store in stores:
        store.wait()


def attend(me, core, blocks, own, sib, starts):
    return pl.pallas_call(
        attend_kernel,
        out_shape=[sds((TOK, GROUP), BF)] * 4
        + [stored((4 * TOK, GROUP), BF), stored((ROW, 2 * GROUP), BF), stored((8, 256), F32)],
        in_specs=[SMEM, SMEM] + [VMEM] * 7,
        out_specs=[VMEM] * 4 + [HBM] * 3,
        scratch_shapes=[
            pltpu.VMEM((4 * TOK, GROUP), BF),
            pltpu.VMEM((ROW, 2 * GROUP), BF),
            pltpu.VMEM((8, 256), F32),
            pltpu.VMEM((4, TOK, GROUP), BF),
            pltpu.SemaphoreType.DMA((3,)),
        ],
        compiler_params=pltpu.CompilerParams(vmem_limit_bytes=12 * MIB),
        cost_estimate=pl.CostEstimate(flops=4 * 5 * 3 * 256 * 256 * 64, bytes_accessed=3 << 20, transcendentals=5 * 3 * 65536),
        name="attend",
    )(me, core, *blocks, own, sib, starts)


def feed_kernel(
    depth, me, x, gain, b0, b1, b2, b3, wo, wg, wu, wd,
    result, acts_out, middle_out, slopes_out,
    groups, acts, middle_b, slopes, sems,
):
    stores = [
        pltpu.make_async_copy(source, out, sems.at[i])
        for i, (source, out) in enumerate(((acts, acts_out), (middle_b, middle_out), (slopes, slopes_out)))
    ]
    mine = me[0]
    for d, b in enumerate((b0, b1, b2, b3)):
        groups[lax.rem(mine - d + 4, 4)] = b[...]
    mixed = jnp.concatenate([groups[g] for g in range(4)], axis=1)
    acts[:, D : 2 * D] = mixed
    middle = x[...] + mm(mixed, wo[depth])
    middle_b[...] = middle
    stores[1].start()
    normed2 = (middle * norm_factor(middle) * gain[...]).astype(BF)
    acts[:, :D] = normed2
    gate = mm(normed2, wg[depth])
    sigma = 1.0 / (1.0 + jnp.exp(-gate))
    swish = gate * sigma
    up = mm(normed2, wu[depth])
    hidden = (swish * up).astype(BF)
    acts[:, 2 * D :] = hidden
    stores[0].start()
    slopes[:, :FF] = up * sigma * (1.0 + gate * (1.0 - sigma))
    slopes[:, FF:] = swish
    stores[2].start()
    result[...] = middle + mm(hidden, wd[depth])
    for store in stores:
        store.wait()


def feed(depth, me, x, gain, blocks, wo, wg, wu, wd):
    return pl.pallas_call(
        lambda *refs: feed_kernel(depth, *refs),
        out_shape=[
            sds((TOK, D), F32), stored((TOK, 2 * D + FF), BF), stored((TOK, D), F32), stored((TOK, 2 * FF), F32),
        ],
        in_specs=[SMEM] + [VMEM] * 10,
        out_specs=[VMEM] + [HBM] * 3,
        scratch_shapes=[
            pltpu.VMEM((4, TOK, GROUP), BF),
            pltpu.VMEM((TOK, 2 * D + FF), BF),
            pltpu.VMEM((TOK, D), F32),
            pltpu.VMEM((TOK, 2 * FF), F32),
            pltpu.SemaphoreType.DMA((3,)),
        ],
        compiler_params=pltpu.CompilerParams(vmem_limit_bytes=16 * MIB),
        cost_estimate=pl.CostEstimate(flops=2 * TOK * D * (D + 3 * FF), bytes_accessed=2 * D * (D + 3 * FF), transcendentals=TOK * FF),
        name="feed",
    )(me, x, gain, *blocks, *pinned(wo, wg, wu, wd))


def feed_back_kernel(
    depth, me, grad, middle, slopes, gain, wd, wg, wu, wo,
    right_ref, dmid_ref, o0, o1, o2, o3,
    groups, slopes_b, middle_b, sems,
):
    stores = [
        pltpu.make_async_copy(source, buf, sems.at[i])
        for i, (source, buf) in enumerate(((slopes, slopes_b), (middle, middle_b)))
    ]
    for store in stores:
        store.start()
    g = grad[...]
    gb = g.astype(BF)
    right_ref[:, 2 * FF : 2 * FF + D] = gb
    dhidden = mm_rt(gb, wd[depth])
    stores[0].wait()
    dgate = (dhidden * slopes_b[:, :FF]).astype(BF)
    dup = (dhidden * slopes_b[:, FF:]).astype(BF)
    right_ref[:, :FF] = dgate
    right_ref[:, FF : 2 * FF] = dup
    dn = mm_rt(dgate, wg[depth]) + mm_rt(dup, wu[depth])
    stores[1].wait()
    mid = middle_b[...]
    factor = norm_factor(mid)
    s = mid * factor
    inner = dn * gain[...]
    dmid = g + factor * (inner - s * jnp.mean(inner * s, axis=-1, keepdims=True))
    dmid_ref[...] = dmid
    dmb = dmid.astype(BF)
    right_ref[:, 2 * FF + D :] = dmb
    dmixed = mm_rt(dmb, wo[depth]).astype(BF)
    for j in range(4):
        groups[j] = dmixed[:, GROUP * j : GROUP * j + GROUP]
    mine = me[0]
    for d, o in enumerate((o0, o1, o2, o3)):
        o[...] = groups[lax.rem(mine + d, 4)]


def feed_back(depth, me, grad, middle, slopes, gain, wd, wg, wu, wo):
    return pl.pallas_call(
        lambda *refs: feed_back_kernel(depth, *refs),
        out_shape=[sds((TOK, 2 * FF + 2 * D), BF), sds((TOK, D), F32)]
        + [sds((TOK, GROUP), BF)] * 4,
        in_specs=[SMEM, VMEM] + [HBM] * 2 + [VMEM] * 5,
        out_specs=[VMEM] * 6,
        scratch_shapes=[
            pltpu.VMEM((4, TOK, GROUP), BF),
            pltpu.VMEM((TOK, 2 * FF), F32),
            pltpu.VMEM((TOK, D), F32),
            pltpu.SemaphoreType.DMA((2,)),
        ],
        compiler_params=pltpu.CompilerParams(vmem_limit_bytes=16 * MIB),
        cost_estimate=pl.CostEstimate(flops=2 * TOK * D * (D + 3 * FF), bytes_accessed=2 * D * (D + 3 * FF), transcendentals=TOK * FF),
        name="feed_back",
    )(me, grad, *map(at_rest, (middle, slopes)), gain, *pinned(wd, wg, wu, wo))


def attend_back_kernel(me, core, q, kv, starts, lse, b0, b1, b2, b3, dq, own, sib, dout, dk, dv):
    mine = me[0]
    for d, b in enumerate((b0, b1, b2, b3)):
        rows = pl.ds(pl.multiple_of(lax.rem(mine - d + 4, 4) * TOK, TOK), TOK)
        dout[rows, :] = b[...]

    def tile(which, pos, first):
        n = 256 * (pos + 1)
        start = starts[which : which + 1, :]
        dqs = []
        for h in range(3):
            lanes = slice(64 * h, 64 * h + 64)
            qs = q[256 * which : 256 * which + 256, lanes] * jnp.asarray(0.125, BF)
            do = dout[256 * which : 256 * which + 256, lanes]
            k = kv[0:n, lanes]
            v = kv[0:n, GROUP + 64 * h : GROUP + 64 * h + 64]
            s = tile_scores(qs, k, start, 256 * pos, n)
            p = jnp.exp(s - lse[3 * which + h : 3 * which + h + 1, :])
            dp = mm_rt(v, do)
            delta = jnp.sum(p * dp, axis=0, keepdims=True)
            ds = (p * (dp - delta)).astype(BF)
            dk_h = mm(ds, qs)
            dv_h = mm(p.astype(BF), do)
            if first:
                dk[0:n, lanes] = dk_h
                dv[0:n, lanes] = dv_h
            else:
                dk[0:n, lanes] += dk_h
                dv[0:n, lanes] += dv_h
            dqs.append(mm_lt(k, ds))
        out = jnp.concatenate(dqs, axis=0).T * 0.125
        dq[256 * which : 256 * which + 256, :] = out

    def put(target, rows, tile_no):
        target[rows : rows + 256, :GROUP] = dk[256 * tile_no : 256 * tile_no + 256, :].astype(target.dtype)
        target[rows : rows + 256, GROUP:] = dv[256 * tile_no : 256 * tile_no + 256, :].astype(target.dtype)

    @pl.when(core[0] == 0)
    def _():
        tile(1, 3, True)
        tile(0, 0, False)
        put(own, 0, 0)
        put(sib, 256, 1)
        put(sib, 0, 2)
        put(own, 256, 3)

    @pl.when(core[0] == 1)
    def _():
        tile(0, 2, True)
        tile(1, 1, False)
        dk[768:1024, :] = jnp.zeros((256, GROUP), F32)
        dv[768:1024, :] = jnp.zeros((256, GROUP), F32)
        put(sib, 0, 0)
        put(own, 256, 1)
        put(own, 0, 2)
        put(sib, 256, 3)


def attend_back(me, core, q, kv, starts, lse, blocks):
    return pl.pallas_call(
        attend_back_kernel,
        out_shape=[sds((4 * TOK, GROUP), F32), sds((4 * TOK, 2 * GROUP), F32), sds((4 * TOK, 2 * GROUP), BF)],
        in_specs=[SMEM, SMEM] + [VMEM] * 8,
        out_specs=[VMEM] * 3,
        scratch_shapes=[
            pltpu.VMEM((4 * TOK, GROUP), BF),
            pltpu.VMEM((ROW, GROUP), F32),
            pltpu.VMEM((ROW, GROUP), F32),
        ],
        compiler_params=pltpu.CompilerParams(vmem_limit_bytes=16 * MIB),
        cost_estimate=pl.CostEstimate(flops=10 * 5 * 3 * 256 * 256 * 64, bytes_accessed=4 << 20, transcendentals=5 * 3 * 65536),
        name="attend_back",
    )(me, core, at_rest(q), at_rest(kv), starts, at_rest(lse), *blocks)


def turn_group(values, cos, sin):
    lane = lax.broadcasted_iota(jnp.int32, (values.shape[0], 128), 1)
    even = lane % 2 == 0
    tail = jnp.concatenate([values[:, 128:], jnp.zeros((values.shape[0], 64), F32)], axis=1)
    parts = []
    for v in (values[:, :128], tail):
        swapped = jnp.where(even, pltpu.roll(v, 127, 1), pltpu.roll(v, 1, 1))
        parts.append(v * cos + swapped * sin)
    return jnp.concatenate([parts[0], parts[1][:, :64]], axis=1)


def spread_kernel(me, dq, own, got, cos, sin, right, o0, o1, o2, o3):
    mine = me[0]
    right[:, :GROUP] = turn_group(dq[...], cos[...], -sin[...]).astype(BF)
    dk = own[:, :GROUP] + got[:, :GROUP].astype(F32)
    right[:, GROUP : 2 * GROUP] = turn_group(dk, cos[...], -sin[...]).astype(BF)
    right[:, 2 * GROUP : 3 * GROUP] = (own[:, GROUP:] + got[:, GROUP:].astype(F32)).astype(BF)
    right[:, 3 * GROUP :] = jnp.zeros((4 * TOK, 64), BF)
    for d, o in enumerate((o0, o1, o2, o3)):
        rows = pl.ds(pl.multiple_of(lax.rem(mine + d, 4) * TOK, TOK), TOK)
        o[...] = right[rows, : 3 * GROUP]


def spread(me, dq, own, got, cos, sin):
    right, *blocks = pl.pallas_call(
        spread_kernel,
        out_shape=[sds((4 * TOK, 3 * GROUP + 64), BF)] + [sds((TOK, 3 * GROUP), BF)] * 4,
        in_specs=[SMEM] + [VMEM] * 5,
        out_specs=[VMEM] * 5,
        compiler_params=pltpu.CompilerParams(vmem_limit_bytes=8 * MIB),
        cost_estimate=pl.CostEstimate(flops=1 << 20, bytes_accessed=2 << 20, transcendentals=0),
        name="spread",
    )(me, dq, own, got, cos, sin)
    return right, blocks


def project_back_kernel(depth, me, dmid, x, gain, b0, b1, b2, b3, wq, wk, wv, grad_ref, groups):
    mine = me[0]
    for d, b in enumerate((b0, b1, b2, b3)):
        groups[lax.rem(mine - d + 4, 4)] = b[...]
    da = jnp.zeros((TOK, D), F32)
    for i, w in enumerate((wq, wk, wv)):
        y = jnp.concatenate([groups[g, :, GROUP * i : GROUP * i + GROUP] for g in range(4)], axis=1)
        da = da + mm_rt(y, w[depth])
    values = x[...]
    factor = norm_factor(values)
    s = values * factor
    inner = da * gain[...]
    grad_ref[...] = dmid[...] + factor * (inner - s * jnp.mean(inner * s, axis=-1, keepdims=True))


def project_back(depth, me, dmid, x, gain, blocks, wq, wk, wv):
    return pl.pallas_call(
        lambda *refs: project_back_kernel(depth, *refs),
        out_shape=sds((TOK, D), F32),
        in_specs=[SMEM] + [VMEM] * 10,
        out_specs=VMEM,
        scratch_shapes=[pltpu.VMEM((4, TOK, 3 * GROUP), BF)],
        compiler_params=pltpu.CompilerParams(vmem_limit_bytes=16 * MIB),
        cost_estimate=pl.CostEstimate(flops=2 * TOK * D * D * 3, bytes_accessed=3 * D * D * 2, transcendentals=0),
        name="project_back",
    )(me, dmid, x, gain, *blocks, *pinned(wq, wk, wv))


def exchange_x(blocks):
    return (blocks[0],) + tuple(send(blocks[d], SHIFT_X[d]) for d in (1, 2, 3))


def left_kernel(jobs, core, acts, acts_sib, both, turned):
    mine = core[0]
    row = 0
    for first, axes in jobs:
        hot = None if first == 2 * D else one_hot(axes, mine)
        for side, source in enumerate((acts, acts_sib)):
            lanes = slice(TOK * side, TOK * side + TOK)
            if hot is None:
                turned[...] = source[:, first : first + FF].T.reshape(FF // 16, 16, TOK)
                half = block_order(axes).reshape(2, 64)
                for i in range(64):
                    block = jnp.where(mine == 0, int(half[0, i]), int(half[1, i]))
                    both[row + 16 * i : row + 16 * i + 16, lanes] = turned[block]
            else:
                both[row : row + D // 2, lanes] = mm_rt(hot, source[:, first : first + D]).astype(BF)
        row += FF // 2 if hot is None else D // 2


def left_sides(core, acts, acts_sib, jobs):
    rows = sum(FF // 2 if first == 2 * D else D // 2 for first, _ in jobs)
    return pl.pallas_call(
        lambda *refs: left_kernel(jobs, *refs),
        out_shape=stored((rows, 2 * TOK), BF),
        in_specs=[SMEM] + [VMEM] * 2,
        out_specs=VMEM,
        scratch_shapes=[pltpu.VMEM((FF // 16, 16, TOK), BF)],
        compiler_params=pltpu.CompilerParams(vmem_limit_bytes=14 * MIB),
        cost_estimate=pl.CostEstimate(flops=8 * 2 * D * D * TOK, bytes_accessed=6 << 20, transcendentals=0),
        name="left_sides",
    )(core, at_rest(acts), acts_sib)


def along_kernel(me, n0, n1, n2, n3, along, rows):
    mine = me[0]
    for d, n in enumerate((n0, n1, n2, n3)):
        rows[pl.ds(pl.multiple_of(lax.rem(mine - d + 4, 4) * TOK, TOK), TOK), :] = n[...]
    for side in range(2):
        along[D // 2 * side : D // 2 * side + D // 2, :] = mm_rt(one_hot("yzx", side, True), rows[...]).astype(BF)


def left_along(me, normed):
    return pl.pallas_call(
        along_kernel,
        out_shape=stored((D, 4 * TOK), BF),
        in_specs=[SMEM] + [VMEM] * 4,
        out_specs=VMEM,
        scratch_shapes=[pltpu.VMEM((4 * TOK, D), BF)],
        compiler_params=pltpu.CompilerParams(vmem_limit_bytes=10 * MIB),
        cost_estimate=pl.CostEstimate(flops=8 * D * D * TOK, bytes_accessed=3 << 20, transcendentals=0),
        name="left_along",
    )(me, *normed)


def rows_kernel(flat, wq, wk, wv, wg, wu, na, nf, rq, rk, rv, rg, ru, gains, bq, bk, bv, bg, bu, sems):
    first = flat[0] * 6
    start = pl.multiple_of(jnp.minimum((first >> 4) << 4, D - 32), 16)
    copies = [
        pltpu.make_async_copy(w.at[:, pl.ds(start, 32), :], buf, sems.at[i])
        for i, (w, buf) in enumerate(((wq, bq), (wk, bk), (wv, bv), (wg, bg), (wu, bu)))
    ]
    for copy in copies:
        copy.start()
    lane = lax.broadcasted_iota(jnp.int32, (8, D), 1)
    pick = lane == lax.broadcasted_iota(jnp.int32, (8, D), 0) + first
    column = lax.broadcasted_iota(jnp.int32, (8, TOK), 1)
    result = jnp.ones((8, TOK), F32)
    for i, row in enumerate((na[0:1, :], na[1:2, :], nf[0:1, :], nf[1:2, :])):
        value = jnp.sum(jnp.where(pick, row, 0.0), axis=1, keepdims=True)
        result = jnp.where(column == i, value, result)
    gains[...] = result
    place = lax.broadcasted_iota(jnp.int32, (8, 32), 1)
    hot = jnp.where(place == lax.broadcasted_iota(jnp.int32, (8, 32), 0) + (first - start), 1.0, 0.0).astype(BF)
    for copy, buf, out in zip(copies, (bq, bk, bv, bg, bu), (rq, rk, rv, rg, ru)):
        copy.wait()
        for layer in range(2):
            out[layer] = mm(hot, buf[layer])


def own_rows(flat, wq, wk, wv, wg, wu, na, nf):
    return pl.pallas_call(
        rows_kernel,
        out_shape=[stored((2, 8, D), F32)] * 3 + [stored((2, 8, FF), F32)] * 2 + [stored((8, TOK), F32)],
        in_specs=[SMEM] + [HBM] * 5 + [VMEM] * 2,
        out_specs=[VMEM] * 6,
        scratch_shapes=[pltpu.VMEM((2, 32, D), BF)] * 3
        + [pltpu.VMEM((2, 32, FF), BF)] * 2
        + [pltpu.SemaphoreType.DMA((5,))],
        compiler_params=pltpu.CompilerParams(vmem_limit_bytes=6 * MIB),
        cost_estimate=pl.CostEstimate(flops=1 << 20, bytes_accessed=1 << 20, transcendentals=0),
        name="own_rows",
    )(flat, *map(at_rest, (wq, wk, wv, wg, wu)), na, nf)


def slot(rows):
    return -(-rows // 16) * 16


class Member:
    def __init__(self, kept, rows, tiles, offset):
        self.kept, self.rows, self.tiles, self.offset = kept, rows, tiles, offset
        self.got = None


def for_tiles(tiles, body):
    if tiles <= 6:
        for t in range(tiles):
            body(t)
    else:
        @pl.loop(0, tiles // 2)
        def _(i):
            body(2 * i)
            body(2 * i + 1)


def aligned(value):
    return value if isinstance(value, int) else pl.multiple_of(value, 16)


def sums_kernel(tasks, bits, *refs):
    for task in tasks:
        kind, bit = task["kind"], bits[task["bit"]]
        pack, offset, kept_ref = refs[task["pack"]], task["offset"], refs[task["kept"]]
        half, tiles = task["half"], task["tiles"]
        out_slot = slot(half)
        if kind == "weights":
            left, right, right_sib = (refs[i] for i in task["ins"])
            for out, base, side in ((pack, offset, 1 - bit), (kept_ref, 0, bit)):
                lhs = left[pl.ds(pl.multiple_of(task["row"] + side * half, 64), half), :]
                for t in range(0, tiles, 2):
                    col = task["column"] + TOK * t
                    rhs = jnp.concatenate(
                        [right[:, col : col + 2 * TOK], right_sib[:, col : col + 2 * TOK]], axis=0
                    )
                    part = mm(lhs, rhs).astype(BF)
                    out[base + t * half : base + (t + 1) * half, :] = part[:, :TOK]
                    out[base + (t + 1) * half : base + (t + 2) * half, :] = part[:, TOK:]
        elif kind == "along":
            left, right = (refs[i] for i in task["ins"])
            for out, base, side in ((pack, offset, 1 - bit), (kept_ref, 0, bit)):
                part = mm(left[pl.ds(pl.multiple_of(side * half, 64), half), :], right[...]).astype(BF)
                for t in range(tiles):
                    out[base + t * half : base + (t + 1) * half, :] = part[:, TOK * t : TOK * t + TOK]
        else:
            value, got = (refs[i] for i in task["ins"])
            came, in_slot = task["came"], slot(2 * half)

            def one(t, half=half, out_slot=out_slot, in_slot=in_slot, came=came, offset=offset, bit=bit,
                    value=value, got=got, pack=pack, kept_ref=kept_ref):
                if half % 16 == 0:
                    for out, base, side in ((pack, offset, 1 - bit), (kept_ref, 0, bit)):
                        at = t * in_slot + side * half
                        total = (
                            value[pl.ds(pl.multiple_of(at, 16), half), :].astype(F32)
                            + got[pl.ds(pl.multiple_of(came + at, 16), half), :].astype(F32)
                        )
                        out[pl.ds(aligned(base + t * out_slot), half), :] = total.astype(BF)
                else:
                    total = (
                        value[pl.ds(aligned(t * in_slot), 2 * half), :].astype(F32)
                        + got[pl.ds(aligned(came + t * in_slot), 2 * half), :].astype(F32)
                    )
                    low, high = total[:half], total[half:]
                    pack[pl.ds(aligned(offset + t * out_slot), half), :] = jnp.where(bit == 0, high, low).astype(BF)
                    kept_ref[pl.ds(aligned(t * out_slot), half), :] = jnp.where(bit == 0, low, high).astype(BF)

            for_tiles(tiles, one)


def sums(bits, jobs):
    arrays, tasks, pack_rows, rest = [], [], {}, []

    def at(array):
        for i, a in enumerate(arrays):
            if a is array:
                return i
        arrays.append(array)
        return len(arrays) - 1

    flops = 0
    for job in jobs:
        if job[0] == "weights":
            _, left, row, rows, right, right_sib, column, columns, bit, pack = job
            rest.append(left)
            task = dict(kind="weights", ins=[at(left), at(right), at(right_sib)], row=row, column=column,
                        half=rows // 2, tiles=columns // TOK, bit=BIT[bit])
            flops += 4 * rows * columns * TOK
        elif job[0] == "along":
            _, left, right, pack = job
            rest.append(left)
            task = dict(kind="along", ins=[at(left), at(right)], half=D // 2, tiles=right.shape[1] // TOK, bit=BIT["c"])
            flops += 2 * D * right.shape[1] * 4 * TOK
        else:
            _, member, bit, pack = job
            task = dict(kind="step", ins=[at(member.kept), at(member.got)], came=member.offset,
                        half=member.rows // 2, tiles=member.tiles, bit=BIT[bit])
        task["pack"], task["offset"] = pack, pack_rows.get(pack, 0)
        pack_rows[pack] = task["offset"] + task["tiles"] * slot(task["half"])
        tasks.append(task)
    names = sorted(pack_rows)
    shapes = [sds((pack_rows[n], TOK), BF) for n in names]
    for i, task in enumerate(tasks):
        task["kept"] = len(arrays) + len(names) + i
        task["pack"] = len(arrays) + names.index(task["pack"])
        shapes.append(sds((task["tiles"] * slot(task["half"]), TOK), BF))
    moved = sum(a.size for a in arrays) + sum(np.prod(s.shape) for s in shapes)
    outs = pl.pallas_call(
        lambda *refs: sums_kernel(tasks, *refs),
        out_shape=shapes,
        in_specs=[SMEM] + [VMEM] * len(arrays),
        out_specs=[VMEM] * len(shapes),
        compiler_params=pltpu.CompilerParams(vmem_limit_bytes=20 * MIB),
        cost_estimate=pl.CostEstimate(flops=flops, bytes_accessed=int(moved) * 2, transcendentals=0),
        name="sums",
    )(bits, *(at_rest(a) if any(a is r for r in rest) else a for a in arrays))
    packs = dict(zip(names, outs))
    members = [
        Member(kept, task["half"], task["tiles"], task["offset"]) for kept, task in zip(outs[len(names) :], tasks)
    ]
    return packs, members


def came(members, got):
    for member in members:
        member.got = got


def pieces_kernel(offsets, ranks, *refs):
    outs, ordered = refs[-5:-1], refs[-1]
    for m, offset in enumerate(offsets):
        value, got = refs[2 * m], refs[2 * m + 1]
        for t in range(5):
            total = value[32 * t : 32 * t + 24, :].astype(F32) + got[offset + 32 * t : offset + 32 * t + 24, :].astype(F32)
            for r in range(4):
                at = 80 * m + 16 * t
                ordered[r, at : at + 6, :] = total[6 * r : 6 * r + 6].astype(BF)
    for d, out in enumerate(outs):
        out[...] = ordered[ranks[d]]


def pieces(ranks, members):
    args = []
    for member in members:
        args += [member.kept, member.got]
    offsets = [member.offset for member in members]
    rows = 80 * len(members)
    return pl.pallas_call(
        lambda *refs: pieces_kernel(offsets, *refs),
        out_shape=[sds((rows, TOK), BF)] * 4,
        in_specs=[SMEM] + [VMEM] * len(args),
        out_specs=[VMEM] * 4,
        scratch_shapes=[pltpu.VMEM((4, rows, TOK), BF)],
        compiler_params=pltpu.CompilerParams(vmem_limit_bytes=4 * MIB),
        cost_estimate=pl.CostEstimate(flops=1 << 16, bytes_accessed=1 << 19, transcendentals=0),
        name="pieces",
    )(ranks, *args)


def finish_kernel(plan, me, *refs):
    p = refs[:4]
    arrays = refs[10:-17]
    gq, gk, gv, go, ggate, gup, gdown, gattn, gffn, by_x = refs[-17:-7]
    wq, wk, wv, wg, wu, gains = refs[-7:-1]
    copies = [
        pltpu.make_async_copy(source, buf, refs[-1].at[i]) for i, (source, buf) in enumerate(zip(refs[4:10], refs[-7:-1]))
    ]
    for copy in copies:
        copy.start()
    mine = me[0]
    for d in range(4):
        by_x[lax.rem(mine - d + 4, 4)] = p[d][...]

    def total(name):
        kept, got, offset, tiles, rows = plan[name]
        parts = []
        for t in range(tiles):
            parts.append(
                arrays[kept][16 * t : 16 * t + rows, :].astype(F32)
                + arrays[got][offset + 16 * t : offset + 16 * t + rows, :].astype(F32)
            )
        return jnp.concatenate(parts, axis=1)

    lane = lax.broadcasted_iota(jnp.int32, (8, TOK), 1)
    result = jnp.zeros((8, TOK), F32)
    filler = jnp.zeros((2, 1), F32)
    for copy in copies:
        copy.wait()
    for layer in range(2):
        m = 1 - layer
        rows = [
            jnp.concatenate(
                [by_x[x, 80 * m + 16 * t : 80 * m + 16 * t + 6, :] for t in range(5)], axis=1
            )
            for x in range(4)
        ]
        acc = jnp.zeros((6, 1), F32)
        for i, (out, w) in enumerate(((gq, wq), (gk, wk), (gv, wv))):
            value = jnp.concatenate([r[:, GROUP * i : GROUP * i + GROUP] for r in rows], axis=1).astype(F32)
            out[:, layer, :] = value
            acc = acc + jnp.sum(value * w[layer][:6], axis=1, keepdims=True)
        result = jnp.where(lane == layer, jnp.concatenate([acc / gains[:6, layer : layer + 1], filler], axis=0), result)
        if layer == 0:
            gate, up = total("gate0"), total("up0")
        else:
            both = total("gu1")
            gate, up = both[:, :FF], both[:, FF:]
        ggate[:, layer, :] = gate
        gup[:, layer, :] = up
        acc = jnp.sum(gate * wg[layer][:6], axis=1, keepdims=True) + jnp.sum(
            up * wu[layer][:6], axis=1, keepdims=True
        )
        result = jnp.where(lane == 2 + layer, jnp.concatenate([acc / gains[:6, 2 + layer : 3 + layer], filler], axis=0), result)
        go[:, layer, :] = total(f"out{layer}")
        gdown[layer] = total(f"down{layer}")
    turned = result.T
    gattn[...] = turned[0:2, :6]
    gffn[...] = turned[2:4, :6]


def finish(me, blocks, rows_of, members):
    arrays, plan = [], {}

    def at(array):
        for i, a in enumerate(arrays):
            if a is array:
                return i
        arrays.append(array)
        return len(arrays) - 1

    for name, m in members.items():
        plan[name] = (at(m.kept), at(m.got), m.offset, m.tiles, m.rows)
    return pl.pallas_call(
        lambda *refs: finish_kernel(plan, *refs),
        out_shape=[sds((6, 2, D), F32)] * 4
        + [sds((6, 2, FF), F32)] * 2
        + [sds((2, 16, D), F32), sds((2, 6), F32), sds((2, 6), F32)],
        in_specs=[SMEM] + [VMEM] * 4 + [HBM] * 6 + [VMEM] * len(arrays),
        out_specs=[VMEM] * 9,
        scratch_shapes=[pltpu.VMEM((4,) + blocks[0].shape, BF)]
        + [pltpu.VMEM((2, 8, D), F32)] * 3
        + [pltpu.VMEM((2, 8, FF), F32)] * 2
        + [pltpu.VMEM((8, TOK), F32), pltpu.SemaphoreType.DMA((6,))],
        compiler_params=pltpu.CompilerParams(vmem_limit_bytes=8 * MIB),
        cost_estimate=pl.CostEstimate(flops=1 << 18, bytes_accessed=2 << 20, transcendentals=0),
        name="finish",
    )(me, *blocks, *map(at_rest, rows_of), *arrays)


def tie(value, *others):
    return lax.optimization_barrier((value,) + others)[0]


BIT = {(axis, step): 2 * i + step for i, axis in enumerate("xyz") for step in (0, 1)}
BIT.update({(axis, step, "swapped"): 6 + 2 * i + step for i, axis in enumerate("xyz") for step in (0, 1)})
BIT["c"] = 12


def rank_of(core, at):
    return jnp.where(core == 0, jnp.where(at == 0, 0, jnp.where(at == 3, 1, at + 1)), at)


def all_bits(spot):
    bits = []
    for core in (spot["c"], 1 - spot["c"]):
        for axis in "xyz":
            rank = rank_of(core, spot[axis])
            bits += [rank // 2, rank % 2]
    return jnp.stack(bits + [spot["c"]]).astype(jnp.int32)


def rope_tables(inside):
    offset = jnp.maximum(inside - 1, 0)
    grid_rows = (offset // GRID).astype(F32)
    grid_cols = (offset % GRID).astype(F32)
    live = (inside > 0).astype(F32)
    freqs = 10000.0 ** (-4.0 * jnp.arange(HEAD_DIM // 4, dtype=F32) / HEAD_DIM)
    angles = jnp.concatenate([grid_rows[:, None] * freqs[None, :], grid_cols[:, None] * freqs[None, :]], axis=1)
    angles = angles * live[:, None]
    cos = jnp.tile(jnp.repeat(jnp.cos(angles), 2, axis=1), (1, 2))
    signs = jnp.tile(jnp.array([-1.0, 1.0], F32), 64)
    sin = jnp.tile(jnp.repeat(jnp.sin(angles), 2, axis=1), (1, 2)) * signs[None, :]
    return cos, sin


def segment_starts(lengths, places):
    ends = jnp.cumsum(lengths)
    starts = ends - lengths
    member = (places[:, None] >= starts[None, :]) & (places[:, None] < ends[None, :])
    return jnp.sum(jnp.where(member, starts[None, :], 0), axis=1)


def per_device(
    tokens, seg_lengths, cotangent, norm_attn, w_query, w_key, w_value, w_out, norm_ffn, w_gate, w_up, w_down
):
    seq = lax.axis_index("seq")
    batch = lax.axis_index("batch")
    spot = {
        "x": seq % 4,
        "y": batch // 4,
        "z": (batch // 2) % 2 * 2 + seq // 4,
        "c": batch % 2,
    }
    me = spot["x"].astype(jnp.int32).reshape(1)
    core = spot["c"].astype(jnp.int32).reshape(1)

    with jax.named_scope("S_setup"):
        moved = send(tokens[0], RELOCATE)
        lengths = send(seg_lengths[0], RELOCATE)
        cot = send(cotangent[0], RELOCATE)
        first = jnp.where(spot["c"] == 0, jnp.array([0, 1, 6, 7], jnp.int32), jnp.array([4, 5, 2, 3], jnp.int32))
        ask_places = (first[:, None] * TOK + jnp.arange(TOK, dtype=jnp.int32)[None, :]).reshape(-1)
        begin = segment_starts(lengths, ask_places)
        starts = begin.reshape(2, 256)
        cos_all, sin_all = rope_tables(ask_places - begin)
        bits = all_bits(spot)
        ranks = rank_of(1 - spot["c"], (spot["x"] + jnp.arange(4, dtype=jnp.int32)) % 4).astype(jnp.int32)
        flat = (seq * 16 + batch).astype(jnp.int32).reshape(1)

    layers = w_query.shape[0]
    x = tie(moved, bits, ranks, flat, me, core, starts).astype(F32)
    kept, lefts, normeds, later = [], [], [], None
    for depth in range(layers):
        with jax.named_scope(f"S_ahead{depth}"):
            gain = norm_attn[depth][None]
            gain2 = norm_ffn[depth][None]
            *blocks, normed = project(depth, me, x, gain, cos_all, sin_all, w_query, w_key, w_value)
            normeds.append(normed)
            blocks = exchange_x(blocks)
            if depth == 1:
                lefts.append(
                    left_sides(core, *later, [(0, "xyz"), (0, "yzx"), (D, "zyx"), (2 * D, "zyx")])
                )
                blocks = (tie(blocks[0], lefts[0]),) + tuple(blocks[1:])
            else:
                rows_of = own_rows(flat, w_query, w_key, w_value, w_gate, w_up, norm_attn, norm_ffn)
                blocks = (tie(blocks[0], *rows_of),) + tuple(blocks[1:])
            own = arrange(me, blocks)
            sib = send(own, CORE)
            *blocks, q, kv, lse = attend(me, core, blocks, own, sib, starts)
            result, acts, middle, slopes = feed(
                depth, me, x, gain2, exchange_x(blocks), w_out, w_gate, w_up, w_down
            )
            kept.append((x, gain, gain2, q, kv, lse, middle, slopes))
            later = [acts, send(acts, CORE)]
            x = result
    activations = send(x.astype(BF), RESTORE)[None]
    grad = cot.astype(F32)
    normed_all1 = exchange_x([tie(normeds[1], x)] * 4)

    def step(members, bit, pack):
        return [("step", m, bit, pack) for m in members]

    half = D // 2
    x, gain, gain2, q, kv, lse, middle, slopes = kept[1]
    with jax.named_scope("S_back1"):
        right, dmid, *blocks = feed_back(1, me, grad, middle, slopes, gain2, w_down, w_gate, w_up, w_out)
        blocks[1] = tie(blocks[1], *normed_all1[1:], activations)
        blocks = exchange_x(blocks)
        right_sib = send(right, CORE)
    with jax.named_scope("S_sum1"):
        left = left_sides(core, *later, [(0, "yzx"), (D, "zyx"), (2 * D, "zyx")])
        packs, (gu1, out1, down1) = sums(
            bits,
            [
                ("weights", left, 0, D // 2, tie(right, *blocks), right_sib, 0, 2 * FF, ("y", 0), "y"),
                ("weights", left, half, D // 2, right, right_sib, 2 * FF + D, D, ("z", 0), "z"),
                ("weights", left, 2 * half, FF // 2, right, right_sib, 2 * FF, D, ("z", 0), "z"),
            ],
        )
        came([gu1], send(packs["y"], PAIR["y", 0]))
        came([out1, down1], send(packs["z"], PAIR["z", 0]))
    with jax.named_scope("S_back1"):
        blocks = (tie(blocks[0], packs["y"], packs["z"]),) + tuple(blocks[1:])
        dq, own, sib = attend_back(me, core, q, kv, starts, lse, blocks)
        right1, blocks = spread(me, dq, own, send(sib, CORE), cos_all, sin_all)
        blocks = exchange_x(blocks)
    with jax.named_scope("S_sum1"):
        gu1.kept = tie(gu1.kept, right1)
        packs, (gu1, out1, down1) = sums(bits, step([gu1], ("y", 1), "y") + step([out1, down1], ("z", 1), "z"))
        came([gu1], send(packs["y"], PAIR["y", 1]))
        came([out1, down1], send(packs["z"], PAIR["z", 1]))
    with jax.named_scope("S_back1"):
        along1 = left_along(me, normed_all1)
        blocks = (tie(blocks[0], packs["y"], packs["z"], along1),) + tuple(blocks[1:])
        grad = project_back(1, me, dmid, x, gain, blocks, w_query, w_key, w_value)
        normed_all0 = exchange_x([tie(normeds[0], grad)] * 4)

    x, gain, gain2, q, kv, lse, middle, slopes = kept[0]
    with jax.named_scope("S_back0"):
        right, dmid, *blocks = feed_back(0, me, grad, middle, slopes, gain2, w_down, w_gate, w_up, w_out)
        blocks[1] = tie(blocks[1], *normed_all0[1:])
        blocks = exchange_x(blocks)
        right_sib = send(right, CORE)
    with jax.named_scope("S_sum0"):
        left = lefts[0]
        packs, (gate0, up0, out0, down0, gu1, out1, down1) = sums(
            bits,
            [
                ("weights", left, 0, D // 2, tie(right, *blocks), right_sib, 0, FF, ("x", 0), "x"),
                ("weights", left, half, D // 2, right, right_sib, FF, FF, ("y", 0), "y"),
                ("weights", left, 2 * half, D // 2, right, right_sib, 2 * FF + D, D, ("z", 0), "z"),
                ("weights", left, 3 * half, FF // 2, right, right_sib, 2 * FF, D, ("z", 0), "z"),
            ]
            + step([gu1], ("z", 0), "z")
            + step([out1, down1], ("y", 0), "y"),
        )
        came([gate0], send(packs["x"], PAIR["x", 0]))
        came([up0, out1, down1], send(packs["y"], PAIR["y", 0]))
        came([out0, down0, gu1], send(packs["z"], PAIR["z", 0]))
    with jax.named_scope("S_back0"):
        blocks = (tie(blocks[0], packs["x"], packs["y"], packs["z"]),) + tuple(blocks[1:])
        dq, own, sib = attend_back(me, core, q, kv, starts, lse, blocks)
        right0, blocks = spread(me, tie(dq, gate0.got), own, send(sib, CORE), cos_all, sin_all)
        blocks = exchange_x(blocks)
    with jax.named_scope("S_sum0"):
        along0 = left_along(me, (tie(normed_all0[0], right0),) + tuple(normed_all0[1:]))
        packs, (qkv1, qkv0) = sums(bits, [("along", along1, right1, "c"), ("along", along0, right0, "c")])
        came([qkv1, qkv0], send(packs["c"], CORE))
    with jax.named_scope("S_back0"):
        blocks = (tie(blocks[0], packs["c"]),) + tuple(blocks[1:])
        grad = project_back(0, me, dmid, x, gain, blocks, w_query, w_key, w_value)
        grad_tokens = send(grad.astype(BF), RESTORE).astype(F32)[None]

    with jax.named_scope("S_sum0"):
        gate0.kept = tie(gate0.kept, right0)
        packs, (gate0, up0, out0, down0, gu1, out1, down1, qkv1, qkv0) = sums(
            bits,
            step([gate0], ("x", 1), "x")
            + step([up0], ("y", 1), "y")
            + step([out0, down0, gu1], ("z", 1), "z")
            + step([out1, down1], ("y", 1), "y")
            + step([qkv1, qkv0], ("y", 0, "swapped"), "y"),
        )
        came([gate0], send(packs["x"], PAIR["x", 1]))
        came([up0, out1, down1, qkv1, qkv0], send(packs["y"], PAIR["y", 1]))
        came([out0, down0, gu1], send(packs["z"], PAIR["z", 1]))
        for i in (0, 1):
            packs, (gate0, up0, out0, down0, qkv1, qkv0) = sums(
                bits,
                step([gate0], ("y", i), "y")
                + step([up0], ("z", i), "z")
                + step([out0, down0], ("y", i), "y")
                + step([qkv1, qkv0], ("yz"[i], 1 - i, "swapped"), "yz"[i]),
            )
            got_y = send(packs["y"], PAIR["y", i])
            if i == 1:
                got_y = tie(got_y, grad_tokens)
            got_z = send(packs["z"], PAIR["z", i])
            came([gate0, out0, down0], got_y)
            came([up0], got_z)
            came([qkv1, qkv0], got_y if i == 0 else got_z)
        packs, (gate0, up0, out0, down0, gu1, out1, down1, qkv1, qkv0) = sums(
            bits,
            step([gate0], ("z", 0), "z")
            + step([up0, out0, down0, gu1, out1, down1], ("x", 0), "x")
            + step([qkv1, qkv0], ("z", 1, "swapped"), "z"),
        )
        came([gate0, qkv1, qkv0], send(packs["z"], PAIR["z", 0]))
        came([up0, out0, down0, gu1, out1, down1], send(packs["x"], PAIR["x", 0]))
        packs, (gate0, up0, out0, down0, gu1, out1, down1) = sums(
            bits,
            step([gate0], ("z", 1), "z") + step([up0, out0, down0, gu1, out1, down1], ("x", 1), "x"),
        )
        blocks = exchange_x(pieces(ranks, [qkv1, qkv0]))
        came([gate0], send(packs["z"], PAIR["z", 1]))
        came([up0, out0, down0, gu1, out1, down1], send(packs["x"], PAIR["x", 1]))
        grad_q, grad_k, grad_v, grad_o, grad_gate, grad_up, grad_down, grad_attn, grad_ffn = finish(
            me, blocks, rows_of,
            dict(gate0=gate0, up0=up0, gu1=gu1, out0=out0, out1=out1, down0=down0, down1=down1),
        )
    return (
        activations,
        grad_tokens,
        grad_attn,
        jnp.swapaxes(grad_q, 0, 1),
        jnp.swapaxes(grad_k, 0, 1),
        jnp.swapaxes(grad_v, 0, 1),
        jnp.swapaxes(grad_o, 0, 1),
        grad_ffn,
        jnp.swapaxes(grad_gate, 0, 1),
        jnp.swapaxes(grad_up, 0, 1),
        grad_down,
    )


def solution(mesh):
    rows = P("batch", "seq", None)
    split = P(None, AXES)
    split3 = P(None, AXES, None)
    return jax.shard_map(
        per_device,
        mesh=mesh,
        in_specs=(rows, P("batch", None), rows) + (P(),) * 9,
        out_specs=(rows, rows, split, split3, split3, split3, split3, split, split3, split3, split3),
        check_vma=False,
    )
```

```python
import jax
import jax.numpy as jnp
import numpy as np
from jax import lax
from jax.experimental import pallas as pl
from jax.experimental.pallas import tpu as pltpu
from jax.sharding import PartitionSpec as P

D = 768
HEADS = 12
HEAD_DIM = 64
FF = 2048
ALONG_X = FF + 512
TOK = 128
ROW = 1024
GRID = 16
GROUP = 3 * HEAD_DIM
OFF = {"k": 0, "v": GROUP, "q": 2 * GROUP}
EPS = 1e-05
AXES = ("seq", "batch")
BF = jnp.bfloat16
F32 = jnp.float32
MIB = 1 << 20


def place(flat):
    seq, batch = divmod(flat, 16)
    z_lo, x = divmod(seq, 4)
    y, rest = divmod(batch, 4)
    z_hi, core = divmod(rest, 2)
    return dict(x=x, y=y, z=z_hi * 2 + z_lo, c=core)


def flat_of(p):
    z_hi, z_lo = divmod(p["z"], 2)
    return (z_lo * 4 + p["x"]) * 16 + p["y"] * 4 + z_hi * 2 + p["c"]


def permutation(move):
    pairs = []
    for flat in range(128):
        p = place(flat)
        move(p)
        pairs.append((flat, flat_of(p)))
    return pairs


def move_relocate(p):
    z_hi, z_lo = divmod(p["z"], 2)
    core = p["c"]
    p["z"] = z_hi * 2 + core
    p["c"] = z_lo ^ (1 if p["x"] >= 2 else 0)


RELOCATE = permutation(move_relocate)
RESTORE = sorted((dst, src) for src, dst in RELOCATE)


def move_core(p):
    p["c"] ^= 1


CORE = permutation(move_core)


def shift_x(by):
    def move(p):
        p["x"] = (p["x"] + by) % 4

    return permutation(move)


SHIFT_X = {d: shift_x(d) for d in (1, 2, 3)}


def pair_step(axis, step):
    def move(p):
        at = p[axis]
        p[axis] = at ^ 1 if (p["c"] == 0) == (step == 0) else 3 - at

    return permutation(move)


PAIR = {(axis, step): pair_step(axis, step) for axis in "xyz" for step in (0, 1)}


def relocate_and_shift(by):
    def move(p):
        move_relocate(p)
        p["x"] = (p["x"] + by) % 4

    return permutation(move)


GATHER = {d: relocate_and_shift(d) for d in (1, 2, 3)}


def send(value, pairs):
    return lax.ppermute(value, AXES, pairs)


RING_ORDER = {0: (0, 3, 1, 2), 1: (0, 1, 2, 3)}


def block_order(axes, swapped=""):
    order = []
    for core in (0, 1):
        first, second, third = (RING_ORDER[1 - core if axis in swapped else core] for axis in axes)
        for a in first:
            for b in second:
                for c in third:
                    order.append(flat_of({axes[0]: a, axes[1]: b, axes[2]: c, "c": core}))
    return np.array(order)


def one_hot(axes, core, swapped=""):
    row = lax.broadcasted_iota(jnp.int32, (D // 2, 1), 0)
    block = (row * 10923) >> 16
    within = row - 6 * block
    places = {}
    for i, axis in enumerate(axes):
        at = (block >> (4 - 2 * i)) & 3
        ring = jnp.where(at == 0, 0, jnp.where(at == 1, 3, at - 1))
        places[axis] = jnp.where(core == (1 if axis in swapped else 0), ring, at)
    z = places["z"]
    flat = ((z & 1) * 4 + places["x"]) * 16 + places["y"] * 4 + (z >> 1) * 2 + core
    lane = lax.broadcasted_iota(jnp.int32, (D // 2, D), 1)
    return jnp.where(lane == flat * 6 + within, 1.0, 0.0).astype(BF)


def mm(left, right):
    return jnp.dot(left, right, preferred_element_type=F32)


def mm_rt(left, right):
    return lax.dot_general(left, right, (((1,), (1,)), ((), ())), preferred_element_type=F32)


def mm_lt(left, right):
    return lax.dot_general(left, right, (((0,), (0,)), ((), ())), preferred_element_type=F32)


VMEM = pl.BlockSpec(memory_space=pltpu.VMEM)
SMEM = pl.BlockSpec(memory_space=pltpu.SMEM)
HBM = pl.BlockSpec(memory_space=pltpu.HBM)


def pinned(*weights):
    return tuple(pltpu.with_memory_space_constraint(w, pltpu.VMEM) for w in weights)


def at_rest(value):
    return pltpu.with_memory_space_constraint(value, pltpu.HBM)


def stored(shape, kind):
    return pltpu.HBM(shape, kind)


def sds(shape, kind):
    return jax.ShapeDtypeStruct(shape, kind)


def here():
    seq, batch = lax.axis_index("seq"), lax.axis_index("batch")
    return dict(
        x=lax.rem(seq, 4), y=batch // 4, z=lax.rem(batch // 2, 2) * 2 + seq // 4, c=lax.rem(batch, 2), flat=seq * 16 + batch
    )


def rank_of(core, at):
    return jnp.where(core == 0, jnp.where(at == 0, 0, jnp.where(at == 3, 1, at + 1)), at)


def ordered_by_x(mine, blocks, out):
    for d, b in enumerate(blocks):
        out[lax.rem(mine - d + 4, 4)] = b[...]


def norm_factor(values):
    return lax.rsqrt(jnp.mean(values * values, axis=-1, keepdims=True) + EPS)


def first_norm_kernel(tokens, gain, x, normed):
    values = tokens[...].astype(F32)
    x[...] = values
    normed[...] = (values * norm_factor(values) * gain[0:1, :]).astype(BF)


def first_norm(tokens, gain, first=False):
    return pl.pallas_call(
        first_norm_kernel,
        out_shape=[sds((TOK, D), F32), sds((TOK, D), BF)],
        in_specs=[VMEM] * 2,
        out_specs=[VMEM] * 2,
        compiler_params=pltpu.CompilerParams(vmem_limit_bytes=4 * MIB),
        cost_estimate=pl.CostEstimate(flops=1 << 19, bytes_accessed=1 << 20, transcendentals=0),
        name="first_norm",
    )(*map(at_rest, (tokens, gain)) if first else (tokens, gain))


def tables_kernel(lengths, freqs, cos, sin, starts):
    core = here()["c"]

    def places(shape, dim, base):
        r = lax.broadcasted_iota(jnp.int32, shape, dim) + base
        block = r >> 7
        block = jnp.where(core == 0, jnp.where(block < 2, block, block + 4), jnp.where(block < 2, block + 4, block))
        return (block << 7) + (r & 127)

    def begin(place):
        start = lengths[0] * 0
        result = jnp.zeros_like(place)
        for i in range(5):
            end = start + lengths[i]
            result = jnp.where((place >= start) & (place < end), start, result)
            start = end
        return result

    for half in range(2):
        starts[half : half + 1, :] = begin(places((1, 256), 1, 256 * half))
    place = places((4 * TOK, 1), 0, 0)
    inside = place - begin(place)
    offset = jnp.maximum(inside - 1, 0)
    lane = lax.broadcasted_iota(jnp.int32, (4 * TOK, TOK), 1)
    rows = (offset >> 4).astype(F32)
    columns = (offset & (GRID - 1)).astype(F32)
    angles = jnp.where((lane & 63) < 32, rows, columns) * freqs[...]
    angles = jnp.where(inside > 0, angles, 0.0)
    cos[...] = jnp.cos(angles)
    sin[...] = jnp.where((lane & 1) == 0, -1.0, 1.0) * jnp.sin(angles)


def tables(lengths):
    freqs = 10000.0 ** (-4.0 * np.arange(HEAD_DIM // 4, dtype=np.float32) / HEAD_DIM)
    freqs = np.tile(np.repeat(freqs.astype(np.float32), 2), 4)[None, :]
    return pl.pallas_call(
        tables_kernel,
        out_shape=[sds((4 * TOK, TOK), F32), sds((4 * TOK, TOK), F32), sds((2, 256), jnp.int32)],
        in_specs=[SMEM, VMEM],
        out_specs=[VMEM] * 3,
        compiler_params=pltpu.CompilerParams(vmem_limit_bytes=4 * MIB),
        cost_estimate=pl.CostEstimate(flops=1 << 23, bytes_accessed=1 << 20, transcendentals=1 << 17),
        name="tables",
    )(lengths, jnp.asarray(freqs))


def own_heads_kernel(wq, wk, wv, out, bq, bk, bv, sems):
    x = here()["x"]
    start = pl.multiple_of((x * GROUP // TOK) * TOK, TOK)
    copies = [
        pltpu.make_async_copy(w.at[:, :, pl.ds(start, 2 * TOK)], buf, sems.at[i])
        for i, (w, buf) in enumerate(((wk, bk), (wv, bv), (wq, bq)))
    ]
    for copy in copies:
        copy.start()
    for i, (copy, buf) in enumerate(zip(copies, (bk, bv, bq))):
        copy.wait()
        for layer in range(2):
            w = buf[layer]
            out[layer, :, GROUP * i : GROUP * i + GROUP] = jnp.where(lax.rem(x, 2) == 0, w[:, :GROUP], w[:, 64:])


def own_heads(wq, wk, wv):
    return pl.pallas_call(
        own_heads_kernel,
        out_shape=sds((2, D, 3 * GROUP), BF),
        in_specs=[HBM] * 3,
        out_specs=VMEM,
        scratch_shapes=[pltpu.VMEM((2, D, 2 * TOK), BF)] * 3 + [pltpu.SemaphoreType.DMA((3,))],
        compiler_params=pltpu.CompilerParams(vmem_limit_bytes=8 * MIB),
        cost_estimate=pl.CostEstimate(flops=1 << 20, bytes_accessed=5 << 20, transcendentals=0),
        name="own_heads",
    )(*map(at_rest, (wq, wk, wv)))


def turn_group(values, cos, sin):
    lane = lax.broadcasted_iota(jnp.int32, (values.shape[0], 128), 1)
    even = lane % 2 == 0
    tail = jnp.concatenate([values[:, 128:], jnp.zeros((values.shape[0], 64), F32)], axis=1)
    parts = []
    for v in (values[:, :128], tail):
        swapped = jnp.where(even, pltpu.roll(v, 127, 1), pltpu.roll(v, 1, 1))
        parts.append(v * cos + swapped * sin)
    return jnp.concatenate([parts[0], parts[1][:, :64]], axis=1)


def project_kernel(depth, n0, n1, n2, n3, w, cos, sin, q, own, rows_out, rows, sem):
    ordered_by_x(here()["x"], (n0, n1, n2, n3), rows)
    store = pltpu.make_async_copy(rows, rows_out, sem)
    store.start()
    normed = rows[...].reshape(4 * TOK, D)
    y = mm(normed, w[depth])
    own[:, :GROUP] = turn_group(y[:, :GROUP], cos[...], sin[...]).astype(BF)
    own[:, GROUP:] = y[:, GROUP : 2 * GROUP].astype(BF)
    q[...] = turn_group(y[:, 2 * GROUP :], cos[...], sin[...]).astype(BF)
    store.wait()


def project(depth, normed, w, cos, sin):
    return pl.pallas_call(
        lambda *refs: project_kernel(depth, *refs),
        out_shape=[sds((4 * TOK, GROUP), BF), sds((4 * TOK, 2 * GROUP), BF), stored((4, TOK, D), BF)],
        in_specs=[VMEM] * 7,
        out_specs=[VMEM] * 2 + [HBM],
        scratch_shapes=[pltpu.VMEM((4, TOK, D), BF), pltpu.SemaphoreType.DMA(())],
        compiler_params=pltpu.CompilerParams(vmem_limit_bytes=8 * MIB),
        cost_estimate=pl.CostEstimate(flops=2 * TOK * D * D * 3, bytes_accessed=3 * D * D * 2, transcendentals=0),
        name="project",
    )(*normed, w, cos, sin)


def tile_scores(q, k, start, place0, n):
    raw = mm_rt(k, q)
    keys = lax.broadcasted_iota(jnp.int32, (256, 256), 0)
    asks = lax.broadcasted_iota(jnp.int32, (256, 256), 1)
    parts = []
    for at in range(0, n, 256):
        allowed = keys >= start - at
        if at == place0:
            allowed = allowed & (keys <= asks)
        parts.append(jnp.where(allowed, raw[at : at + 256], -1e30))
    return parts[0] if len(parts) == 1 else jnp.concatenate(parts, axis=0)


def attend_kernel(q, own, sib, starts, m0, m1, m2, m3, q_out, kv_out, lse_out, kv, lse, mixed, sems):
    spot = here()
    core, mine = spot["c"], spot["x"]
    stores = [
        pltpu.make_async_copy(source, out, sems.at[i])
        for i, (source, out) in enumerate(((q, q_out), (kv, kv_out), (lse, lse_out)))
    ]
    stores[0].start()

    @pl.when(core == 0)
    def _():
        kv[0:256, :] = own[0:256, :]
        kv[256:512, :] = sib[256:512, :]
        kv[512:768, :] = sib[0:256, :]
        kv[768:1024, :] = own[256:512, :]

    @pl.when(core == 1)
    def _():
        kv[0:256, :] = sib[0:256, :]
        kv[256:512, :] = own[256:512, :]
        kv[512:768, :] = own[0:256, :]
        kv[768:1024, :] = sib[256:512, :]

    stores[1].start()

    def tile(which, pos):
        n = 256 * (pos + 1)
        outs = []
        start = starts[which : which + 1, :]
        for h in range(3):
            qs = q[256 * which : 256 * which + 256, 64 * h : 64 * h + 64] * jnp.asarray(0.125, BF)
            s = tile_scores(qs, kv[0:n, 64 * h : 64 * h + 64], start, 256 * pos, n)
            top = jnp.max(s, axis=0, keepdims=True)
            e = jnp.exp(s - top)
            total = jnp.sum(e, axis=0, keepdims=True)
            probs = (e * (1.0 / total)).astype(BF)
            lse[3 * which + h : 3 * which + h + 1, :] = top + jnp.log(total)
            outs.append(mm_lt(kv[0:n, GROUP + 64 * h : GROUP + 64 * h + 64], probs))
        out = jnp.concatenate(outs, axis=0).T.astype(BF)
        mixed[2 * which] = out[:TOK]
        mixed[2 * which + 1] = out[TOK:]

    @pl.when(core == 0)
    def _():
        tile(0, 0)
        tile(1, 3)

    @pl.when(core == 1)
    def _():
        tile(0, 2)
        tile(1, 1)

    stores[2].start()
    for d, m in enumerate((m0, m1, m2, m3)):
        m[...] = mixed[lax.rem(mine + d, 4)]
    for store in stores:
        store.wait()


def attend(q, own, sib, starts):
    return pl.pallas_call(
        attend_kernel,
        out_shape=[sds((TOK, GROUP), BF)] * 4
        + [stored((4 * TOK, GROUP), BF), stored((ROW, 2 * GROUP), BF), stored((8, 256), F32)],
        in_specs=[VMEM] * 4,
        out_specs=[VMEM] * 4 + [HBM] * 3,
        scratch_shapes=[
            pltpu.VMEM((ROW, 2 * GROUP), BF),
            pltpu.VMEM((8, 256), F32),
            pltpu.VMEM((4, TOK, GROUP), BF),
            pltpu.SemaphoreType.DMA((3,)),
        ],
        compiler_params=pltpu.CompilerParams(vmem_limit_bytes=8 * MIB),
        cost_estimate=pl.CostEstimate(flops=4 * 5 * 3 * 256 * 256 * 64, bytes_accessed=3 << 20, transcendentals=5 * 3 * 65536),
        name="attend",
    )(q, own, sib, starts)


def feed_kernel(
    depth, x, gain, next_gain, b0, b1, b2, b3, wo, wg, wu, wd,
    result, normed_next, acts_out, middle_out, slopes_out,
    groups, acts, middle_b, slopes, sems,
):
    stores = [
        pltpu.make_async_copy(source, out, sems.at[i])
        for i, (source, out) in enumerate(((acts, acts_out), (middle_b, middle_out), (slopes, slopes_out)))
    ]
    ordered_by_x(here()["x"], (b0, b1, b2, b3), groups)
    mixed = jnp.concatenate([groups[g] for g in range(4)], axis=1)
    acts[:, D : 2 * D] = mixed
    middle = x[...] + mm(mixed, wo[depth])
    middle_b[...] = middle
    stores[1].start()
    normed2 = (middle * norm_factor(middle) * gain[depth : depth + 1, :]).astype(BF)
    acts[:, :D] = normed2
    gate = mm(normed2, wg[depth])
    sigma = 1.0 / (1.0 + jnp.exp(-gate))
    swish = gate * sigma
    up = mm(normed2, wu[depth])
    hidden = (swish * up).astype(BF)
    acts[:, 2 * D :] = hidden
    stores[0].start()
    slopes[:, :FF] = (up * sigma * (1.0 + gate * (1.0 - sigma))).astype(BF)
    slopes[:, FF:] = swish.astype(BF)
    stores[2].start()
    values = middle + mm(hidden, wd[depth])
    if depth == 0:
        result[...] = values
        normed_next[...] = (values * norm_factor(values) * next_gain[1:2, :]).astype(BF)
    else:
        result[...] = values.astype(BF)
        normed_next[...] = jnp.zeros((TOK, D), BF)
    for store in stores:
        store.wait()


def feed(depth, x, gain, next_gain, blocks, wo, wg, wu, wd):
    return pl.pallas_call(
        lambda *refs: feed_kernel(depth, *refs),
        out_shape=[
            sds((TOK, D), BF if depth else F32), sds((TOK, D), BF),
            stored((TOK, 2 * D + FF), BF), stored((TOK, D), F32), stored((TOK, 2 * FF), BF),
        ],
        in_specs=[VMEM] * 11,
        out_specs=[VMEM] * 2 + [HBM] * 3,
        scratch_shapes=[
            pltpu.VMEM((4, TOK, GROUP), BF),
            pltpu.VMEM((TOK, 2 * D + FF), BF),
            pltpu.VMEM((TOK, D), F32),
            pltpu.VMEM((TOK, 2 * FF), BF),
            pltpu.SemaphoreType.DMA((3,)),
        ],
        compiler_params=pltpu.CompilerParams(vmem_limit_bytes=12 * MIB),
        cost_estimate=pl.CostEstimate(flops=2 * TOK * D * (D + 3 * FF), bytes_accessed=2 * D * (D + 3 * FF), transcendentals=TOK * FF),
        name="feed",
    )(x, gain, next_gain, *blocks, *pinned(wo, wg, wu, wd))


def feed_back_kernel(
    depth, carried, grad, middle, slopes, gain, wd, wg, wu, wo, *refs,
):
    acts = refs[:carried]
    right_ref, dmid_ref, o0, o1, o2, o3, groups, slopes_b, middle_b, sems = refs[carried:]
    width = 2 * FF + 2 * D
    carries = [
        pltpu.make_async_copy(source, right_ref.at[:, pl.ds(width + i * (2 * D + FF), 2 * D + FF)], sems.at[2 + i])
        for i, source in enumerate(acts)
    ]
    stores = [
        pltpu.make_async_copy(source, buf, sems.at[i])
        for i, (source, buf) in enumerate(((slopes, slopes_b), (middle, middle_b)))
    ]
    for store in stores + carries:
        store.start()
    g = grad[...].astype(F32)
    gb = g.astype(BF)
    right_ref[:, 2 * FF : 2 * FF + D] = gb
    dhidden = mm_rt(gb, wd[depth])
    stores[0].wait()
    dgate = (dhidden * slopes_b[:, :FF]).astype(BF)
    dup = (dhidden * slopes_b[:, FF:]).astype(BF)
    right_ref[:, :FF] = dgate
    right_ref[:, FF : 2 * FF] = dup
    dn = mm_rt(dgate, wg[depth]) + mm_rt(dup, wu[depth])
    stores[1].wait()
    mid = middle_b[...]
    factor = norm_factor(mid)
    s = mid * factor
    inner = dn * gain[depth : depth + 1, :]
    dmid = g + factor * (inner - s * jnp.mean(inner * s, axis=-1, keepdims=True))
    dmid_ref[...] = dmid
    dmb = dmid.astype(BF)
    right_ref[:, 2 * FF + D : width] = dmb
    dmixed = mm_rt(dmb, wo[depth]).astype(BF)
    for j in range(4):
        groups[j] = dmixed[:, GROUP * j : GROUP * j + GROUP]
    mine = here()["x"]
    for d, o in enumerate((o0, o1, o2, o3)):
        o[...] = groups[lax.rem(mine + d, 4)]
    for carry in carries:
        carry.wait()


def feed_back(depth, grad, middle, slopes, gain, wd, wg, wu, wo, acts):
    width = 2 * FF + 2 * D + len(acts) * (2 * D + FF)
    return pl.pallas_call(
        lambda *refs: feed_back_kernel(depth, len(acts), *refs),
        out_shape=[sds((TOK, width), BF), sds((TOK, D), F32)] + [sds((TOK, GROUP), BF)] * 4,
        in_specs=[VMEM] + [HBM] * 2 + [VMEM] * 5 + [HBM] * len(acts),
        out_specs=[VMEM] * 6,
        scratch_shapes=[
            pltpu.VMEM((4, TOK, GROUP), BF),
            pltpu.VMEM((TOK, 2 * FF), BF),
            pltpu.VMEM((TOK, D), F32),
            pltpu.SemaphoreType.DMA((4,)),
        ],
        compiler_params=pltpu.CompilerParams(vmem_limit_bytes=12 * MIB),
        cost_estimate=pl.CostEstimate(flops=2 * TOK * D * (D + 3 * FF), bytes_accessed=2 * D * (D + 3 * FF), transcendentals=TOK * FF),
        name="feed_back",
    )(grad, *map(at_rest, (middle, slopes)), gain, *pinned(wd, wg, wu, wo), *map(at_rest, acts))


def attend_back_kernel(q, kv, starts, lse, b0, b1, b2, b3, dq, own, sib, dout, dk, dv):
    spot = here()
    core, mine = spot["c"], spot["x"]
    for d, b in enumerate((b0, b1, b2, b3)):
        rows = pl.ds(pl.multiple_of(lax.rem(mine - d + 4, 4) * TOK, TOK), TOK)
        dout[rows, :] = b[...]

    def tile(which, pos, first):
        n = 256 * (pos + 1)
        start = starts[which : which + 1, :]
        dqs = []
        for h in range(3):
            lanes = slice(64 * h, 64 * h + 64)
            qs = q[256 * which : 256 * which + 256, lanes] * jnp.asarray(0.125, BF)
            do = dout[256 * which : 256 * which + 256, lanes]
            k = kv[0:n, lanes]
            v = kv[0:n, GROUP + 64 * h : GROUP + 64 * h + 64]
            s = tile_scores(qs, k, start, 256 * pos, n)
            p = jnp.exp(s - lse[3 * which + h : 3 * which + h + 1, :])
            dp = mm_rt(v, do)
            delta = jnp.sum(p * dp, axis=0, keepdims=True)
            ds = (p * (dp - delta)).astype(BF)
            dk_h = mm(ds, qs)
            dv_h = mm(p.astype(BF), do)
            if first:
                dk[0:n, lanes] = dk_h
                dv[0:n, lanes] = dv_h
            else:
                dk[0:n, lanes] += dk_h
                dv[0:n, lanes] += dv_h
            dqs.append(mm_lt(k, ds))
        out = jnp.concatenate(dqs, axis=0).T * 0.125
        dq[256 * which : 256 * which + 256, :] = out

    def put(target, rows, tile_no):
        target[rows : rows + 256, :GROUP] = dk[256 * tile_no : 256 * tile_no + 256, :].astype(target.dtype)
        target[rows : rows + 256, GROUP:] = dv[256 * tile_no : 256 * tile_no + 256, :].astype(target.dtype)

    @pl.when(core == 0)
    def _():
        tile(1, 3, True)
        tile(0, 0, False)
        put(own, 0, 0)
        put(sib, 256, 1)
        put(sib, 0, 2)
        put(own, 256, 3)

    @pl.when(core == 1)
    def _():
        tile(0, 2, True)
        tile(1, 1, False)
        dk[768:1024, :] = jnp.zeros((256, GROUP), F32)
        dv[768:1024, :] = jnp.zeros((256, GROUP), F32)
        put(sib, 0, 0)
        put(own, 256, 1)
        put(own, 0, 2)
        put(sib, 256, 3)


def attend_back(q, kv, starts, lse, blocks):
    return pl.pallas_call(
        attend_back_kernel,
        out_shape=[sds((4 * TOK, GROUP), F32), sds((4 * TOK, 2 * GROUP), F32), sds((4 * TOK, 2 * GROUP), BF)],
        in_specs=[VMEM] * 8,
        out_specs=[VMEM] * 3,
        scratch_shapes=[
            pltpu.VMEM((4 * TOK, GROUP), BF),
            pltpu.VMEM((ROW, GROUP), F32),
            pltpu.VMEM((ROW, GROUP), F32),
        ],
        compiler_params=pltpu.CompilerParams(vmem_limit_bytes=10 * MIB),
        cost_estimate=pl.CostEstimate(flops=10 * 5 * 3 * 256 * 256 * 64, bytes_accessed=4 << 20, transcendentals=5 * 3 * 65536),
        name="attend_back",
    )(at_rest(q), at_rest(kv), starts, at_rest(lse), *blocks)


def spread_kernel(depth, dq, own, got, cos, sin, w, right, *refs):
    right[:, : GROUP] = turn_group(own[:, :GROUP] + got[:, :GROUP].astype(F32), cos[...], -sin[...]).astype(BF)
    right[:, GROUP : 2 * GROUP] = (own[:, GROUP:] + got[:, GROUP:].astype(F32)).astype(BF)
    right[:, 2 * GROUP : 3 * GROUP] = turn_group(dq[...], cos[...], -sin[...]).astype(BF)
    right[:, 3 * GROUP :] = jnp.zeros((4 * TOK, 64), BF)
    da = mm_rt(right[:, : 3 * GROUP], w[depth]).astype(BF)
    spot = here()
    if depth == 1:
        groups = refs[-1]
        groups[...] = da.reshape(4, TOK, D)
        for d, o in enumerate(refs[:4]):
            o[...] = groups[lax.rem(spot["x"] + d, 4)]
    else:
        (stack,) = refs
        for x in range(4):
            rank = rank_of(1 - spot["c"], x)
            for t in range(6):
                rows = pl.ds(pl.multiple_of((4 * t + rank) * TOK, TOK), TOK)
                stack[rows, :] = da[TOK * x : TOK * x + TOK, TOK * t : TOK * t + TOK]


def spread(depth, dq, own, got, cos, sin, w):
    shapes = [sds((TOK, D), BF)] * 4 if depth == 1 else [sds((6 * 4 * TOK, TOK), BF)]
    right, *blocks = pl.pallas_call(
        lambda *refs: spread_kernel(depth, *refs),
        out_shape=[sds((4 * TOK, 3 * GROUP + 64), BF)] + shapes,
        in_specs=[VMEM] * 6,
        out_specs=[VMEM] * (1 + len(shapes)),
        scratch_shapes=[pltpu.VMEM((4, TOK, D), BF)] if depth == 1 else [],
        compiler_params=pltpu.CompilerParams(vmem_limit_bytes=8 * MIB),
        cost_estimate=pl.CostEstimate(flops=2 * TOK * D * D * 3, bytes_accessed=2 << 20, transcendentals=0),
        name="spread",
    )(dq, own, got, cos, sin, w)
    return right, blocks


def norm_back(da, dmid, x, gain):
    factor = norm_factor(x)
    s = x * factor
    inner = da * gain
    return dmid + factor * (inner - s * jnp.mean(inner * s, axis=-1, keepdims=True))


def project_back_kernel(dmid, x, gain, b0, b1, b2, b3, grad):
    da = b0[...].astype(F32) + b1[...].astype(F32) + b2[...].astype(F32) + b3[...].astype(F32)
    grad[...] = norm_back(da, dmid[...], x[...], gain[1:2, :])


def project_back(dmid, x, gain, blocks):
    return pl.pallas_call(
        project_back_kernel,
        out_shape=sds((TOK, D), F32),
        in_specs=[VMEM] * 7,
        out_specs=VMEM,
        compiler_params=pltpu.CompilerParams(vmem_limit_bytes=6 * MIB),
        cost_estimate=pl.CostEstimate(flops=1 << 20, bytes_accessed=3 << 20, transcendentals=0),
        name="project_back",
    )(dmid, x, gain, *blocks)


def last_grad_kernel(offset, kept, got, dmid, x, gain, activations, back):
    parts = []
    for t in range(6):
        rows = slice(TOK * t, TOK * t + TOK)
        parts.append(kept[rows, :].astype(F32) + got[offset + TOK * t : offset + TOK * t + TOK, :].astype(F32))
    da = jnp.concatenate(parts, axis=1)
    back[:TOK, :] = norm_back(da, dmid[...], x[...], gain[0:1, :]).astype(BF)
    back[TOK:, :] = activations[...]


def last_grad(member, dmid, x, gain, activations):
    return pl.pallas_call(
        lambda *refs: last_grad_kernel(member.offset, *refs),
        out_shape=sds((2 * TOK, D), BF),
        in_specs=[VMEM] * 6,
        out_specs=VMEM,
        compiler_params=pltpu.CompilerParams(vmem_limit_bytes=6 * MIB),
        cost_estimate=pl.CostEstimate(flops=1 << 20, bytes_accessed=3 << 20, transcendentals=0),
        name="last_grad",
    )(member.kept, member.got, dmid, x, gain, activations)


def exchange_x(blocks):
    return (blocks[0],) + tuple(send(blocks[d], SHIFT_X[d]) for d in (1, 2, 3))


def left_kernel(jobs, base, acts, acts_sib, both, turned):
    mine = here()["c"]
    row = 0
    for first, axes, swapped in jobs:
        hot = None if first == 2 * D else one_hot(axes, mine, swapped)
        for side, source in enumerate((acts, acts_sib)):
            lanes = slice(TOK * side, TOK * side + TOK)
            if hot is None:
                turned[...] = source[:, base + first : base + first + FF].T.reshape(FF // 16, 16, TOK)
                half = block_order(axes, swapped).reshape(2, 64)
                for i in range(64):
                    block = jnp.where(mine == 0, int(half[0, i]), int(half[1, i]))
                    both[row + 16 * i : row + 16 * i + 16, lanes] = turned[block]
            else:
                both[row : row + D // 2, lanes] = mm_rt(hot, source[:, base + first : base + first + D]).astype(BF)
        row += FF // 2 if hot is None else D // 2


def left_sides(base, right, right_sib, jobs):
    rows = sum(FF // 2 if first == 2 * D else D // 2 for first, _, _ in jobs)
    return pl.pallas_call(
        lambda *refs: left_kernel(jobs, base, *refs),
        out_shape=stored((rows, 2 * TOK), BF),
        in_specs=[VMEM] * 2,
        out_specs=VMEM,
        scratch_shapes=[pltpu.VMEM((FF // 16, 16, TOK), BF)],
        compiler_params=pltpu.CompilerParams(vmem_limit_bytes=8 * MIB),
        cost_estimate=pl.CostEstimate(flops=8 * 2 * D * D * TOK, bytes_accessed=6 << 20, transcendentals=0),
        name="left_sides",
    )(right, right_sib)


def along_kernel(rows, along):
    normed = rows[...].reshape(4 * TOK, D)
    for side in range(2):
        along[D // 2 * side : D // 2 * side + D // 2, :] = mm_rt(one_hot("yzx", side, "yz"), normed).astype(BF)


def left_along(rows):
    return pl.pallas_call(
        along_kernel,
        out_shape=stored((D, 4 * TOK), BF),
        in_specs=[VMEM],
        out_specs=VMEM,
        compiler_params=pltpu.CompilerParams(vmem_limit_bytes=8 * MIB),
        cost_estimate=pl.CostEstimate(flops=8 * D * D * TOK, bytes_accessed=3 << 20, transcendentals=0),
        name="left_along",
    )(at_rest(rows))


def rows_kernel(wq, wk, wv, wg, wu, na, nf, rq, rk, rv, rg, ru, gains, bq, bk, bv, bg, bu, sems):
    first = here()["flat"] * 6
    start = pl.multiple_of(jnp.minimum((first >> 4) << 4, D - 32), 16)
    copies = [
        pltpu.make_async_copy(w.at[:, pl.ds(start, 32), :], buf, sems.at[i])
        for i, (w, buf) in enumerate(((wq, bq), (wk, bk), (wv, bv), (wg, bg), (wu, bu)))
    ]
    for copy in copies:
        copy.start()
    lane = lax.broadcasted_iota(jnp.int32, (8, D), 1)
    pick = lane == lax.broadcasted_iota(jnp.int32, (8, D), 0) + first
    column = lax.broadcasted_iota(jnp.int32, (8, TOK), 1)
    result = jnp.ones((8, TOK), F32)
    for i, row in enumerate((na[0:1, :], na[1:2, :], nf[0:1, :], nf[1:2, :])):
        value = jnp.sum(jnp.where(pick, row, 0.0), axis=1, keepdims=True)
        result = jnp.where(column == i, value, result)
    gains[...] = result
    place = lax.broadcasted_iota(jnp.int32, (8, 32), 1)
    hot = jnp.where(place == lax.broadcasted_iota(jnp.int32, (8, 32), 0) + (first - start), 1.0, 0.0).astype(BF)
    for copy, buf, out in zip(copies, (bq, bk, bv, bg, bu), (rq, rk, rv, rg, ru)):
        copy.wait()
        for layer in range(2):
            out[layer] = mm(hot, buf[layer])


def own_rows(wq, wk, wv, wg, wu, na, nf):
    return pl.pallas_call(
        rows_kernel,
        out_shape=[stored((2, 8, D), F32)] * 3 + [stored((2, 8, FF), F32)] * 2 + [stored((8, TOK), F32)],
        in_specs=[HBM] * 5 + [VMEM] * 2,
        out_specs=[VMEM] * 6,
        scratch_shapes=[pltpu.VMEM((2, 32, D), BF)] * 3
        + [pltpu.VMEM((2, 32, FF), BF)] * 2
        + [pltpu.SemaphoreType.DMA((5,))],
        compiler_params=pltpu.CompilerParams(vmem_limit_bytes=6 * MIB),
        cost_estimate=pl.CostEstimate(flops=1 << 20, bytes_accessed=1 << 20, transcendentals=0),
        name="own_rows",
    )(*map(at_rest, (wq, wk, wv, wg, wu)), na, nf)


def slot(rows):
    return -(-rows // 16) * 16


class Member:
    def __init__(self, kept, rows, tiles, offset):
        self.kept, self.rows, self.tiles, self.offset = kept, rows, tiles, offset
        self.got = None


def for_tiles(tiles, body):
    if tiles <= 6:
        for t in range(tiles):
            body(t)
    else:
        @pl.loop(0, tiles // 2)
        def _(i):
            body(2 * i)
            body(2 * i + 1)


def aligned(value):
    return value if isinstance(value, int) else pl.multiple_of(value, 16)


def bit_of(spot, which):
    if which == "c":
        return spot["c"]
    axis, step = which[0], which[1]
    rank = rank_of(1 - spot["c"] if len(which) > 2 else spot["c"], spot[axis])
    return rank // 2 if step == 0 else lax.rem(rank, 2)


def sums_kernel(tasks, *refs):
    spot = here()
    for task in tasks:
        kind, bit = task["kind"], bit_of(spot, task["bit"])
        pack, offset, kept_ref = refs[task["pack"]], task["offset"], refs[task["kept"]]
        half, tiles = task["half"], task["tiles"]
        out_slot = slot(half)
        if kind == "weights":
            left, right, right_sib = (refs[i] for i in task["ins"])
            for out, base, side in ((pack, offset, 1 - bit), (kept_ref, 0, bit)):
                lhs = left[pl.ds(pl.multiple_of(task["row"] + side * half, 64), half), :]
                for t in range(0, tiles, 2):
                    col = task["column"] + TOK * t
                    rhs = jnp.concatenate(
                        [right[:, col : col + 2 * TOK], right_sib[:, col : col + 2 * TOK]], axis=0
                    )
                    part = mm(lhs, rhs).astype(BF)
                    out[base + t * half : base + (t + 1) * half, :] = part[:, :TOK]
                    out[base + (t + 1) * half : base + (t + 2) * half, :] = part[:, TOK:]
        elif kind == "along":
            left, right = (refs[i] for i in task["ins"])
            for out, base, side in ((pack, offset, 1 - bit), (kept_ref, 0, bit)):
                part = mm(left[pl.ds(pl.multiple_of(side * half, 64), half), :], right[...]).astype(BF)
                for t in range(tiles):
                    out[base + t * half : base + (t + 1) * half, :] = part[:, TOK * t : TOK * t + TOK]
        elif kind == "first":
            value, base, in_slot = refs[task["ins"][0]], task["came"], slot(2 * half)
            for t in range(tiles):
                at = base + t * in_slot
                if half % 16 == 0:
                    pack[offset + t * out_slot : offset + t * out_slot + half, :] = value[
                        pl.ds(pl.multiple_of(at + (1 - bit) * half, 16), half), :
                    ]
                    kept_ref[t * out_slot : t * out_slot + half, :] = value[
                        pl.ds(pl.multiple_of(at + bit * half, 16), half), :
                    ]
                else:
                    both = value[at : at + 2 * half, :].astype(F32)
                    low, high = both[:half], both[half:]
                    pack[offset + t * out_slot : offset + t * out_slot + half, :] = jnp.where(bit == 0, high, low).astype(BF)
                    kept_ref[t * out_slot : t * out_slot + half, :] = jnp.where(bit == 0, low, high).astype(BF)
        else:
            value, got = (refs[i] for i in task["ins"])
            came, in_slot = task["came"], slot(2 * half)

            def one(t, half=half, out_slot=out_slot, in_slot=in_slot, came=came, offset=offset, bit=bit,
                    value=value, got=got, pack=pack, kept_ref=kept_ref):
                if half % 16 == 0:
                    for out, base, side in ((pack, offset, 1 - bit), (kept_ref, 0, bit)):
                        at = t * in_slot + side * half
                        total = (
                            value[pl.ds(pl.multiple_of(at, 16), half), :].astype(F32)
                            + got[pl.ds(pl.multiple_of(came + at, 16), half), :].astype(F32)
                        )
                        out[pl.ds(aligned(base + t * out_slot), half), :] = total.astype(BF)
                else:
                    total = (
                        value[pl.ds(aligned(t * in_slot), 2 * half), :].astype(F32)
                        + got[pl.ds(aligned(came + t * in_slot), 2 * half), :].astype(F32)
                    )
                    low, high = total[:half], total[half:]
                    pack[pl.ds(aligned(offset + t * out_slot), half), :] = jnp.where(bit == 0, high, low).astype(BF)
                    kept_ref[pl.ds(aligned(t * out_slot), half), :] = jnp.where(bit == 0, low, high).astype(BF)

            for_tiles(tiles, one)


def sums(jobs):
    arrays, tasks, pack_rows, rest = [], [], {}, []

    def at(array):
        for i, a in enumerate(arrays):
            if a is array:
                return i
        arrays.append(array)
        return len(arrays) - 1

    flops = 0
    for job in jobs:
        if job[0] == "weights":
            _, left, row, rows, right, right_sib, column, columns, bit, pack = job
            rest.append(left)
            task = dict(kind="weights", ins=[at(left), at(right), at(right_sib)], row=row, column=column,
                        half=rows // 2, tiles=columns // TOK, bit=bit)
            flops += 4 * rows * columns * TOK
        elif job[0] == "along":
            _, left, right, pack = job
            rest.append(left)
            task = dict(kind="along", ins=[at(left), at(right)], half=D // 2, tiles=right.shape[1] // TOK, bit="c")
            flops += 2 * D * right.shape[1] * 4 * TOK
        elif job[0] == "first":
            _, array, base, rows, tiles, bit, pack = job
            task = dict(kind="first", ins=[at(array)], came=base, half=rows // 2, tiles=tiles, bit=bit)
        else:
            _, member, bit, pack = job
            task = dict(kind="step", ins=[at(member.kept), at(member.got)], came=member.offset,
                        half=member.rows // 2, tiles=member.tiles, bit=bit)
        task["pack"], task["offset"] = pack, pack_rows.get(pack, 0)
        pack_rows[pack] = task["offset"] + task["tiles"] * slot(task["half"])
        tasks.append(task)
    names = sorted(pack_rows)
    shapes = [sds((pack_rows[n], TOK), BF) for n in names]
    for i, task in enumerate(tasks):
        task["kept"] = len(arrays) + len(names) + i
        task["pack"] = len(arrays) + names.index(task["pack"])
        shapes.append(sds((task["tiles"] * slot(task["half"]), TOK), BF))
    moved = sum(a.size for a in arrays) + sum(np.prod(s.shape) for s in shapes)
    outs = pl.pallas_call(
        lambda *refs: sums_kernel(tasks, *refs),
        out_shape=shapes,
        in_specs=[VMEM] * len(arrays),
        out_specs=[VMEM] * len(shapes),
        compiler_params=pltpu.CompilerParams(vmem_limit_bytes=10 * MIB),
        cost_estimate=pl.CostEstimate(flops=flops, bytes_accessed=int(moved) * 2, transcendentals=0),
        name="sums",
    )(*(at_rest(a) if any(a is r for r in rest) else a for a in arrays))
    packs = dict(zip(names, outs))
    members = [
        Member(kept, task["half"], task["tiles"], task["offset"]) for kept, task in zip(outs[len(names) :], tasks)
    ]
    return packs, members


def came(members, got):
    for member in members:
        member.got = got


def finish_kernel(plan, places, *refs):
    back, arrays = refs[6], refs[7:-19]
    acts, gtok, gq, gk, gv, go, ggate, gup, gdown, gattn, gffn, by_x = refs[-19:-7]
    wq, wk, wv, wg, wu, gains = refs[-7:-1]
    copies = [
        pltpu.make_async_copy(source, buf, refs[-1].at[i]) for i, (source, buf) in enumerate(zip(refs[:6], refs[-7:-1]))
    ]
    for copy in copies:
        copy.start()
    gtok[...] = back[:TOK, :].astype(F32)
    acts[...] = back[TOK:, :]
    spot = here()
    mine = spot["x"]
    across, beside = 3 - mine, mine + 1 - 2 * lax.rem(mine, 2)
    first = jnp.where(spot["c"] == 0, beside, across)
    second = jnp.where(spot["c"] == 0, across, beside)
    opposite = lax.rem(mine + 2, 4)
    for m in range(2):
        (kept, got, offset), (kept_b, got_b, offset_b) = places[m]
        for group, array, base in (
            (mine, kept, 0), (first, kept_b, 0), (second, got, offset), (opposite, got_b, offset_b)
        ):
            by_x[4 * m + group] = arrays[array][base : base + 80, :]

    def total(name):
        kept, got, offset, tiles, rows = plan[name]
        parts = []
        for t in range(tiles):
            parts.append(
                arrays[kept][16 * t : 16 * t + rows, :].astype(F32)
                + arrays[got][offset + 16 * t : offset + 16 * t + rows, :].astype(F32)
            )
        return jnp.concatenate(parts, axis=1)

    lane = lax.broadcasted_iota(jnp.int32, (8, TOK), 1)
    result = jnp.zeros((8, TOK), F32)
    filler = jnp.zeros((2, 1), F32)
    both = jnp.concatenate([total("gate0"), total("up0")], axis=1), total("gu1")
    gates = [b[:, :FF] for b in both]
    ups = [b[:, FF:] for b in both]
    for layer in range(2):
        ggate[:, layer, :] = gates[layer]
        gup[:, layer, :] = ups[layer]
        go[:, layer, :] = total(f"out{layer}")
        gdown[layer] = total(f"down{layer}")
    for copy in copies:
        copy.wait()
    for layer in range(2):
        m = 1 - layer
        rows = [
            jnp.concatenate([by_x[4 * m + x, 16 * t : 16 * t + 6, :] for t in range(5)], axis=1) for x in range(4)
        ]
        acc = jnp.zeros((6, 1), F32)
        for i, (out, w) in enumerate(((gk, wk), (gv, wv), (gq, wq))):
            value = jnp.concatenate([r[:, GROUP * i : GROUP * i + GROUP] for r in rows], axis=1).astype(F32)
            out[:, layer, :] = value
            acc = acc + jnp.sum(value * w[layer][:6], axis=1, keepdims=True)
        result = jnp.where(lane == layer, jnp.concatenate([acc / gains[:6, layer : layer + 1], filler], axis=0), result)
        gate, up = gates[layer], ups[layer]
        acc = jnp.sum(gate * wg[layer][:6], axis=1, keepdims=True) + jnp.sum(
            up * wu[layer][:6], axis=1, keepdims=True
        )
        result = jnp.where(lane == 2 + layer, jnp.concatenate([acc / gains[:6, 2 + layer : 3 + layer], filler], axis=0), result)
    turned = result.T
    gattn[...] = turned[0:2, :6]
    gffn[...] = turned[2:4, :6]


def finish(rows_of, back, members, projections):
    arrays, plan = [], {}

    def at(array):
        for i, a in enumerate(arrays):
            if a is array:
                return i
        arrays.append(array)
        return len(arrays) - 1

    for name, m in members.items():
        plan[name] = (at(m.kept), at(m.got), m.offset, m.tiles, m.rows)
    places = [[(at(m.kept), at(m.got), m.offset) for m in pair] for pair in projections]
    return pl.pallas_call(
        lambda *refs: finish_kernel(plan, places, *refs),
        out_shape=[sds((TOK, D), BF), sds((TOK, D), F32)]
        + [sds((6, 2, D), F32)] * 4
        + [sds((6, 2, FF), F32)] * 2
        + [sds((2, 16, D), F32), sds((2, 6), F32), sds((2, 6), F32)],
        in_specs=[HBM] * 6 + [VMEM] * (1 + len(arrays)),
        out_specs=[VMEM] * 11,
        scratch_shapes=[pltpu.VMEM((8, 80, TOK), BF)]
        + [pltpu.VMEM((2, 8, D), F32)] * 3
        + [pltpu.VMEM((2, 8, FF), F32)] * 2
        + [pltpu.VMEM((8, TOK), F32), pltpu.SemaphoreType.DMA((6,))],
        compiler_params=pltpu.CompilerParams(vmem_limit_bytes=8 * MIB),
        cost_estimate=pl.CostEstimate(flops=1 << 18, bytes_accessed=2 << 20, transcendentals=0),
        name="finish",
    )(*map(at_rest, rows_of), back, *arrays)


def tie(value, *others):
    return lax.optimization_barrier((value,) + others)[0]


def per_device(
    tokens, seg_lengths, cotangent, norm_attn, w_query, w_key, w_value, w_out, norm_ffn, w_gate, w_up, w_down
):
    with jax.named_scope("S_setup"):
        _, early = first_norm(tokens[0], norm_attn, True)
        first_blocks = [send(early, GATHER[d]) for d in (1, 2, 3)]
        moved = send(tokens[0], RELOCATE)
        lengths = send(seg_lengths[0], RELOCATE)
        cot = send(cotangent[0], RELOCATE)
        x, normed = first_norm(moved, norm_attn)
        heads = own_heads(w_query, w_key, w_value)
        cos, sin, starts = tables(lengths)

    kept, carried, alongs = [], [], []
    for depth in range(2):
        with jax.named_scope(f"S_ahead{depth}"):
            blocks = exchange_x([normed] * 4) if depth else (normed, *first_blocks)
            if depth == 1:
                alongs.append(left_along(rows))
                cot = tie(cot, alongs[0])
                blocks = (tie(blocks[0], cot),) + tuple(blocks[1:])
            q, own, rows = project(depth, blocks, heads, cos, sin)
            sib = send(own, CORE)
            *blocks, q, kv, lse = attend(q, own, sib, starts)
            blocks = exchange_x(blocks)
            if depth == 0:
                rows_of = own_rows(w_query, w_key, w_value, w_gate, w_up, norm_attn, norm_ffn)
                blocks = (tie(blocks[0], *rows_of),) + tuple(blocks[1:])
            else:
                alongs.append(left_along(rows))
                blocks = (tie(blocks[0], alongs[1]),) + tuple(blocks[1:])
            result, normed, acts, middle, slopes = feed(
                depth, x, norm_ffn, norm_attn, blocks, w_out, w_gate, w_up, w_down
            )
            kept.append((x, q, kv, lse, middle, slopes))
            carried.append(acts)
            x = result
    activations = x

    def step(members, bit, pack):
        return [("step", m, bit, pack) for m in members]

    half = D // 2
    x, q, kv, lse, middle, slopes = kept[1]
    with jax.named_scope("S_back1"):
        right, dmid, *blocks = feed_back(
            1, cot, middle, slopes, norm_ffn, w_down, w_gate, w_up, w_out, [carried[1], carried[0]]
        )
        blocks = exchange_x(blocks)
        right_sib = send(right, CORE)
    with jax.named_scope("S_sum1"):
        width = 2 * FF + 2 * D
        left = left_sides(width, right, right_sib, [(0, "yzx", "yz"), (D, "zyx", "yz"), (2 * D, "zyx", "yz")])
        packs, (gu1, out1, down1) = sums(
            [
                ("weights", left, 0, D // 2, tie(right, *blocks), right_sib, 0, 2 * FF, ("y", 0, "swapped"), "y"),
                ("weights", left, half, D // 2, right, right_sib, 2 * FF + D, D, ("z", 0, "swapped"), "z"),
                ("weights", left, 2 * half, FF // 2, right, right_sib, 2 * FF, D, ("z", 0, "swapped"), "z"),
            ],
        )
        came([gu1], send(packs["y"], PAIR["y", 1]))
        came([out1, down1], send(packs["z"], PAIR["z", 1]))
    with jax.named_scope("S_back1"):
        blocks = (tie(blocks[0], packs["y"], packs["z"]),) + tuple(blocks[1:])
        dq, own, sib = attend_back(q, kv, starts, lse, blocks)
        right1, blocks = spread(1, dq, own, send(sib, CORE), cos, sin, heads)
        blocks = exchange_x(blocks)
    with jax.named_scope("S_sum1"):
        left = left_sides(
            width + 2 * D + FF, tie(right, right1), right_sib, [(0, "xyz", ""), (0, "yzx", ""), (D, "xyz", ""), (2 * D, "zyx", "")]
        )
    with jax.named_scope("S_back1"):
        blocks = (tie(blocks[0], left, gu1.got, out1.got),) + tuple(blocks[1:])
        grad = project_back(dmid, x, norm_attn, blocks)

    x, q, kv, lse, middle, slopes = kept[0]
    with jax.named_scope("S_back0"):
        right, dmid, *blocks = feed_back(0, grad, middle, slopes, norm_ffn, w_down, w_gate, w_up, w_out, [])
        blocks = exchange_x(blocks)
        right_sib = send(right, CORE)
    with jax.named_scope("S_sum0"):
        packs, (gate0, up0, out0, down0, gu1, out1, down1) = sums(
            [
                ("weights", left, 0, D // 2, tie(right, *blocks), right_sib, 0, ALONG_X, ("x", 0), "x"),
                ("weights", left, half, D // 2, right, right_sib, ALONG_X, 2 * FF - ALONG_X, ("y", 0), "y"),
                ("weights", left, 2 * half, D // 2, right, right_sib, 2 * FF + D, D, ("x", 0), "x"),
                ("weights", left, 3 * half, FF // 2, right, right_sib, 2 * FF, D, ("z", 0), "z"),
            ]
            + step([gu1], ("y", 1, "swapped"), "y")
            + step([out1, down1], ("z", 1, "swapped"), "z"),
        )
        came([gate0, out0], send(packs["x"], PAIR["x", 0]))
        came([up0, gu1], send(packs["y"], PAIR["y", 0]))
        came([down0, out1, down1], send(packs["z"], PAIR["z", 0]))
    with jax.named_scope("S_back0"):
        blocks = (tie(blocks[0], packs["x"], packs["y"], packs["z"]),) + tuple(blocks[1:])
        dq, own, sib = attend_back(q, kv, starts, lse, blocks)
        right0, (partial,) = spread(0, dq, own, send(sib, CORE), cos, sin, heads)

    with jax.named_scope("S_sum0"):
        packs, (qkv1, qkv0) = sums([("along", alongs[1], right1, "c"), ("along", alongs[0], right0, "c")])
        came([qkv1, qkv0], send(tie(packs["c"], gate0.got, up0.got, down0.got), CORE))
        packs, (gate0, out0, up0, down0, gu1, out1, down1, qkv1, qkv0, da) = sums(
            step([gate0, out0], ("x", 1), "x")
            + step([up0], ("y", 1), "y")
            + step([down0], ("z", 1), "z")
            + step([gu1], ("z", 0, "swapped"), "z")
            + step([out1, down1, qkv1, qkv0], ("y", 0, "swapped"), "y")
            + [("first", partial, 0, 4 * TOK, 6, ("x", 0, "swapped"), "x")],
        )
        came([gate0, out0, da], send(packs["x"], PAIR["x", 1]))
        came([up0, out1, down1, qkv1, qkv0], send(packs["y"], PAIR["y", 1]))
        came([down0, gu1], send(packs["z"], PAIR["z", 1]))
        packs, (gate0, out0, down0, up0, gu1, out1, down1, qkv1, qkv0, da) = sums(
            step([gate0, out0, down0], ("y", 0), "y")
            + step([up0], ("z", 0), "z")
            + step([gu1], ("z", 1, "swapped"), "z")
            + step([out1, down1, qkv1, qkv0], ("y", 1, "swapped"), "y")
            + step([da], ("x", 1, "swapped"), "x"),
        )
        came([gate0, out0, down0, out1, down1, qkv1, qkv0], send(packs["y"], PAIR["y", 0]))
        came([up0, gu1], send(packs["z"], PAIR["z", 0]))
        came([da], send(packs["x"], PAIR["x", 0]))
        back = send(last_grad(da, dmid, x, norm_attn, activations), RESTORE)
        packs, (gate0, out0, down0, up0, qkv1, qkv0) = sums(
            step([gate0, out0, down0], ("y", 1), "y")
            + step([up0], ("z", 1), "z")
            + step([qkv1, qkv0], ("z", 0, "swapped"), "z"),
        )
        came([gate0, out0, down0], send(packs["y"], PAIR["y", 1]))
        came([up0, qkv1, qkv0], tie(send(packs["z"], PAIR["z", 1]), back))
        packs, (gate0, out0, qkv1, qkv0) = sums(
            step([gate0, out0], ("z", 0), "z") + step([qkv1, qkv0], ("z", 1, "swapped"), "z")
        )
        came([gate0, out0, qkv1, qkv0], send(packs["z"], PAIR["z", 0]))
        packs, (gate0, out0, up0, down0, gu1, out1, down1, qkv1, qkv0) = sums(
            step([gate0, out0], ("z", 1), "z")
            + step([up0, down0, gu1, out1, down1, qkv1, qkv0], ("x", 0), "x"),
        )
        came([gate0, out0], send(packs["z"], PAIR["z", 1]))
        came([up0, down0, gu1, out1, down1, qkv1, qkv0], send(packs["x"], PAIR["x", 0]))
        packs, (up0, down0, gu1, out1, down1, mine1, first1, mine0, first0) = sums(
            step([up0, down0, gu1, out1, down1], ("x", 1), "x")
            + [
                ("first", array, offset, 12, 5, ("x", 1), "x")
                for m in (qkv1, qkv0)
                for array, offset in ((m.kept, 0), (m.got, m.offset))
            ],
        )
        came([up0, down0, gu1, out1, down1, mine1, first1, mine0, first0], send(packs["x"], PAIR["x", 1]))
        activations, grad_tokens, grad_q, grad_k, grad_v, grad_o, grad_gate, grad_up, grad_down, grad_attn, grad_ffn = finish(
            rows_of, back,
            dict(gate0=gate0, up0=up0, gu1=gu1, out0=out0, out1=out1, down0=down0, down1=down1),
            [(mine1, first1), (mine0, first0)],
        )
    return (
        activations[None],
        grad_tokens[None],
        grad_attn,
        jnp.swapaxes(grad_q, 0, 1),
        jnp.swapaxes(grad_k, 0, 1),
        jnp.swapaxes(grad_v, 0, 1),
        jnp.swapaxes(grad_o, 0, 1),
        grad_ffn,
        jnp.swapaxes(grad_gate, 0, 1),
        jnp.swapaxes(grad_up, 0, 1),
        grad_down,
    )


def solution(mesh):
    rows = P("batch", "seq", None)
    split = P(None, AXES)
    split3 = P(None, AXES, None)
    return jax.shard_map(
        per_device,
        mesh=mesh,
        in_specs=(rows, P("batch", None), rows) + (P(),) * 9,
        out_specs=(rows, rows, split, split3, split3, split3, split3, split, split3, split3, split3),
        check_vma=False,
    )
```

```python
import jax
import jax.numpy as jnp
import numpy as np
from jax import lax
from jax.experimental import pallas as pl
from jax.experimental.pallas import tpu as pltpu
from jax.sharding import PartitionSpec as P

D = 768
HEADS = 12
HEAD_DIM = 64
FF = 2048
ALONG_X = FF + 256
TOK = 128
ROW = 1024
GRID = 16
GROUP = 3 * HEAD_DIM
OFF = {"k": 0, "v": GROUP, "q": 2 * GROUP}
EPS = 1e-05
AXES = ("seq", "batch")
BF = jnp.bfloat16
F32 = jnp.float32
MIB = 1 << 20


def place(flat):
    seq, batch = divmod(flat, 16)
    z_lo, x = divmod(seq, 4)
    y, rest = divmod(batch, 4)
    z_hi, core = divmod(rest, 2)
    return dict(x=x, y=y, z=z_hi * 2 + z_lo, c=core)


def flat_of(p):
    z_hi, z_lo = divmod(p["z"], 2)
    return (z_lo * 4 + p["x"]) * 16 + p["y"] * 4 + z_hi * 2 + p["c"]


def permutation(move):
    pairs = []
    for flat in range(128):
        p = place(flat)
        move(p)
        pairs.append((flat, flat_of(p)))
    return pairs


def move_relocate(p):
    z_hi, z_lo = divmod(p["z"], 2)
    core = p["c"]
    p["z"] = z_hi * 2 + core
    p["c"] = z_lo ^ (1 if p["x"] >= 2 else 0)


RELOCATE = permutation(move_relocate)
RESTORE = sorted((dst, src) for src, dst in RELOCATE)


def move_core(p):
    p["c"] ^= 1


CORE = permutation(move_core)


def shift_x(by):
    def move(p):
        p["x"] = (p["x"] + by) % 4

    return permutation(move)


SHIFT_X = {d: shift_x(d) for d in (1, 2, 3)}


def pair_step(axis, step):
    def move(p):
        at = p[axis]
        p[axis] = at ^ 1 if (p["c"] == 0) == (step == 0) else 3 - at

    return permutation(move)


PAIR = {(axis, step): pair_step(axis, step) for axis in "xyz" for step in (0, 1)}


def relocate_and_shift(by):
    def move(p):
        move_relocate(p)
        p["x"] = (p["x"] + by) % 4

    return permutation(move)


GATHER = {d: relocate_and_shift(d) for d in (1, 2, 3)}


def send(value, pairs):
    return lax.ppermute(value, AXES, pairs)


RING_ORDER = {0: (0, 3, 1, 2), 1: (0, 1, 2, 3)}


def block_order(axes, swapped=""):
    order = []
    for core in (0, 1):
        first, second, third = (RING_ORDER[1 - core if axis in swapped else core] for axis in axes)
        for a in first:
            for b in second:
                for c in third:
                    order.append(flat_of({axes[0]: a, axes[1]: b, axes[2]: c, "c": core}))
    return np.array(order)


def one_hot(axes, core, swapped=""):
    row = lax.broadcasted_iota(jnp.int32, (D // 2, 1), 0)
    block = (row * 10923) >> 16
    within = row - 6 * block
    places = {}
    for i, axis in enumerate(axes):
        at = (block >> (4 - 2 * i)) & 3
        ring = jnp.where(at == 0, 0, jnp.where(at == 1, 3, at - 1))
        places[axis] = jnp.where(core == (1 if axis in swapped else 0), ring, at)
    z = places["z"]
    flat = ((z & 1) * 4 + places["x"]) * 16 + places["y"] * 4 + (z >> 1) * 2 + core
    lane = lax.broadcasted_iota(jnp.int32, (D // 2, D), 1)
    return jnp.where(lane == flat * 6 + within, 1.0, 0.0).astype(BF)


def mm(left, right):
    return jnp.dot(left, right, preferred_element_type=F32)


def mm_rt(left, right):
    return lax.dot_general(left, right, (((1,), (1,)), ((), ())), preferred_element_type=F32)


def mm_lt(left, right):
    return lax.dot_general(left, right, (((0,), (0,)), ((), ())), preferred_element_type=F32)


VMEM = pl.BlockSpec(memory_space=pltpu.VMEM)
SMEM = pl.BlockSpec(memory_space=pltpu.SMEM)
HBM = pl.BlockSpec(memory_space=pltpu.HBM)


def pinned(*weights):
    return tuple(pltpu.with_memory_space_constraint(w, pltpu.VMEM) for w in weights)


def at_rest(value):
    return pltpu.with_memory_space_constraint(value, pltpu.HBM)


def stored(shape, kind):
    return pltpu.HBM(shape, kind)


def sds(shape, kind):
    return jax.ShapeDtypeStruct(shape, kind)


def here():
    seq, batch = lax.axis_index("seq"), lax.axis_index("batch")
    return dict(
        x=lax.rem(seq, 4), y=batch // 4, z=lax.rem(batch // 2, 2) * 2 + seq // 4, c=lax.rem(batch, 2), flat=seq * 16 + batch
    )


def rank_of(core, at):
    return jnp.where(core == 0, jnp.where(at == 0, 0, jnp.where(at == 3, 1, at + 1)), at)


def ordered_by_x(mine, blocks, out):
    for d, b in enumerate(blocks):
        out[lax.rem(mine - d + 4, 4)] = b[...]


def norm_factor(values):
    return lax.rsqrt(jnp.mean(values * values, axis=-1, keepdims=True) + EPS)


def first_norm_kernel(tokens, gain, x, normed):
    values = tokens[...].astype(F32)
    x[...] = values
    normed[...] = (values * norm_factor(values) * gain[0:1, :]).astype(BF)


def first_norm(tokens, gain, first=False):
    return pl.pallas_call(
        first_norm_kernel,
        out_shape=[sds((TOK, D), F32), sds((TOK, D), BF)],
        in_specs=[VMEM] * 2,
        out_specs=[VMEM] * 2,
        compiler_params=pltpu.CompilerParams(vmem_limit_bytes=4 * MIB),
        cost_estimate=pl.CostEstimate(flops=0, bytes_accessed=0, transcendentals=0),
        name="first_norm",
    )(*map(at_rest, (tokens, gain)) if first else (tokens, gain))


def tables_kernel(lengths, freqs, cos, sin, starts):
    core = here()["c"]

    def places(shape, dim, base):
        r = lax.broadcasted_iota(jnp.int32, shape, dim) + base
        block = r >> 7
        block = jnp.where(core == 0, jnp.where(block < 2, block, block + 4), jnp.where(block < 2, block + 4, block))
        return (block << 7) + (r & 127)

    def begin(place):
        start = lengths[0] * 0
        result = jnp.zeros_like(place)
        for i in range(5):
            end = start + lengths[i]
            result = jnp.where((place >= start) & (place < end), start, result)
            start = end
        return result

    for half in range(2):
        starts[half : half + 1, :] = begin(places((1, 256), 1, 256 * half))
    place = places((4 * TOK, 1), 0, 0)
    inside = place - begin(place)
    offset = jnp.maximum(inside - 1, 0)
    lane = lax.broadcasted_iota(jnp.int32, (4 * TOK, TOK), 1)
    rows = (offset >> 4).astype(F32)
    columns = (offset & (GRID - 1)).astype(F32)
    angles = jnp.where((lane & 63) < 32, rows, columns) * freqs[...]
    angles = jnp.where(inside > 0, angles, 0.0)
    cos[...] = jnp.cos(angles)
    sin[...] = jnp.where((lane & 1) == 0, -1.0, 1.0) * jnp.sin(angles)


def tables(lengths):
    freqs = 10000.0 ** (-4.0 * np.arange(HEAD_DIM // 4, dtype=np.float32) / HEAD_DIM)
    freqs = np.tile(np.repeat(freqs.astype(np.float32), 2), 4)[None, :]
    return pl.pallas_call(
        tables_kernel,
        out_shape=[sds((4 * TOK, TOK), F32), sds((4 * TOK, TOK), F32), sds((2, 256), jnp.int32)],
        in_specs=[SMEM, VMEM],
        out_specs=[VMEM] * 3,
        compiler_params=pltpu.CompilerParams(vmem_limit_bytes=4 * MIB),
        cost_estimate=pl.CostEstimate(flops=0, bytes_accessed=0, transcendentals=0),
        name="tables",
    )(lengths, jnp.asarray(freqs))


def own_heads_kernel(wq, wk, wv, out, bq, bk, bv, sems):
    x = here()["x"]
    start = pl.multiple_of((x * GROUP // TOK) * TOK, TOK)
    copies = [
        pltpu.make_async_copy(w.at[:, :, pl.ds(start, 2 * TOK)], buf, sems.at[i])
        for i, (w, buf) in enumerate(((wk, bk), (wv, bv), (wq, bq)))
    ]
    for copy in copies:
        copy.start()
    for i, (copy, buf) in enumerate(zip(copies, (bk, bv, bq))):
        copy.wait()
        for layer in range(2):
            w = buf[layer]
            out[layer, :, GROUP * i : GROUP * i + GROUP] = jnp.where(lax.rem(x, 2) == 0, w[:, :GROUP], w[:, 64:])


def own_heads(wq, wk, wv):
    return pl.pallas_call(
        own_heads_kernel,
        out_shape=sds((2, D, 3 * GROUP), BF),
        in_specs=[HBM] * 3,
        out_specs=VMEM,
        scratch_shapes=[pltpu.VMEM((2, D, 2 * TOK), BF)] * 3 + [pltpu.SemaphoreType.DMA((3,))],
        compiler_params=pltpu.CompilerParams(vmem_limit_bytes=8 * MIB),
        cost_estimate=pl.CostEstimate(flops=0, bytes_accessed=0, transcendentals=0),
        name="own_heads",
    )(*map(at_rest, (wq, wk, wv)))


def turn_group(values, cos, sin):
    lane = lax.broadcasted_iota(jnp.int32, (values.shape[0], 128), 1)
    even = lane % 2 == 0
    tail = jnp.concatenate([values[:, 128:], jnp.zeros((values.shape[0], 64), F32)], axis=1)
    parts = []
    for v in (values[:, :128], tail):
        swapped = jnp.where(even, pltpu.roll(v, 127, 1), pltpu.roll(v, 1, 1))
        parts.append(v * cos + swapped * sin)
    return jnp.concatenate([parts[0], parts[1][:, :64]], axis=1)


def project_kernel(depth, n0, n1, n2, n3, w, cos, sin, q, own, rows_out, rows, sem):
    ordered_by_x(here()["x"], (n0, n1, n2, n3), rows)
    store = pltpu.make_async_copy(rows, rows_out, sem)
    store.start()
    normed = rows[...].reshape(4 * TOK, D)
    y = mm(normed, w[depth])
    own[:, :GROUP] = turn_group(y[:, :GROUP], cos[...], sin[...]).astype(BF)
    own[:, GROUP:] = y[:, GROUP : 2 * GROUP].astype(BF)
    q[...] = turn_group(y[:, 2 * GROUP :], cos[...], sin[...]).astype(BF)
    store.wait()


def project(depth, normed, w, cos, sin):
    return pl.pallas_call(
        lambda *refs: project_kernel(depth, *refs),
        out_shape=[sds((4 * TOK, GROUP), BF), sds((4 * TOK, 2 * GROUP), BF), stored((4, TOK, D), BF)],
        in_specs=[VMEM] * 7,
        out_specs=[VMEM] * 2 + [HBM],
        scratch_shapes=[pltpu.VMEM((4, TOK, D), BF), pltpu.SemaphoreType.DMA(())],
        compiler_params=pltpu.CompilerParams(vmem_limit_bytes=8 * MIB),
        cost_estimate=pl.CostEstimate(flops=0, bytes_accessed=0, transcendentals=0),
        name="project",
    )(*normed, w, cos, sin)


def tile_scores(q, k, start, place0, n):
    raw = mm_rt(k, q)
    keys = lax.broadcasted_iota(jnp.int32, (256, 256), 0)
    asks = lax.broadcasted_iota(jnp.int32, (256, 256), 1)
    parts = []
    for at in range(0, n, 256):
        allowed = keys >= start - at
        if at == place0:
            allowed = allowed & (keys <= asks)
        parts.append(jnp.where(allowed, raw[at : at + 256], -1e30))
    return parts[0] if len(parts) == 1 else jnp.concatenate(parts, axis=0)


def attend_kernel(q, own, sib, starts, m0, m1, m2, m3, q_out, kv_out, lse_out, kv, lse, mixed, sems):
    spot = here()
    core, mine = spot["c"], spot["x"]
    stores = [
        pltpu.make_async_copy(source, out, sems.at[i])
        for i, (source, out) in enumerate(((q, q_out), (kv, kv_out), (lse, lse_out)))
    ]
    stores[0].start()

    @pl.when(core == 0)
    def _():
        kv[0:256, :] = own[0:256, :]
        kv[256:512, :] = sib[256:512, :]
        kv[512:768, :] = sib[0:256, :]
        kv[768:1024, :] = own[256:512, :]

    @pl.when(core == 1)
    def _():
        kv[0:256, :] = sib[0:256, :]
        kv[256:512, :] = own[256:512, :]
        kv[512:768, :] = own[0:256, :]
        kv[768:1024, :] = sib[256:512, :]

    stores[1].start()

    def tile(which, pos):
        n = 256 * (pos + 1)
        outs = []
        start = starts[which : which + 1, :]
        for h in range(3):
            qs = q[256 * which : 256 * which + 256, 64 * h : 64 * h + 64] * jnp.asarray(0.125, BF)
            s = tile_scores(qs, kv[0:n, 64 * h : 64 * h + 64], start, 256 * pos, n)
            top = jnp.max(s, axis=0, keepdims=True)
            e = jnp.exp(s - top)
            total = jnp.sum(e, axis=0, keepdims=True)
            probs = (e * (1.0 / total)).astype(BF)
            lse[3 * which + h : 3 * which + h + 1, :] = top + jnp.log(total)
            outs.append(mm_lt(kv[0:n, GROUP + 64 * h : GROUP + 64 * h + 64], probs))
        out = jnp.concatenate(outs, axis=0).T.astype(BF)
        mixed[2 * which] = out[:TOK]
        mixed[2 * which + 1] = out[TOK:]

    @pl.when(core == 0)
    def _():
        tile(0, 0)
        tile(1, 3)

    @pl.when(core == 1)
    def _():
        tile(0, 2)
        tile(1, 1)

    stores[2].start()
    for d, m in enumerate((m0, m1, m2, m3)):
        m[...] = mixed[lax.rem(mine + d, 4)]
    for store in stores:
        store.wait()


def attend(q, own, sib, starts):
    return pl.pallas_call(
        attend_kernel,
        out_shape=[sds((TOK, GROUP), BF)] * 4
        + [stored((4 * TOK, GROUP), BF), stored((ROW, 2 * GROUP), BF), stored((8, 256), F32)],
        in_specs=[VMEM] * 4,
        out_specs=[VMEM] * 4 + [HBM] * 3,
        scratch_shapes=[
            pltpu.VMEM((ROW, 2 * GROUP), BF),
            pltpu.VMEM((8, 256), F32),
            pltpu.VMEM((4, TOK, GROUP), BF),
            pltpu.SemaphoreType.DMA((3,)),
        ],
        compiler_params=pltpu.CompilerParams(vmem_limit_bytes=8 * MIB),
        cost_estimate=pl.CostEstimate(flops=0, bytes_accessed=0, transcendentals=0),
        name="attend",
    )(q, own, sib, starts)


def feed_kernel(
    depth, x, gain, next_gain, b0, b1, b2, b3, wo, wg, wu, wd,
    result, normed_next, acts_out, middle_out, slopes_out,
    groups, acts, middle_b, slopes, sems, *own,
):
    if own:
        copies = [
            pltpu.make_async_copy(w.at[depth], buf, sems.at[3 + i]) for i, (w, buf) in enumerate(zip((wo, wd), own))
        ]
        for copy in copies:
            copy.start()
    stores = [
        pltpu.make_async_copy(source, out, sems.at[i])
        for i, (source, out) in enumerate(((acts, acts_out), (middle_b, middle_out), (slopes, slopes_out)))
    ]
    ordered_by_x(here()["x"], (b0, b1, b2, b3), groups)
    mixed = jnp.concatenate([groups[g] for g in range(4)], axis=1)
    acts[:, D : 2 * D] = mixed
    if own:
        copies[0].wait()
    middle = x[...] + mm(mixed, own[0][...] if own else wo[depth])
    middle_b[...] = middle
    stores[1].start()
    normed2 = (middle * norm_factor(middle) * gain[depth : depth + 1, :]).astype(BF)
    acts[:, :D] = normed2
    gate = mm(normed2, wg[depth])
    sigma = 1.0 / (1.0 + jnp.exp(-gate))
    swish = gate * sigma
    up = mm(normed2, wu[depth])
    hidden = (swish * up).astype(BF)
    acts[:, 2 * D :] = hidden
    stores[0].start()
    slopes[:, :FF] = (up * sigma * (1.0 + gate * (1.0 - sigma))).astype(BF)
    slopes[:, FF:] = swish.astype(BF)
    stores[2].start()
    if own:
        copies[1].wait()
    values = middle + mm(hidden, own[1][...] if own else wd[depth])
    if depth == 0:
        result[...] = values
        normed_next[...] = (values * norm_factor(values) * next_gain[1:2, :]).astype(BF)
    else:
        result[...] = values.astype(BF)
        normed_next[...] = jnp.zeros((TOK, D), BF)
    for store in stores:
        store.wait()


def feed(depth, x, gain, next_gain, blocks, wo, wg, wu, wd):
    return pl.pallas_call(
        lambda *refs: feed_kernel(depth, *refs),
        out_shape=[
            sds((TOK, D), BF if depth else F32), sds((TOK, D), BF),
            stored((TOK, 2 * D + FF), BF), stored((TOK, D), F32), stored((TOK, 2 * FF), BF),
        ],
        in_specs=[VMEM] * 7 + [VMEM if depth else HBM, VMEM, VMEM, VMEM if depth else HBM],
        out_specs=[VMEM] * 2 + [HBM] * 3,
        scratch_shapes=[
            pltpu.VMEM((4, TOK, GROUP), BF),
            pltpu.VMEM((TOK, 2 * D + FF), BF),
            pltpu.VMEM((TOK, D), F32),
            pltpu.VMEM((TOK, 2 * FF), BF),
            pltpu.SemaphoreType.DMA((5,)),
        ]
        + ([] if depth else [pltpu.VMEM((D, D), BF), pltpu.VMEM((FF, D), BF)]),
        compiler_params=pltpu.CompilerParams(vmem_limit_bytes=(12 if depth else 16) * MIB),
        cost_estimate=pl.CostEstimate(flops=0, bytes_accessed=0, transcendentals=0),
        name="feed",
    )(x, gain, next_gain, *blocks, *(pinned(wo, wg, wu, wd) if depth else (at_rest(wo), *pinned(wg, wu), at_rest(wd))))


def feed_back_kernel(
    depth, carried, grad, middle, slopes, gain, wd, wg, wu, wo, *refs,
):
    acts = refs[:carried]
    right_ref, dmid_ref, o0, o1, o2, o3, groups, slopes_b, middle_b, sems = refs[carried:]
    width = 2 * FF + 2 * D
    carries = [
        pltpu.make_async_copy(source, right_ref.at[:, pl.ds(width + i * (2 * D + FF), 2 * D + FF)], sems.at[2 + i])
        for i, source in enumerate(acts)
    ]
    stores = [
        pltpu.make_async_copy(source, buf, sems.at[i])
        for i, (source, buf) in enumerate(((slopes, slopes_b), (middle, middle_b)))
    ]
    for store in stores + carries:
        store.start()
    g = grad[...].astype(F32)
    gb = g.astype(BF)
    right_ref[:, 2 * FF : 2 * FF + D] = gb
    dhidden = mm_rt(gb, wd[depth])
    stores[0].wait()
    dgate = (dhidden * slopes_b[:, :FF]).astype(BF)
    dup = (dhidden * slopes_b[:, FF:]).astype(BF)
    right_ref[:, :FF] = dgate
    right_ref[:, FF : 2 * FF] = dup
    dn = mm_rt(dgate, wg[depth]) + mm_rt(dup, wu[depth])
    stores[1].wait()
    mid = middle_b[...]
    factor = norm_factor(mid)
    s = mid * factor
    inner = dn * gain[depth : depth + 1, :]
    dmid = g + factor * (inner - s * jnp.mean(inner * s, axis=-1, keepdims=True))
    dmid_ref[...] = dmid
    dmb = dmid.astype(BF)
    right_ref[:, 2 * FF + D : width] = dmb
    dmixed = mm_rt(dmb, wo[depth]).astype(BF)
    for j in range(4):
        groups[j] = dmixed[:, GROUP * j : GROUP * j + GROUP]
    mine = here()["x"]
    for d, o in enumerate((o0, o1, o2, o3)):
        o[...] = groups[lax.rem(mine + d, 4)]
    for carry in carries:
        carry.wait()


def feed_back(depth, grad, middle, slopes, gain, wd, wg, wu, wo, acts):
    width = 2 * FF + 2 * D + len(acts) * (2 * D + FF)
    return pl.pallas_call(
        lambda *refs: feed_back_kernel(depth, len(acts), *refs),
        out_shape=[sds((TOK, width), BF), sds((TOK, D), F32)] + [sds((TOK, GROUP), BF)] * 4,
        in_specs=[VMEM] + [HBM] * 2 + [VMEM] * 5 + [HBM] * len(acts),
        out_specs=[VMEM] * 6,
        scratch_shapes=[
            pltpu.VMEM((4, TOK, GROUP), BF),
            pltpu.VMEM((TOK, 2 * FF), BF),
            pltpu.VMEM((TOK, D), F32),
            pltpu.SemaphoreType.DMA((4,)),
        ],
        compiler_params=pltpu.CompilerParams(vmem_limit_bytes=12 * MIB),
        cost_estimate=pl.CostEstimate(flops=0, bytes_accessed=0, transcendentals=0),
        name="feed_back",
    )(grad, *map(at_rest, (middle, slopes)), gain, *pinned(wd, wg, wu, wo), *map(at_rest, acts))


def attend_back_kernel(q, kv, starts, lse, b0, b1, b2, b3, dq, own, sib, dout, dk, dv):
    spot = here()
    core, mine = spot["c"], spot["x"]
    for d, b in enumerate((b0, b1, b2, b3)):
        rows = pl.ds(pl.multiple_of(lax.rem(mine - d + 4, 4) * TOK, TOK), TOK)
        dout[rows, :] = b[...]

    def tile(which, pos, first):
        n = 256 * (pos + 1)
        start = starts[which : which + 1, :]
        dqs = []
        for h in range(3):
            lanes = slice(64 * h, 64 * h + 64)
            qs = q[256 * which : 256 * which + 256, lanes] * jnp.asarray(0.125, BF)
            do = dout[256 * which : 256 * which + 256, lanes]
            k = kv[0:n, lanes]
            v = kv[0:n, GROUP + 64 * h : GROUP + 64 * h + 64]
            s = tile_scores(qs, k, start, 256 * pos, n)
            p = jnp.exp(s - lse[3 * which + h : 3 * which + h + 1, :])
            dp = mm_rt(v, do)
            delta = jnp.sum(p * dp, axis=0, keepdims=True)
            ds = (p * (dp - delta)).astype(BF)
            dk_h = mm(ds, qs)
            dv_h = mm(p.astype(BF), do)
            if first:
                dk[0:n, lanes] = dk_h
                dv[0:n, lanes] = dv_h
            else:
                dk[0:n, lanes] += dk_h
                dv[0:n, lanes] += dv_h
            dqs.append(mm_lt(k, ds))
        out = jnp.concatenate(dqs, axis=0).T * 0.125
        dq[256 * which : 256 * which + 256, :] = out

    def put(target, rows, tile_no):
        target[rows : rows + 256, :GROUP] = dk[256 * tile_no : 256 * tile_no + 256, :].astype(target.dtype)
        target[rows : rows + 256, GROUP:] = dv[256 * tile_no : 256 * tile_no + 256, :].astype(target.dtype)

    @pl.when(core == 0)
    def _():
        tile(1, 3, True)
        tile(0, 0, False)
        put(own, 0, 0)
        put(sib, 256, 1)
        put(sib, 0, 2)
        put(own, 256, 3)

    @pl.when(core == 1)
    def _():
        tile(0, 2, True)
        tile(1, 1, False)
        dk[768:1024, :] = jnp.zeros((256, GROUP), F32)
        dv[768:1024, :] = jnp.zeros((256, GROUP), F32)
        put(sib, 0, 0)
        put(own, 256, 1)
        put(own, 0, 2)
        put(sib, 256, 3)


def attend_back(q, kv, starts, lse, blocks):
    return pl.pallas_call(
        attend_back_kernel,
        out_shape=[sds((4 * TOK, GROUP), F32), sds((4 * TOK, 2 * GROUP), F32), sds((4 * TOK, 2 * GROUP), BF)],
        in_specs=[VMEM] * 8,
        out_specs=[VMEM] * 3,
        scratch_shapes=[
            pltpu.VMEM((4 * TOK, GROUP), BF),
            pltpu.VMEM((ROW, GROUP), F32),
            pltpu.VMEM((ROW, GROUP), F32),
        ],
        compiler_params=pltpu.CompilerParams(vmem_limit_bytes=10 * MIB),
        cost_estimate=pl.CostEstimate(flops=0, bytes_accessed=0, transcendentals=0),
        name="attend_back",
    )(at_rest(q), at_rest(kv), starts, at_rest(lse), *blocks)


def spread_kernel(depth, dq, own, got, cos, sin, w, right, *refs):
    right[:, : GROUP] = turn_group(own[:, :GROUP] + got[:, :GROUP].astype(F32), cos[...], -sin[...]).astype(BF)
    right[:, GROUP : 2 * GROUP] = (own[:, GROUP:] + got[:, GROUP:].astype(F32)).astype(BF)
    right[:, 2 * GROUP : 3 * GROUP] = turn_group(dq[...], cos[...], -sin[...]).astype(BF)
    right[:, 3 * GROUP :] = jnp.zeros((4 * TOK, 64), BF)
    da = mm_rt(right[:, : 3 * GROUP], w[depth]).astype(BF)
    spot = here()
    if depth == 1:
        groups = refs[-1]
        groups[...] = da.reshape(4, TOK, D)
        for d, o in enumerate(refs[:4]):
            o[...] = groups[lax.rem(spot["x"] + d, 4)]
    else:
        (stack,) = refs
        for x in range(4):
            rank = rank_of(1 - spot["c"], x)
            for t in range(6):
                rows = pl.ds(pl.multiple_of((4 * t + rank) * TOK, TOK), TOK)
                stack[rows, :] = da[TOK * x : TOK * x + TOK, TOK * t : TOK * t + TOK]


def spread(depth, dq, own, got, cos, sin, w):
    shapes = [sds((TOK, D), BF)] * 4 if depth == 1 else [sds((6 * 4 * TOK, TOK), BF)]
    right, *blocks = pl.pallas_call(
        lambda *refs: spread_kernel(depth, *refs),
        out_shape=[sds((4 * TOK, 3 * GROUP + 64), BF)] + shapes,
        in_specs=[VMEM] * 6,
        out_specs=[VMEM] * (1 + len(shapes)),
        scratch_shapes=[pltpu.VMEM((4, TOK, D), BF)] if depth == 1 else [],
        compiler_params=pltpu.CompilerParams(vmem_limit_bytes=8 * MIB),
        cost_estimate=pl.CostEstimate(flops=0, bytes_accessed=0, transcendentals=0),
        name="spread",
    )(dq, own, got, cos, sin, w)
    return right, blocks


def norm_back(da, dmid, x, gain):
    factor = norm_factor(x)
    s = x * factor
    inner = da * gain
    return dmid + factor * (inner - s * jnp.mean(inner * s, axis=-1, keepdims=True))


def project_back_kernel(dmid, x, gain, b0, b1, b2, b3, grad):
    da = b0[...].astype(F32) + b1[...].astype(F32) + b2[...].astype(F32) + b3[...].astype(F32)
    grad[...] = norm_back(da, dmid[...], x[...], gain[1:2, :])


def project_back(dmid, x, gain, blocks):
    return pl.pallas_call(
        project_back_kernel,
        out_shape=sds((TOK, D), F32),
        in_specs=[VMEM] * 7,
        out_specs=VMEM,
        compiler_params=pltpu.CompilerParams(vmem_limit_bytes=6 * MIB),
        cost_estimate=pl.CostEstimate(flops=0, bytes_accessed=0, transcendentals=0),
        name="project_back",
    )(dmid, x, gain, *blocks)


def last_grad_kernel(offset, kept, got, dmid, x, gain, activations, back):
    parts = []
    for t in range(6):
        rows = slice(TOK * t, TOK * t + TOK)
        parts.append(kept[rows, :].astype(F32) + got[offset + TOK * t : offset + TOK * t + TOK, :].astype(F32))
    da = jnp.concatenate(parts, axis=1)
    back[:TOK, :] = norm_back(da, dmid[...], x[...], gain[0:1, :]).astype(BF)
    back[TOK:, :] = activations[...]


def last_grad(member, dmid, x, gain, activations):
    return pl.pallas_call(
        lambda *refs: last_grad_kernel(member.offset, *refs),
        out_shape=sds((2 * TOK, D), BF),
        in_specs=[VMEM] * 6,
        out_specs=VMEM,
        compiler_params=pltpu.CompilerParams(vmem_limit_bytes=6 * MIB),
        cost_estimate=pl.CostEstimate(flops=0, bytes_accessed=0, transcendentals=0),
        name="last_grad",
    )(member.kept, member.got, dmid, x, gain, activations)


def exchange_x(blocks):
    return (blocks[0],) + tuple(send(blocks[d], SHIFT_X[d]) for d in (1, 2, 3))


def left_kernel(jobs, right, right_sib, both, turned):
    mine = here()["c"]
    row = 0
    for first, columns, axes, swapped in jobs:
        hot = one_hot(axes, mine, swapped) if columns == D else None
        for side, source in enumerate((right, right_sib)):
            lanes = slice(TOK * side, TOK * side + TOK)
            if hot is None:
                turned[...] = source[:, first : first + FF].T.reshape(FF // 16, 16, TOK)
                half = block_order(axes, swapped).reshape(2, 64)
                for i in range(64):
                    block = jnp.where(mine == 0, int(half[0, i]), int(half[1, i]))
                    both[row + 16 * i : row + 16 * i + 16, lanes] = turned[block]
            else:
                both[row : row + D // 2, lanes] = mm_rt(hot, source[:, first : first + D]).astype(BF)
        row += columns // 2


def left_sides(right, right_sib, jobs):
    rows = sum(columns // 2 for _, columns, _, _ in jobs)
    return pl.pallas_call(
        lambda *refs: left_kernel(jobs, *refs),
        out_shape=stored((rows, 2 * TOK), BF),
        in_specs=[VMEM] * 2,
        out_specs=VMEM,
        scratch_shapes=[pltpu.VMEM((FF // 16, 16, TOK), BF)],
        compiler_params=pltpu.CompilerParams(vmem_limit_bytes=8 * MIB),
        cost_estimate=pl.CostEstimate(flops=0, bytes_accessed=0, transcendentals=0),
        name="left_sides",
    )(right, right_sib)


def along_kernel(rows, along):
    normed = rows[...].reshape(4 * TOK, D)
    for side in range(2):
        along[D // 2 * side : D // 2 * side + D // 2, :] = mm_rt(one_hot("yzx", side, "yz"), normed).astype(BF)


def left_along(rows):
    return pl.pallas_call(
        along_kernel,
        out_shape=stored((D, 4 * TOK), BF),
        in_specs=[VMEM],
        out_specs=VMEM,
        compiler_params=pltpu.CompilerParams(vmem_limit_bytes=8 * MIB),
        cost_estimate=pl.CostEstimate(flops=0, bytes_accessed=0, transcendentals=0),
        name="left_along",
    )(at_rest(rows))


def rows_kernel(wq, wk, wv, wg, wu, na, nf, rq, rk, rv, rg, ru, gains, bq, bk, bv, bg, bu, sems):
    first = here()["flat"] * 6
    start = pl.multiple_of(jnp.minimum((first >> 4) << 4, D - 32), 16)
    copies = [
        pltpu.make_async_copy(w.at[:, pl.ds(start, 32), :], buf, sems.at[i])
        for i, (w, buf) in enumerate(((wq, bq), (wk, bk), (wv, bv), (wg, bg), (wu, bu)))
    ]
    for copy in copies:
        copy.start()
    lane = lax.broadcasted_iota(jnp.int32, (8, D), 1)
    pick = lane == lax.broadcasted_iota(jnp.int32, (8, D), 0) + first
    column = lax.broadcasted_iota(jnp.int32, (8, TOK), 1)
    result = jnp.ones((8, TOK), F32)
    for i, row in enumerate((na[0:1, :], na[1:2, :], nf[0:1, :], nf[1:2, :])):
        value = jnp.sum(jnp.where(pick, row, 0.0), axis=1, keepdims=True)
        result = jnp.where(column == i, value, result)
    gains[...] = result
    place = lax.broadcasted_iota(jnp.int32, (8, 32), 1)
    hot = jnp.where(place == lax.broadcasted_iota(jnp.int32, (8, 32), 0) + (first - start), 1.0, 0.0).astype(BF)
    for copy, buf, out in zip(copies, (bq, bk, bv, bg, bu), (rq, rk, rv, rg, ru)):
        copy.wait()
        for layer in range(2):
            out[layer] = mm(hot, buf[layer])


def own_rows(wq, wk, wv, wg, wu, na, nf):
    return pl.pallas_call(
        rows_kernel,
        out_shape=[stored((2, 8, D), F32)] * 3 + [stored((2, 8, FF), F32)] * 2 + [stored((8, TOK), F32)],
        in_specs=[HBM] * 5 + [VMEM] * 2,
        out_specs=[VMEM] * 6,
        scratch_shapes=[pltpu.VMEM((2, 32, D), BF)] * 3
        + [pltpu.VMEM((2, 32, FF), BF)] * 2
        + [pltpu.SemaphoreType.DMA((5,))],
        compiler_params=pltpu.CompilerParams(vmem_limit_bytes=6 * MIB),
        cost_estimate=pl.CostEstimate(flops=0, bytes_accessed=0, transcendentals=0),
        name="own_rows",
    )(*map(at_rest, (wq, wk, wv, wg, wu)), na, nf)


def slot(rows):
    return -(-rows // 16) * 16


class Member:
    def __init__(self, kept, rows, tiles, offset):
        self.kept, self.rows, self.tiles, self.offset = kept, rows, tiles, offset
        self.got = None


def for_tiles(tiles, body):
    if tiles <= 6:
        for t in range(tiles):
            body(t)
    else:
        @pl.loop(0, tiles // 2)
        def _(i):
            body(2 * i)
            body(2 * i + 1)


def aligned(value):
    return value if isinstance(value, int) else pl.multiple_of(value, 16)


def bit_of(spot, which):
    if which == "c":
        return spot["c"]
    axis, step = which[0], which[1]
    rank = rank_of(1 - spot["c"] if len(which) > 2 else spot["c"], spot[axis])
    return rank // 2 if step == 0 else lax.rem(rank, 2)


def sums_kernel(tasks, *refs):
    spot = here()
    for task in tasks:
        kind, bit = task["kind"], bit_of(spot, task["bit"])
        pack, offset, kept_ref = refs[task["pack"]], task["offset"], refs[task["kept"]]
        half, tiles = task["half"], task["tiles"]
        out_slot = slot(half)
        if kind == "weights":
            left, right, right_sib = (refs[i] for i in task["ins"])
            for out, base, side in ((pack, offset, 1 - bit), (kept_ref, 0, bit)):
                lhs = left[pl.ds(pl.multiple_of(task["row"] + side * half, 64), half), :]
                for t in range(0, tiles, 2):
                    col = task["column"] + TOK * t
                    rhs = jnp.concatenate(
                        [right[:, col : col + 2 * TOK], right_sib[:, col : col + 2 * TOK]], axis=0
                    )
                    part = mm(lhs, rhs).astype(BF)
                    out[base + t * half : base + (t + 1) * half, :] = part[:, :TOK]
                    out[base + (t + 1) * half : base + (t + 2) * half, :] = part[:, TOK:]
        elif kind == "along":
            left, right = (refs[i] for i in task["ins"])
            for out, base, side in ((pack, offset, 1 - bit), (kept_ref, 0, bit)):
                part = mm(left[pl.ds(pl.multiple_of(side * half, 64), half), :], right[...]).astype(BF)
                for t in range(tiles):
                    out[base + t * half : base + (t + 1) * half, :] = part[:, TOK * t : TOK * t + TOK]
        elif kind == "first":
            value, base, in_slot = refs[task["ins"][0]], task["came"], slot(2 * half)
            for t in range(tiles):
                at = base + t * in_slot
                if half % 16 == 0:
                    pack[offset + t * out_slot : offset + t * out_slot + half, :] = value[
                        pl.ds(pl.multiple_of(at + (1 - bit) * half, 16), half), :
                    ]
                    kept_ref[t * out_slot : t * out_slot + half, :] = value[
                        pl.ds(pl.multiple_of(at + bit * half, 16), half), :
                    ]
                else:
                    both = value[at : at + 2 * half, :].astype(F32)
                    low, high = both[:half], both[half:]
                    pack[offset + t * out_slot : offset + t * out_slot + half, :] = jnp.where(bit == 0, high, low).astype(BF)
                    kept_ref[t * out_slot : t * out_slot + half, :] = jnp.where(bit == 0, low, high).astype(BF)
        else:
            value, got = (refs[i] for i in task["ins"])
            came, in_slot = task["came"], slot(2 * half)

            def one(t, half=half, out_slot=out_slot, in_slot=in_slot, came=came, offset=offset, bit=bit,
                    value=value, got=got, pack=pack, kept_ref=kept_ref):
                if half % 16 == 0:
                    for out, base, side in ((pack, offset, 1 - bit), (kept_ref, 0, bit)):
                        at = t * in_slot + side * half
                        total = (
                            value[pl.ds(pl.multiple_of(at, 16), half), :].astype(F32)
                            + got[pl.ds(pl.multiple_of(came + at, 16), half), :].astype(F32)
                        )
                        out[pl.ds(aligned(base + t * out_slot), half), :] = total.astype(BF)
                else:
                    total = (
                        value[pl.ds(aligned(t * in_slot), 2 * half), :].astype(F32)
                        + got[pl.ds(aligned(came + t * in_slot), 2 * half), :].astype(F32)
                    )
                    low, high = total[:half], total[half:]
                    pack[pl.ds(aligned(offset + t * out_slot), half), :] = jnp.where(bit == 0, high, low).astype(BF)
                    kept_ref[pl.ds(aligned(t * out_slot), half), :] = jnp.where(bit == 0, low, high).astype(BF)

            for_tiles(tiles, one)


def sums(jobs):
    arrays, tasks, pack_rows, rest = [], [], {}, []

    def at(array):
        for i, a in enumerate(arrays):
            if a is array:
                return i
        arrays.append(array)
        return len(arrays) - 1

    flops = 0
    for job in jobs:
        if job[0] == "weights":
            _, left, row, rows, right, right_sib, column, columns, bit, pack = job
            rest.append(left)
            task = dict(kind="weights", ins=[at(left), at(right), at(right_sib)], row=row, column=column,
                        half=rows // 2, tiles=columns // TOK, bit=bit)
            flops += 4 * rows * columns * TOK
        elif job[0] == "along":
            _, left, right, pack = job
            rest.append(left)
            task = dict(kind="along", ins=[at(left), at(right)], half=D // 2, tiles=right.shape[1] // TOK, bit="c")
            flops += 2 * D * right.shape[1] * 4 * TOK
        elif job[0] == "first":
            _, array, base, rows, tiles, bit, pack = job
            task = dict(kind="first", ins=[at(array)], came=base, half=rows // 2, tiles=tiles, bit=bit)
        else:
            _, member, bit, pack = job
            task = dict(kind="step", ins=[at(member.kept), at(member.got)], came=member.offset,
                        half=member.rows // 2, tiles=member.tiles, bit=bit)
        task["pack"], task["offset"] = pack, pack_rows.get(pack, 0)
        pack_rows[pack] = task["offset"] + task["tiles"] * slot(task["half"])
        tasks.append(task)
    names = sorted(pack_rows)
    shapes = [sds((pack_rows[n], TOK), BF) for n in names]
    for i, task in enumerate(tasks):
        task["kept"] = len(arrays) + len(names) + i
        task["pack"] = len(arrays) + names.index(task["pack"])
        shapes.append(sds((task["tiles"] * slot(task["half"]), TOK), BF))
    moved = sum(a.size for a in arrays) + sum(np.prod(s.shape) for s in shapes)
    outs = pl.pallas_call(
        lambda *refs: sums_kernel(tasks, *refs),
        out_shape=shapes,
        in_specs=[VMEM] * len(arrays),
        out_specs=[VMEM] * len(shapes),
        compiler_params=pltpu.CompilerParams(vmem_limit_bytes=10 * MIB),
        cost_estimate=pl.CostEstimate(flops=0, bytes_accessed=0, transcendentals=0),
        name="sums",
    )(*(at_rest(a) if any(a is r for r in rest) else a for a in arrays))
    packs = dict(zip(names, outs))
    members = [
        Member(kept, task["half"], task["tiles"], task["offset"]) for kept, task in zip(outs[len(names) :], tasks)
    ]
    return packs, members


def came(members, got):
    for member in members:
        member.got = got


def finish_kernel(plan, places, *refs):
    back, arrays = refs[6], refs[7:-19]
    acts, gtok, gq, gk, gv, go, ggate, gup, gdown, gattn, gffn, by_x = refs[-19:-7]
    wq, wk, wv, wg, wu, gains = refs[-7:-1]
    copies = [
        pltpu.make_async_copy(source, buf, refs[-1].at[i]) for i, (source, buf) in enumerate(zip(refs[:6], refs[-7:-1]))
    ]
    for copy in copies:
        copy.start()
    gtok[...] = back[:TOK, :].astype(F32)
    acts[...] = back[TOK:, :]
    spot = here()
    mine = spot["x"]
    across, beside = 3 - mine, mine + 1 - 2 * lax.rem(mine, 2)
    first = jnp.where(spot["c"] == 0, beside, across)
    second = jnp.where(spot["c"] == 0, across, beside)
    opposite = lax.rem(mine + 2, 4)
    for m in range(2):
        (kept, got, offset), (kept_b, got_b, offset_b) = places[m]
        for group, array, base in (
            (mine, kept, 0), (first, kept_b, 0), (second, got, offset), (opposite, got_b, offset_b)
        ):
            by_x[4 * m + group] = arrays[array][base : base + 80, :]

    def total(name):
        kept, got, offset, tiles, rows = plan[name]
        parts = []
        for t in range(tiles):
            parts.append(
                arrays[kept][16 * t : 16 * t + rows, :].astype(F32)
                + arrays[got][offset + 16 * t : offset + 16 * t + rows, :].astype(F32)
            )
        return jnp.concatenate(parts, axis=1)

    lane = lax.broadcasted_iota(jnp.int32, (8, TOK), 1)
    result = jnp.zeros((8, TOK), F32)
    filler = jnp.zeros((2, 1), F32)
    both = jnp.concatenate([total("gate0"), total("up0")], axis=1), total("gu1")
    gates = [b[:, :FF] for b in both]
    ups = [b[:, FF:] for b in both]
    for layer in range(2):
        ggate[:, layer, :] = gates[layer]
        gup[:, layer, :] = ups[layer]
        go[:, layer, :] = total(f"out{layer}")
        gdown[layer] = total(f"down{layer}")
    for copy in copies:
        copy.wait()
    for layer in range(2):
        m = 1 - layer
        rows = [
            jnp.concatenate([by_x[4 * m + x, 16 * t : 16 * t + 6, :] for t in range(5)], axis=1) for x in range(4)
        ]
        acc = jnp.zeros((6, 1), F32)
        for i, (out, w) in enumerate(((gk, wk), (gv, wv), (gq, wq))):
            value = jnp.concatenate([r[:, GROUP * i : GROUP * i + GROUP] for r in rows], axis=1).astype(F32)
            out[:, layer, :] = value
            acc = acc + jnp.sum(value * w[layer][:6], axis=1, keepdims=True)
        result = jnp.where(lane == layer, jnp.concatenate([acc / gains[:6, layer : layer + 1], filler], axis=0), result)
        gate, up = gates[layer], ups[layer]
        acc = jnp.sum(gate * wg[layer][:6], axis=1, keepdims=True) + jnp.sum(
            up * wu[layer][:6], axis=1, keepdims=True
        )
        result = jnp.where(lane == 2 + layer, jnp.concatenate([acc / gains[:6, 2 + layer : 3 + layer], filler], axis=0), result)
    turned = result.T
    gattn[...] = turned[0:2, :6]
    gffn[...] = turned[2:4, :6]


def finish(rows_of, back, members, projections):
    arrays, plan = [], {}

    def at(array):
        for i, a in enumerate(arrays):
            if a is array:
                return i
        arrays.append(array)
        return len(arrays) - 1

    for name, m in members.items():
        plan[name] = (at(m.kept), at(m.got), m.offset, m.tiles, m.rows)
    places = [[(at(m.kept), at(m.got), m.offset) for m in pair] for pair in projections]
    return pl.pallas_call(
        lambda *refs: finish_kernel(plan, places, *refs),
        out_shape=[sds((TOK, D), BF), sds((TOK, D), F32)]
        + [sds((6, 2, D), F32)] * 4
        + [sds((6, 2, FF), F32)] * 2
        + [sds((2, 16, D), F32), sds((2, 6), F32), sds((2, 6), F32)],
        in_specs=[HBM] * 6 + [VMEM] * (1 + len(arrays)),
        out_specs=[VMEM] * 11,
        scratch_shapes=[pltpu.VMEM((8, 80, TOK), BF)]
        + [pltpu.VMEM((2, 8, D), F32)] * 3
        + [pltpu.VMEM((2, 8, FF), F32)] * 2
        + [pltpu.VMEM((8, TOK), F32), pltpu.SemaphoreType.DMA((6,))],
        compiler_params=pltpu.CompilerParams(vmem_limit_bytes=8 * MIB),
        cost_estimate=pl.CostEstimate(flops=0, bytes_accessed=0, transcendentals=0),
        name="finish",
    )(*map(at_rest, rows_of), back, *arrays)


def tie(value, *others):
    return lax.optimization_barrier((value,) + others)[0]


def per_device(
    tokens, seg_lengths, cotangent, norm_attn, w_query, w_key, w_value, w_out, norm_ffn, w_gate, w_up, w_down
):
    with jax.named_scope("S_setup"):
        _, early = first_norm(tokens[0], norm_attn, True)
        first_blocks = [send(early, GATHER[d]) for d in (1, 2, 3)]
        moved = send(tokens[0], RELOCATE)
        lengths = send(seg_lengths[0], RELOCATE)
        cot = send(cotangent[0], RELOCATE)
        x, normed = first_norm(moved, norm_attn)
        heads = own_heads(w_query, w_key, w_value)
        cos, sin, starts = tables(lengths)

    kept, carried, alongs = [], [], []
    for depth in range(2):
        with jax.named_scope(f"S_ahead{depth}"):
            blocks = exchange_x([normed] * 4) if depth else (normed, *first_blocks)
            if depth == 1:
                alongs.append(left_along(rows))
                cot = tie(cot, alongs[0])
                rows_of = own_rows(w_query, w_key, w_value, w_gate, w_up, norm_attn, norm_ffn)
                blocks = (tie(blocks[0], cot, *rows_of),) + tuple(blocks[1:])
            q, own, rows = project(depth, blocks, heads, cos, sin)
            sib = send(own, CORE)
            *blocks, q, kv, lse = attend(q, own, sib, starts)
            blocks = exchange_x(blocks)
            if depth == 1:
                alongs.append(left_along(rows))
                blocks = (tie(blocks[0], alongs[1]),) + tuple(blocks[1:])
            result, normed, acts, middle, slopes = feed(
                depth, x, norm_ffn, norm_attn, blocks, w_out, w_gate, w_up, w_down
            )
            kept.append((x, q, kv, lse, middle, slopes))
            carried.append(acts)
            x = result
    activations = x

    def step(members, bit, pack):
        return [("step", m, bit, pack) for m in members]

    half = D // 2
    x, q, kv, lse, middle, slopes = kept[1]
    with jax.named_scope("S_back1"):
        right, dmid, *blocks = feed_back(
            1, cot, middle, slopes, norm_ffn, w_down, w_gate, w_up, w_out, [carried[1], carried[0]]
        )
        blocks = exchange_x(blocks)
        right_sib = send(right, CORE)
    with jax.named_scope("S_back1"):
        dq, own, sib = attend_back(q, kv, starts, lse, blocks)
        right1, blocks = spread(1, dq, own, send(sib, CORE), cos, sin, heads)
        blocks = exchange_x(blocks)
    with jax.named_scope("S_sum1"):
        base1 = 2 * FF + 2 * D
        base0 = base1 + 2 * D + FF
        left = left_sides(tie(right, right1), right_sib, [(base1, D, "yzx", "yz")])
        packs, (gu1,) = sums([("weights", left, 0, D // 2, right, right_sib, 0, 2 * FF, ("y", 0, "swapped"), "y")])
        came([gu1], send(packs["y"], PAIR["y", 1]))
        left = left_sides(
            tie(right, gu1.got), right_sib,
            [
                (base0, D, "xzy", ""),
                (base0, D, "yzx", ""),
                (base0 + D, D, "xzy", ""),
                (base0 + 2 * D, FF, "zyx", ""),
                (base1 + D, D, "xzy", ""),
                (base1 + 2 * D, FF, "zyx", ""),
            ],
        )
        late, late_sib = right, right_sib
    with jax.named_scope("S_back1"):
        blocks = (tie(blocks[0], packs["y"]),) + tuple(blocks[1:])
        grad = project_back(dmid, x, norm_attn, blocks)

    x, q, kv, lse, middle, slopes = kept[0]
    with jax.named_scope("S_back0"):
        right, dmid, *blocks = feed_back(0, grad, middle, slopes, norm_ffn, w_down, w_gate, w_up, w_out, [])
        blocks = exchange_x(blocks)
        right_sib = send(right, CORE)
    with jax.named_scope("S_sum0"):
        packs, (gate0, up0, out0, down0, out1, down1, gu1) = sums(
            [
                ("weights", left, 0, D // 2, tie(right, *blocks), right_sib, 0, ALONG_X, ("x", 0), "x"),
                ("weights", left, half, D // 2, right, right_sib, ALONG_X, 2 * FF - ALONG_X, ("y", 0), "y"),
                ("weights", left, 2 * half, D // 2, right, right_sib, 2 * FF + D, D, ("x", 0), "x"),
                ("weights", left, 3 * half, FF // 2, right, right_sib, 2 * FF, D, ("z", 0), "z"),
                ("weights", left, 3 * half + FF // 2, D // 2, late, late_sib, 2 * FF + D, D, ("x", 0), "x"),
                ("weights", left, 4 * half + FF // 2, FF // 2, late, late_sib, 2 * FF, D, ("z", 0), "z"),
            ]
            + step([gu1], ("y", 1, "swapped"), "y")
        )
        came([gate0, out0, out1], send(packs["x"], PAIR["x", 0]))
        came([up0, gu1], send(packs["y"], PAIR["y", 0]))
        came([down0, down1], send(packs["z"], PAIR["z", 0]))
    with jax.named_scope("S_back0"):
        blocks = (tie(blocks[0], packs["x"], packs["y"], packs["z"]),) + tuple(blocks[1:])
        dq, own, sib = attend_back(q, kv, starts, lse, blocks)
        right0, (partial,) = spread(0, dq, own, send(sib, CORE), cos, sin, heads)

    with jax.named_scope("S_sum0"):
        packs, (qkv1, qkv0) = sums([("along", alongs[1], right1, "c"), ("along", alongs[0], right0, "c")])
        came([qkv1, qkv0], send(packs["c"], CORE))
        packs, (gate0, out0, out1, up0, down0, down1, gu1, qkv1, qkv0, da) = sums(
            step([gate0, out0, out1], ("x", 1), "x")
            + step([up0], ("y", 1), "y")
            + step([down0, down1], ("z", 1), "z")
            + step([gu1], ("z", 0, "swapped"), "z")
            + step([qkv1, qkv0], ("y", 0, "swapped"), "y")
            + [("first", partial, 0, 4 * TOK, 6, ("x", 0, "swapped"), "x")],
        )
        came([down0, down1, gu1], send(packs["z"], PAIR["z", 1]))
        came([gate0, out0, out1, da], send(packs["x"], PAIR["x", 1]))
        came([up0, qkv1, qkv0], send(packs["y"], PAIR["y", 1]))
        packs, (down0, down1, gate0, out0, out1, up0, gu1, qkv1, qkv0, da) = sums(
            step([down0, down1], ("y", 0), "y")
            + step([gate0, out0, out1, up0], ("z", 0), "z")
            + step([gu1], ("z", 1, "swapped"), "z")
            + step([qkv1, qkv0], ("y", 1, "swapped"), "y")
            + step([da], ("x", 1, "swapped"), "x"),
        )
        came([gate0, out0, out1, up0, gu1], send(packs["z"], PAIR["z", 0]))
        came([down0, down1, qkv1, qkv0], send(packs["y"], PAIR["y", 0]))
        came([da], send(packs["x"], PAIR["x", 0]))
        back = send(last_grad(da, dmid, x, norm_attn, activations), RESTORE)
        packs, (down0, down1, gate0, out0, out1, up0, qkv1, qkv0) = sums(
            step([down0, down1], ("y", 1), "y")
            + step([gate0, out0, out1, up0], ("z", 1), "z")
            + step([qkv1, qkv0], ("z", 0, "swapped"), "z"),
        )
        came([gate0, out0, out1, up0, qkv1, qkv0], send(packs["z"], PAIR["z", 1]))
        came([down0, down1], send(packs["y"], PAIR["y", 1]))
        packs, (gate0, out0, out1, qkv1, qkv0) = sums(
            step([gate0, out0, out1], ("y", 0), "y") + step([qkv1, qkv0], ("z", 1, "swapped"), "z")
        )
        came([gate0, out0, out1], send(packs["y"], PAIR["y", 0]))
        came([qkv1, qkv0], send(packs["z"], PAIR["z", 0]))
        packs, (gate0, out0, out1, up0, down0, down1, gu1, qkv1, qkv0) = sums(
            step([gate0, out0, out1], ("y", 1), "y")
            + step([up0, down0, down1, gu1, qkv1, qkv0], ("x", 0), "x"),
        )
        came([up0, down0, down1, gu1, qkv1, qkv0], send(packs["x"], PAIR["x", 0]))
        came([gate0, out0, out1], send(packs["y"], PAIR["y", 1]))
        gu1.kept = tie(gu1.kept, back)
        packs, (up0, down0, down1, gu1, mine1, first1, mine0, first0) = sums(
            step([up0, down0, down1, gu1], ("x", 1), "x")
            + [
                ("first", array, offset, 12, 5, ("x", 1), "x")
                for m in (qkv1, qkv0)
                for array, offset in ((m.kept, 0), (m.got, m.offset))
            ],
        )
        came([up0, down0, down1, gu1, mine1, first1, mine0, first0], send(packs["x"], PAIR["x", 1]))
        activations, grad_tokens, grad_q, grad_k, grad_v, grad_o, grad_gate, grad_up, grad_down, grad_attn, grad_ffn = finish(
            rows_of, back,
            dict(gate0=gate0, up0=up0, gu1=gu1, out0=out0, out1=out1, down0=down0, down1=down1),
            [(mine1, first1), (mine0, first0)],
        )
    return (
        activations[None],
        grad_tokens[None],
        grad_attn,
        jnp.swapaxes(grad_q, 0, 1),
        jnp.swapaxes(grad_k, 0, 1),
        jnp.swapaxes(grad_v, 0, 1),
        jnp.swapaxes(grad_o, 0, 1),
        grad_ffn,
        jnp.swapaxes(grad_gate, 0, 1),
        jnp.swapaxes(grad_up, 0, 1),
        grad_down,
    )


def solution(mesh):
    rows = P("batch", "seq", None)
    split = P(None, AXES)
    split3 = P(None, AXES, None)
    return jax.shard_map(
        per_device,
        mesh=mesh,
        in_specs=(rows, P("batch", None), rows) + (P(),) * 9,
        out_specs=(rows, rows, split, split3, split3, split3, split3, split, split3, split3, split3),
        check_vma=False,
    )
```

```python
import jax
import jax.numpy as jnp
import numpy as np
from jax import lax
from jax.experimental import pallas as pl
from jax.experimental.pallas import tpu as pltpu
from jax.sharding import PartitionSpec as P

D = 768
HEADS = 12
HEAD_DIM = 64
FF = 2048
ALONG_X = FF + 256
TOK = 128
ROW = 1024
GRID = 16
GROUP = 3 * HEAD_DIM
OFF = {"k": 0, "v": GROUP, "q": 2 * GROUP}
EPS = 1e-05
AXES = ("seq", "batch")
BF = jnp.bfloat16
F32 = jnp.float32
MIB = 1 << 20


def place(flat):
    seq, batch = divmod(flat, 16)
    z_lo, x = divmod(seq, 4)
    y, rest = divmod(batch, 4)
    z_hi, core = divmod(rest, 2)
    return dict(x=x, y=y, z=z_hi * 2 + z_lo, c=core)


def flat_of(p):
    z_hi, z_lo = divmod(p["z"], 2)
    return (z_lo * 4 + p["x"]) * 16 + p["y"] * 4 + z_hi * 2 + p["c"]


def permutation(move):
    pairs = []
    for flat in range(128):
        p = place(flat)
        move(p)
        pairs.append((flat, flat_of(p)))
    return pairs


def move_relocate(p):
    z_hi, z_lo = divmod(p["z"], 2)
    core = p["c"]
    p["z"] = z_hi * 2 + core
    p["c"] = z_lo ^ (1 if p["x"] >= 2 else 0)


RELOCATE = permutation(move_relocate)
RESTORE = sorted((dst, src) for src, dst in RELOCATE)


def move_core(p):
    p["c"] ^= 1


CORE = permutation(move_core)


def shift_x(by):
    def move(p):
        p["x"] = (p["x"] + by) % 4

    return permutation(move)


SHIFT_X = {d: shift_x(d) for d in (1, 2, 3)}


def pair_step(axis, step):
    def move(p):
        at = p[axis]
        p[axis] = at ^ 1 if (p["c"] == 0) == (step == 0) else 3 - at

    return permutation(move)


PAIR = {(axis, step): pair_step(axis, step) for axis in "xyz" for step in (0, 1)}


def relocate_and_shift(by):
    def move(p):
        move_relocate(p)
        p["x"] = (p["x"] + by) % 4

    return permutation(move)


GATHER = {d: relocate_and_shift(d) for d in (1, 2, 3)}


def send(value, pairs):
    return lax.ppermute(value, AXES, pairs)


RING_ORDER = {0: (0, 3, 1, 2), 1: (0, 1, 2, 3)}


def block_order(axes, swapped=""):
    order = []
    for core in (0, 1):
        first, second, third = (RING_ORDER[1 - core if axis in swapped else core] for axis in axes)
        for a in first:
            for b in second:
                for c in third:
                    order.append(flat_of({axes[0]: a, axes[1]: b, axes[2]: c, "c": core}))
    return np.array(order)


def one_hot(axes, core, swapped=""):
    row = lax.broadcasted_iota(jnp.int32, (D // 2, 1), 0)
    block = (row * 10923) >> 16
    within = row - 6 * block
    places = {}
    for i, axis in enumerate(axes):
        at = (block >> (4 - 2 * i)) & 3
        ring = jnp.where(at == 0, 0, jnp.where(at == 1, 3, at - 1))
        places[axis] = jnp.where(core == (1 if axis in swapped else 0), ring, at)
    z = places["z"]
    flat = ((z & 1) * 4 + places["x"]) * 16 + places["y"] * 4 + (z >> 1) * 2 + core
    lane = lax.broadcasted_iota(jnp.int32, (D // 2, D), 1)
    return jnp.where(lane == flat * 6 + within, 1.0, 0.0).astype(BF)


def mm(left, right):
    return jnp.dot(left, right, preferred_element_type=F32)


def mm_rt(left, right):
    return lax.dot_general(left, right, (((1,), (1,)), ((), ())), preferred_element_type=F32)


def mm_lt(left, right):
    return lax.dot_general(left, right, (((0,), (0,)), ((), ())), preferred_element_type=F32)


VMEM = pl.BlockSpec(memory_space=pltpu.VMEM)
SMEM = pl.BlockSpec(memory_space=pltpu.SMEM)
HBM = pl.BlockSpec(memory_space=pltpu.HBM)


def pinned(*weights):
    return tuple(pltpu.with_memory_space_constraint(w, pltpu.VMEM) for w in weights)


def at_rest(value):
    return pltpu.with_memory_space_constraint(value, pltpu.HBM)


def stored(shape, kind):
    return pltpu.HBM(shape, kind)


def sds(shape, kind):
    return jax.ShapeDtypeStruct(shape, kind)


def here():
    seq, batch = lax.axis_index("seq"), lax.axis_index("batch")
    return dict(
        x=lax.rem(seq, 4), y=batch // 4, z=lax.rem(batch // 2, 2) * 2 + seq // 4, c=lax.rem(batch, 2), flat=seq * 16 + batch
    )


def rank_of(core, at):
    return jnp.where(core == 0, jnp.where(at == 0, 0, jnp.where(at == 3, 1, at + 1)), at)


def ordered_by_x(mine, blocks, out):
    for d, b in enumerate(blocks):
        out[lax.rem(mine - d + 4, 4)] = b[...]


def norm_factor(values):
    return lax.rsqrt(jnp.mean(values * values, axis=-1, keepdims=True) + EPS)


def first_norm_kernel(tokens, gain, x, normed):
    values = tokens[...].astype(F32)
    x[...] = values
    normed[...] = (values * norm_factor(values) * gain[0:1, :]).astype(BF)


def first_norm(tokens, gain, first=False):
    return pl.pallas_call(
        first_norm_kernel,
        out_shape=[sds((TOK, D), F32), sds((TOK, D), BF)],
        in_specs=[VMEM] * 2,
        out_specs=[VMEM] * 2,
        compiler_params=pltpu.CompilerParams(vmem_limit_bytes=4 * MIB),
        cost_estimate=pl.CostEstimate(flops=0, bytes_accessed=0, transcendentals=0),
        name="first_norm",
    )(*map(at_rest, (tokens, gain)) if first else (tokens, gain))


def tables_kernel(lengths, freqs, cos, sin, starts):
    core = here()["c"]

    def places(shape, dim, base):
        r = lax.broadcasted_iota(jnp.int32, shape, dim) + base
        block = r >> 7
        block = jnp.where(core == 0, jnp.where(block < 2, block, block + 4), jnp.where(block < 2, block + 4, block))
        return (block << 7) + (r & 127)

    def begin(place):
        start = lengths[0] * 0
        result = jnp.zeros_like(place)
        for i in range(5):
            end = start + lengths[i]
            result = jnp.where((place >= start) & (place < end), start, result)
            start = end
        return result

    for half in range(2):
        starts[half : half + 1, :] = begin(places((1, 256), 1, 256 * half))
    place = places((4 * TOK, 1), 0, 0)
    inside = place - begin(place)
    offset = jnp.maximum(inside - 1, 0)
    lane = lax.broadcasted_iota(jnp.int32, (4 * TOK, TOK), 1)
    rows = (offset >> 4).astype(F32)
    columns = (offset & (GRID - 1)).astype(F32)
    angles = jnp.where((lane & 63) < 32, rows, columns) * freqs[...]
    angles = jnp.where(inside > 0, angles, 0.0)
    cos[...] = jnp.cos(angles)
    sin[...] = jnp.where((lane & 1) == 0, -1.0, 1.0) * jnp.sin(angles)


def tables(lengths):
    freqs = 10000.0 ** (-4.0 * np.arange(HEAD_DIM // 4, dtype=np.float32) / HEAD_DIM)
    freqs = np.tile(np.repeat(freqs.astype(np.float32), 2), 4)[None, :]
    return pl.pallas_call(
        tables_kernel,
        out_shape=[sds((4 * TOK, TOK), F32), sds((4 * TOK, TOK), F32), sds((2, 256), jnp.int32)],
        in_specs=[SMEM, VMEM],
        out_specs=[VMEM] * 3,
        compiler_params=pltpu.CompilerParams(vmem_limit_bytes=4 * MIB),
        cost_estimate=pl.CostEstimate(flops=0, bytes_accessed=0, transcendentals=0),
        name="tables",
    )(lengths, jnp.asarray(freqs))


def own_heads_kernel(wq, wk, wv, out, bq, bk, bv, sems):
    x = here()["x"]
    start = pl.multiple_of((x * GROUP // TOK) * TOK, TOK)
    copies = [
        pltpu.make_async_copy(w.at[:, :, pl.ds(start, 2 * TOK)], buf, sems.at[i])
        for i, (w, buf) in enumerate(((wk, bk), (wv, bv), (wq, bq)))
    ]
    for copy in copies:
        copy.start()
    for i, (copy, buf) in enumerate(zip(copies, (bk, bv, bq))):
        copy.wait()
        for layer in range(2):
            w = buf[layer]
            out[layer, :, GROUP * i : GROUP * i + GROUP] = jnp.where(lax.rem(x, 2) == 0, w[:, :GROUP], w[:, 64:])


def own_heads(wq, wk, wv):
    return pl.pallas_call(
        own_heads_kernel,
        out_shape=sds((2, D, 3 * GROUP), BF),
        in_specs=[HBM] * 3,
        out_specs=VMEM,
        scratch_shapes=[pltpu.VMEM((2, D, 2 * TOK), BF)] * 3 + [pltpu.SemaphoreType.DMA((3,))],
        compiler_params=pltpu.CompilerParams(vmem_limit_bytes=8 * MIB),
        cost_estimate=pl.CostEstimate(flops=0, bytes_accessed=0, transcendentals=0),
        name="own_heads",
    )(*map(at_rest, (wq, wk, wv)))


def turn_group(values, cos, sin):
    lane = lax.broadcasted_iota(jnp.int32, (values.shape[0], 128), 1)
    even = lane % 2 == 0
    tail = jnp.concatenate([values[:, 128:], jnp.zeros((values.shape[0], 64), F32)], axis=1)
    parts = []
    for v in (values[:, :128], tail):
        swapped = jnp.where(even, pltpu.roll(v, 127, 1), pltpu.roll(v, 1, 1))
        parts.append(v * cos + swapped * sin)
    return jnp.concatenate([parts[0], parts[1][:, :64]], axis=1)


def project_kernel(depth, n0, n1, n2, n3, w, cos, sin, q, own, rows_out, rows, sem):
    ordered_by_x(here()["x"], (n0, n1, n2, n3), rows)
    store = pltpu.make_async_copy(rows, rows_out, sem)
    store.start()
    normed = rows[...].reshape(4 * TOK, D)
    y = mm(normed, w[depth])
    own[:, :GROUP] = turn_group(y[:, :GROUP], cos[...], sin[...]).astype(BF)
    own[:, GROUP:] = y[:, GROUP : 2 * GROUP].astype(BF)
    q[...] = turn_group(y[:, 2 * GROUP :], cos[...], sin[...]).astype(BF)
    store.wait()


def project(depth, normed, w, cos, sin):
    return pl.pallas_call(
        lambda *refs: project_kernel(depth, *refs),
        out_shape=[sds((4 * TOK, GROUP), BF), sds((4 * TOK, 2 * GROUP), BF), stored((4, TOK, D), BF)],
        in_specs=[VMEM] * 7,
        out_specs=[VMEM] * 2 + [HBM],
        scratch_shapes=[pltpu.VMEM((4, TOK, D), BF), pltpu.SemaphoreType.DMA(())],
        compiler_params=pltpu.CompilerParams(vmem_limit_bytes=8 * MIB),
        cost_estimate=pl.CostEstimate(flops=0, bytes_accessed=0, transcendentals=0),
        name="project",
    )(*normed, w, cos, sin)


def tile_scores(q, k, start, place0, n):
    raw = mm_rt(k, q)
    keys = lax.broadcasted_iota(jnp.int32, (256, 256), 0)
    asks = lax.broadcasted_iota(jnp.int32, (256, 256), 1)
    parts = []
    for at in range(0, n, 256):
        allowed = keys >= start - at
        if at == place0:
            allowed = allowed & (keys <= asks)
        parts.append(jnp.where(allowed, raw[at : at + 256], -1e30))
    return parts[0] if len(parts) == 1 else jnp.concatenate(parts, axis=0)


def attend_kernel(q, own, sib, starts, m0, m1, m2, m3, q_out, kv_out, lse_out, kv, lse, mixed, sems):
    spot = here()
    core, mine = spot["c"], spot["x"]
    stores = [
        pltpu.make_async_copy(source, out, sems.at[i])
        for i, (source, out) in enumerate(((q, q_out), (kv, kv_out), (lse, lse_out)))
    ]
    stores[0].start()

    @pl.when(core == 0)
    def _():
        kv[0:256, :] = own[0:256, :]
        kv[256:512, :] = sib[256:512, :]
        kv[512:768, :] = sib[0:256, :]
        kv[768:1024, :] = own[256:512, :]

    @pl.when(core == 1)
    def _():
        kv[0:256, :] = sib[0:256, :]
        kv[256:512, :] = own[256:512, :]
        kv[512:768, :] = own[0:256, :]
        kv[768:1024, :] = sib[256:512, :]

    stores[1].start()

    def tile(which, pos):
        n = 256 * (pos + 1)
        outs = []
        start = starts[which : which + 1, :]
        for h in range(3):
            qs = q[256 * which : 256 * which + 256, 64 * h : 64 * h + 64] * jnp.asarray(0.125, BF)
            s = tile_scores(qs, kv[0:n, 64 * h : 64 * h + 64], start, 256 * pos, n)
            top = jnp.max(s, axis=0, keepdims=True)
            e = jnp.exp(s - top)
            total = jnp.sum(e, axis=0, keepdims=True)
            probs = (e * (1.0 / total)).astype(BF)
            lse[3 * which + h : 3 * which + h + 1, :] = top + jnp.log(total)
            outs.append(mm_lt(kv[0:n, GROUP + 64 * h : GROUP + 64 * h + 64], probs))
        out = jnp.concatenate(outs, axis=0).T.astype(BF)
        mixed[2 * which] = out[:TOK]
        mixed[2 * which + 1] = out[TOK:]

    @pl.when(core == 0)
    def _():
        tile(0, 0)
        tile(1, 3)

    @pl.when(core == 1)
    def _():
        tile(0, 2)
        tile(1, 1)

    stores[2].start()
    for d, m in enumerate((m0, m1, m2, m3)):
        m[...] = mixed[lax.rem(mine + d, 4)]
    for store in stores:
        store.wait()


def attend(q, own, sib, starts):
    return pl.pallas_call(
        attend_kernel,
        out_shape=[sds((TOK, GROUP), BF)] * 4
        + [stored((4 * TOK, GROUP), BF), stored((ROW, 2 * GROUP), BF), stored((8, 256), F32)],
        in_specs=[VMEM] * 4,
        out_specs=[VMEM] * 4 + [HBM] * 3,
        scratch_shapes=[
            pltpu.VMEM((ROW, 2 * GROUP), BF),
            pltpu.VMEM((8, 256), F32),
            pltpu.VMEM((4, TOK, GROUP), BF),
            pltpu.SemaphoreType.DMA((3,)),
        ],
        compiler_params=pltpu.CompilerParams(vmem_limit_bytes=8 * MIB),
        cost_estimate=pl.CostEstimate(flops=0, bytes_accessed=0, transcendentals=0),
        name="attend",
    )(q, own, sib, starts)


def feed_kernel(
    depth, x, gain, next_gain, b0, b1, b2, b3, wo, wg, wu, wd,
    result, normed_next, acts_out, middle_out, slopes_out,
    groups, acts, middle_b, slopes, sems, *own,
):
    if own:
        copies = [
            pltpu.make_async_copy(w.at[depth], buf, sems.at[3 + i]) for i, (w, buf) in enumerate(zip((wo, wd), own))
        ]
        for copy in copies:
            copy.start()
    stores = [
        pltpu.make_async_copy(source, out, sems.at[i])
        for i, (source, out) in enumerate(((acts, acts_out), (middle_b, middle_out), (slopes, slopes_out)))
    ]
    ordered_by_x(here()["x"], (b0, b1, b2, b3), groups)
    mixed = jnp.concatenate([groups[g] for g in range(4)], axis=1)
    acts[:, D : 2 * D] = mixed
    if own:
        copies[0].wait()
    middle = x[...] + mm(mixed, own[0][...] if own else wo[depth])
    middle_b[...] = middle
    stores[1].start()
    normed2 = (middle * norm_factor(middle) * gain[depth : depth + 1, :]).astype(BF)
    acts[:, :D] = normed2
    gate = mm(normed2, wg[depth])
    sigma = 1.0 / (1.0 + jnp.exp(-gate))
    swish = gate * sigma
    up = mm(normed2, wu[depth])
    hidden = (swish * up).astype(BF)
    acts[:, 2 * D :] = hidden
    stores[0].start()
    slopes[:, :FF] = (up * sigma * (1.0 + gate * (1.0 - sigma))).astype(BF)
    slopes[:, FF:] = swish.astype(BF)
    stores[2].start()
    if own:
        copies[1].wait()
    values = middle + mm(hidden, own[1][...] if own else wd[depth])
    if depth == 0:
        result[...] = values
        normed_next[...] = (values * norm_factor(values) * next_gain[1:2, :]).astype(BF)
    else:
        result[...] = values.astype(BF)
        normed_next[...] = jnp.zeros((TOK, D), BF)
    for store in stores:
        store.wait()


def feed(depth, x, gain, next_gain, blocks, wo, wg, wu, wd):
    return pl.pallas_call(
        lambda *refs: feed_kernel(depth, *refs),
        out_shape=[
            sds((TOK, D), BF if depth else F32), sds((TOK, D), BF),
            stored((TOK, 2 * D + FF), BF), stored((TOK, D), F32), stored((TOK, 2 * FF), BF),
        ],
        in_specs=[VMEM] * 7 + [VMEM if depth else HBM, VMEM, VMEM, VMEM if depth else HBM],
        out_specs=[VMEM] * 2 + [HBM] * 3,
        scratch_shapes=[
            pltpu.VMEM((4, TOK, GROUP), BF),
            pltpu.VMEM((TOK, 2 * D + FF), BF),
            pltpu.VMEM((TOK, D), F32),
            pltpu.VMEM((TOK, 2 * FF), BF),
            pltpu.SemaphoreType.DMA((5,)),
        ]
        + ([] if depth else [pltpu.VMEM((D, D), BF), pltpu.VMEM((FF, D), BF)]),
        compiler_params=pltpu.CompilerParams(vmem_limit_bytes=(12 if depth else 16) * MIB),
        cost_estimate=pl.CostEstimate(flops=0, bytes_accessed=0, transcendentals=0),
        name="feed",
    )(x, gain, next_gain, *blocks, *(pinned(wo, wg, wu, wd) if depth else (at_rest(wo), *pinned(wg, wu), at_rest(wd))))


def feed_back_kernel(
    depth, carried, grad, middle, slopes, gain, wd, wg, wu, wo, *refs,
):
    acts = refs[:carried]
    right_ref, dmid_ref, o0, o1, o2, o3, groups, slopes_b, middle_b, sems = refs[carried:]
    width = 2 * FF + 2 * D
    carries = [
        pltpu.make_async_copy(source, right_ref.at[:, pl.ds(width + i * (2 * D + FF), 2 * D + FF)], sems.at[2 + i])
        for i, source in enumerate(acts)
    ]
    stores = [
        pltpu.make_async_copy(source, buf, sems.at[i])
        for i, (source, buf) in enumerate(((slopes, slopes_b), (middle, middle_b)))
    ]
    for store in stores + carries:
        store.start()
    g = grad[...].astype(F32)
    gb = g.astype(BF)
    right_ref[:, 2 * FF : 2 * FF + D] = gb
    dhidden = mm_rt(gb, wd[depth])
    stores[0].wait()
    dgate = (dhidden * slopes_b[:, :FF]).astype(BF)
    dup = (dhidden * slopes_b[:, FF:]).astype(BF)
    right_ref[:, :FF] = dgate
    right_ref[:, FF : 2 * FF] = dup
    dn = mm_rt(dgate, wg[depth]) + mm_rt(dup, wu[depth])
    stores[1].wait()
    mid = middle_b[...]
    factor = norm_factor(mid)
    s = mid * factor
    inner = dn * gain[depth : depth + 1, :]
    dmid = g + factor * (inner - s * jnp.mean(inner * s, axis=-1, keepdims=True))
    dmid_ref[...] = dmid
    dmb = dmid.astype(BF)
    right_ref[:, 2 * FF + D : width] = dmb
    dmixed = mm_rt(dmb, wo[depth]).astype(BF)
    for j in range(4):
        groups[j] = dmixed[:, GROUP * j : GROUP * j + GROUP]
    mine = here()["x"]
    for d, o in enumerate((o0, o1, o2, o3)):
        o[...] = groups[lax.rem(mine + d, 4)]
    for carry in carries:
        carry.wait()


def feed_back(depth, grad, middle, slopes, gain, wd, wg, wu, wo, acts):
    width = 2 * FF + 2 * D + len(acts) * (2 * D + FF)
    return pl.pallas_call(
        lambda *refs: feed_back_kernel(depth, len(acts), *refs),
        out_shape=[sds((TOK, width), BF), sds((TOK, D), F32)] + [sds((TOK, GROUP), BF)] * 4,
        in_specs=[VMEM] + [HBM] * 2 + [VMEM] * 5 + [HBM] * len(acts),
        out_specs=[VMEM] * 6,
        scratch_shapes=[
            pltpu.VMEM((4, TOK, GROUP), BF),
            pltpu.VMEM((TOK, 2 * FF), BF),
            pltpu.VMEM((TOK, D), F32),
            pltpu.SemaphoreType.DMA((4,)),
        ],
        compiler_params=pltpu.CompilerParams(vmem_limit_bytes=12 * MIB),
        cost_estimate=pl.CostEstimate(flops=0, bytes_accessed=0, transcendentals=0),
        name="feed_back",
    )(grad, *map(at_rest, (middle, slopes)), gain, *pinned(wd, wg, wu, wo), *map(at_rest, acts))


def attend_back_kernel(q, kv, starts, lse, b0, b1, b2, b3, dq, own, sib, dout, dk, dv):
    spot = here()
    core, mine = spot["c"], spot["x"]
    for d, b in enumerate((b0, b1, b2, b3)):
        rows = pl.ds(pl.multiple_of(lax.rem(mine - d + 4, 4) * TOK, TOK), TOK)
        dout[rows, :] = b[...]

    def tile(which, pos, first):
        n = 256 * (pos + 1)
        start = starts[which : which + 1, :]
        dqs = []
        for h in range(3):
            lanes = slice(64 * h, 64 * h + 64)
            qs = q[256 * which : 256 * which + 256, lanes] * jnp.asarray(0.125, BF)
            do = dout[256 * which : 256 * which + 256, lanes]
            k = kv[0:n, lanes]
            v = kv[0:n, GROUP + 64 * h : GROUP + 64 * h + 64]
            s = tile_scores(qs, k, start, 256 * pos, n)
            p = jnp.exp(s - lse[3 * which + h : 3 * which + h + 1, :])
            dp = mm_rt(v, do)
            delta = jnp.sum(p * dp, axis=0, keepdims=True)
            ds = (p * (dp - delta)).astype(BF)
            dk_h = mm(ds, qs)
            dv_h = mm(p.astype(BF), do)
            if first:
                dk[0:n, lanes] = dk_h
                dv[0:n, lanes] = dv_h
            else:
                dk[0:n, lanes] += dk_h
                dv[0:n, lanes] += dv_h
            dqs.append(mm_lt(k, ds))
        out = jnp.concatenate(dqs, axis=0).T * 0.125
        dq[256 * which : 256 * which + 256, :] = out

    def put(target, rows, tile_no):
        target[rows : rows + 256, :GROUP] = dk[256 * tile_no : 256 * tile_no + 256, :].astype(target.dtype)
        target[rows : rows + 256, GROUP:] = dv[256 * tile_no : 256 * tile_no + 256, :].astype(target.dtype)

    @pl.when(core == 0)
    def _():
        tile(1, 3, True)
        tile(0, 0, False)
        put(own, 0, 0)
        put(sib, 256, 1)
        put(sib, 0, 2)
        put(own, 256, 3)

    @pl.when(core == 1)
    def _():
        tile(0, 2, True)
        tile(1, 1, False)
        dk[768:1024, :] = jnp.zeros((256, GROUP), F32)
        dv[768:1024, :] = jnp.zeros((256, GROUP), F32)
        put(sib, 0, 0)
        put(own, 256, 1)
        put(own, 0, 2)
        put(sib, 256, 3)


def attend_back(q, kv, starts, lse, blocks):
    return pl.pallas_call(
        attend_back_kernel,
        out_shape=[sds((4 * TOK, GROUP), F32), sds((4 * TOK, 2 * GROUP), F32), sds((4 * TOK, 2 * GROUP), BF)],
        in_specs=[VMEM] * 8,
        out_specs=[VMEM] * 3,
        scratch_shapes=[
            pltpu.VMEM((4 * TOK, GROUP), BF),
            pltpu.VMEM((ROW, GROUP), F32),
            pltpu.VMEM((ROW, GROUP), F32),
        ],
        compiler_params=pltpu.CompilerParams(vmem_limit_bytes=10 * MIB),
        cost_estimate=pl.CostEstimate(flops=0, bytes_accessed=0, transcendentals=0),
        name="attend_back",
    )(q, kv, starts, lse, *blocks)


def spread_kernel(depth, dq, own, got, cos, sin, w, right, *refs):
    right[:, : GROUP] = turn_group(own[:, :GROUP] + got[:, :GROUP].astype(F32), cos[...], -sin[...]).astype(BF)
    right[:, GROUP : 2 * GROUP] = (own[:, GROUP:] + got[:, GROUP:].astype(F32)).astype(BF)
    right[:, 2 * GROUP : 3 * GROUP] = turn_group(dq[...], cos[...], -sin[...]).astype(BF)
    right[:, 3 * GROUP :] = jnp.zeros((4 * TOK, 64), BF)
    da = mm_rt(right[:, : 3 * GROUP], w[depth]).astype(BF)
    spot = here()
    if depth == 1:
        groups = refs[-1]
        groups[...] = da.reshape(4, TOK, D)
        for d, o in enumerate(refs[:4]):
            o[...] = groups[lax.rem(spot["x"] + d, 4)]
    else:
        (stack,) = refs
        for x in range(4):
            rank = rank_of(1 - spot["c"], x)
            for t in range(6):
                rows = pl.ds(pl.multiple_of((4 * t + rank) * TOK, TOK), TOK)
                stack[rows, :] = da[TOK * x : TOK * x + TOK, TOK * t : TOK * t + TOK]


def spread(depth, dq, own, got, cos, sin, w):
    shapes = [sds((TOK, D), BF)] * 4 if depth == 1 else [sds((6 * 4 * TOK, TOK), BF)]
    right, *blocks = pl.pallas_call(
        lambda *refs: spread_kernel(depth, *refs),
        out_shape=[sds((4 * TOK, 3 * GROUP + 64), BF)] + shapes,
        in_specs=[VMEM] * 6,
        out_specs=[VMEM] * (1 + len(shapes)),
        scratch_shapes=[pltpu.VMEM((4, TOK, D), BF)] if depth == 1 else [],
        compiler_params=pltpu.CompilerParams(vmem_limit_bytes=8 * MIB),
        cost_estimate=pl.CostEstimate(flops=0, bytes_accessed=0, transcendentals=0),
        name="spread",
    )(dq, own, got, cos, sin, w)
    return right, blocks


def norm_back(da, dmid, x, gain):
    factor = norm_factor(x)
    s = x * factor
    inner = da * gain
    return dmid + factor * (inner - s * jnp.mean(inner * s, axis=-1, keepdims=True))


def project_back_kernel(dmid, x, gain, b0, b1, b2, b3, grad):
    da = b0[...].astype(F32) + b1[...].astype(F32) + b2[...].astype(F32) + b3[...].astype(F32)
    grad[...] = norm_back(da, dmid[...], x[...], gain[1:2, :])


def project_back(dmid, x, gain, blocks):
    return pl.pallas_call(
        project_back_kernel,
        out_shape=sds((TOK, D), F32),
        in_specs=[VMEM] * 7,
        out_specs=VMEM,
        compiler_params=pltpu.CompilerParams(vmem_limit_bytes=6 * MIB),
        cost_estimate=pl.CostEstimate(flops=0, bytes_accessed=0, transcendentals=0),
        name="project_back",
    )(dmid, x, gain, *blocks)


def last_grad_kernel(offset, kept, got, dmid, x, gain, activations, back):
    parts = []
    for t in range(6):
        rows = slice(TOK * t, TOK * t + TOK)
        parts.append(kept[rows, :].astype(F32) + got[offset + TOK * t : offset + TOK * t + TOK, :].astype(F32))
    da = jnp.concatenate(parts, axis=1)
    back[:TOK, :] = norm_back(da, dmid[...], x[...], gain[0:1, :]).astype(BF)
    back[TOK:, :] = activations[...]


def last_grad(member, dmid, x, gain, activations):
    return pl.pallas_call(
        lambda *refs: last_grad_kernel(member.offset, *refs),
        out_shape=sds((2 * TOK, D), BF),
        in_specs=[VMEM] * 6,
        out_specs=VMEM,
        compiler_params=pltpu.CompilerParams(vmem_limit_bytes=6 * MIB),
        cost_estimate=pl.CostEstimate(flops=0, bytes_accessed=0, transcendentals=0),
        name="last_grad",
    )(member.kept, member.got, dmid, x, gain, activations)


def exchange_x(blocks):
    return (blocks[0],) + tuple(send(blocks[d], SHIFT_X[d]) for d in (1, 2, 3))


def left_kernel(jobs, right, right_sib, both, turned):
    mine = here()["c"]
    row = 0
    for first, columns, axes, swapped in jobs:
        hot = one_hot(axes, mine, swapped) if columns == D else None
        for side, source in enumerate((right, right_sib)):
            lanes = slice(TOK * side, TOK * side + TOK)
            if hot is None:
                turned[...] = source[:, first : first + FF].T.reshape(FF // 16, 16, TOK)
                half = block_order(axes, swapped).reshape(2, 64)
                for i in range(64):
                    block = jnp.where(mine == 0, int(half[0, i]), int(half[1, i]))
                    both[row + 16 * i : row + 16 * i + 16, lanes] = turned[block]
            else:
                both[row : row + D // 2, lanes] = mm_rt(hot, source[:, first : first + D]).astype(BF)
        row += columns // 2


def left_sides(right, right_sib, jobs):
    rows = sum(columns // 2 for _, columns, _, _ in jobs)
    return pl.pallas_call(
        lambda *refs: left_kernel(jobs, *refs),
        out_shape=sds((rows, 2 * TOK), BF),
        in_specs=[VMEM] * 2,
        out_specs=VMEM,
        scratch_shapes=[pltpu.VMEM((FF // 16, 16, TOK), BF)],
        compiler_params=pltpu.CompilerParams(vmem_limit_bytes=8 * MIB),
        cost_estimate=pl.CostEstimate(flops=0, bytes_accessed=0, transcendentals=0),
        name="left_sides",
    )(right, right_sib)


def along_kernel(rows, along):
    normed = rows[...].reshape(4 * TOK, D)
    for side in range(2):
        along[D // 2 * side : D // 2 * side + D // 2, :] = mm_rt(one_hot("yzx", side, "yz"), normed).astype(BF)


def left_along(rows):
    return pl.pallas_call(
        along_kernel,
        out_shape=stored((D, 4 * TOK), BF),
        in_specs=[VMEM],
        out_specs=VMEM,
        compiler_params=pltpu.CompilerParams(vmem_limit_bytes=8 * MIB),
        cost_estimate=pl.CostEstimate(flops=0, bytes_accessed=0, transcendentals=0),
        name="left_along",
    )(at_rest(rows))


def rows_kernel(wq, wk, wv, wg, wu, na, nf, rq, rk, rv, rg, ru, gains, bq, bk, bv, bg, bu, sems):
    first = here()["flat"] * 6
    start = pl.multiple_of(jnp.minimum((first >> 4) << 4, D - 32), 16)
    copies = [
        pltpu.make_async_copy(w.at[:, pl.ds(start, 32), :], buf, sems.at[i])
        for i, (w, buf) in enumerate(((wq, bq), (wk, bk), (wv, bv), (wg, bg), (wu, bu)))
    ]
    for copy in copies:
        copy.start()
    lane = lax.broadcasted_iota(jnp.int32, (8, D), 1)
    pick = lane == lax.broadcasted_iota(jnp.int32, (8, D), 0) + first
    column = lax.broadcasted_iota(jnp.int32, (8, TOK), 1)
    result = jnp.ones((8, TOK), F32)
    for i, row in enumerate((na[0:1, :], na[1:2, :], nf[0:1, :], nf[1:2, :])):
        value = jnp.sum(jnp.where(pick, row, 0.0), axis=1, keepdims=True)
        result = jnp.where(column == i, value, result)
    gains[...] = result
    place = lax.broadcasted_iota(jnp.int32, (8, 32), 1)
    hot = jnp.where(place == lax.broadcasted_iota(jnp.int32, (8, 32), 0) + (first - start), 1.0, 0.0).astype(BF)
    for copy, buf, out in zip(copies, (bq, bk, bv, bg, bu), (rq, rk, rv, rg, ru)):
        copy.wait()
        for layer in range(2):
            out[layer] = mm(hot, buf[layer])


def own_rows(wq, wk, wv, wg, wu, na, nf):
    return pl.pallas_call(
        rows_kernel,
        out_shape=[stored((2, 8, D), F32)] * 3 + [stored((2, 8, FF), F32)] * 2 + [stored((8, TOK), F32)],
        in_specs=[HBM] * 5 + [VMEM] * 2,
        out_specs=[VMEM] * 6,
        scratch_shapes=[pltpu.VMEM((2, 32, D), BF)] * 3
        + [pltpu.VMEM((2, 32, FF), BF)] * 2
        + [pltpu.SemaphoreType.DMA((5,))],
        compiler_params=pltpu.CompilerParams(vmem_limit_bytes=6 * MIB),
        cost_estimate=pl.CostEstimate(flops=0, bytes_accessed=0, transcendentals=0),
        name="own_rows",
    )(*map(at_rest, (wq, wk, wv, wg, wu)), na, nf)


def slot(rows):
    return -(-rows // 16) * 16


class Member:
    def __init__(self, kept, rows, tiles, offset):
        self.kept, self.rows, self.tiles, self.offset = kept, rows, tiles, offset
        self.got = None


def for_tiles(tiles, body):
    if tiles <= 6:
        for t in range(tiles):
            body(t)
    else:
        @pl.loop(0, tiles // 2)
        def _(i):
            body(2 * i)
            body(2 * i + 1)


def aligned(value):
    return value if isinstance(value, int) else pl.multiple_of(value, 16)


def bit_of(spot, which):
    if which == "c":
        return spot["c"]
    axis, step = which[0], which[1]
    rank = rank_of(1 - spot["c"] if len(which) > 2 else spot["c"], spot[axis])
    return rank // 2 if step == 0 else lax.rem(rank, 2)


def sums_kernel(tasks, *refs):
    spot = here()
    for task in tasks:
        kind, bit = task["kind"], bit_of(spot, task["bit"])
        pack, offset, kept_ref = refs[task["pack"]], task["offset"], refs[task["kept"]]
        half, tiles = task["half"], task["tiles"]
        out_slot = slot(half)
        if kind == "weights":
            left, right, right_sib = (refs[i] for i in task["ins"])
            lhs = jnp.concatenate(
                [left[pl.ds(pl.multiple_of(task["row"] + side * half, 64), half), :] for side in (1 - bit, bit)], axis=0
            )
            for t in range(0, tiles, 2):
                col = task["column"] + TOK * t
                rhs = jnp.concatenate([right[:, col : col + 2 * TOK], right_sib[:, col : col + 2 * TOK]], axis=0)
                part = mm(lhs, rhs).astype(BF)
                for out, base, rows in ((pack, offset, part[:half]), (kept_ref, 0, part[half:])):
                    out[base + t * half : base + (t + 1) * half, :] = rows[:, :TOK]
                    out[base + (t + 1) * half : base + (t + 2) * half, :] = rows[:, TOK:]
        elif kind == "along":
            left, right = (refs[i] for i in task["ins"])
            lhs = jnp.concatenate(
                [left[pl.ds(pl.multiple_of(side * half, 64), half), :] for side in (1 - bit, bit)], axis=0
            )
            part = mm(lhs, right[...]).astype(BF)
            for out, base, rows in ((pack, offset, part[:half]), (kept_ref, 0, part[half:])):
                for t in range(tiles):
                    out[base + t * half : base + (t + 1) * half, :] = rows[:, TOK * t : TOK * t + TOK]
        elif kind == "first":
            value, base, in_slot = refs[task["ins"][0]], task["came"], slot(2 * half)
            for t in range(tiles):
                at = base + t * in_slot
                if half % 16 == 0:
                    pack[offset + t * out_slot : offset + t * out_slot + half, :] = value[
                        pl.ds(pl.multiple_of(at + (1 - bit) * half, 16), half), :
                    ]
                    kept_ref[t * out_slot : t * out_slot + half, :] = value[
                        pl.ds(pl.multiple_of(at + bit * half, 16), half), :
                    ]
                else:
                    both = value[at : at + 2 * half, :].astype(F32)
                    low, high = both[:half], both[half:]
                    pack[offset + t * out_slot : offset + t * out_slot + half, :] = jnp.where(bit == 0, high, low).astype(BF)
                    kept_ref[t * out_slot : t * out_slot + half, :] = jnp.where(bit == 0, low, high).astype(BF)
        else:
            value, got = (refs[i] for i in task["ins"])
            came, in_slot = task["came"], slot(2 * half)

            def one(t, half=half, out_slot=out_slot, in_slot=in_slot, came=came, offset=offset, bit=bit,
                    value=value, got=got, pack=pack, kept_ref=kept_ref):
                if half % 16 == 0:
                    for out, base, side in ((pack, offset, 1 - bit), (kept_ref, 0, bit)):
                        at = t * in_slot + side * half
                        total = (
                            value[pl.ds(pl.multiple_of(at, 16), half), :].astype(F32)
                            + got[pl.ds(pl.multiple_of(came + at, 16), half), :].astype(F32)
                        )
                        out[pl.ds(aligned(base + t * out_slot), half), :] = total.astype(BF)
                else:
                    total = (
                        value[pl.ds(aligned(t * in_slot), 2 * half), :].astype(F32)
                        + got[pl.ds(aligned(came + t * in_slot), 2 * half), :].astype(F32)
                    )
                    low, high = total[:half], total[half:]
                    pack[pl.ds(aligned(offset + t * out_slot), half), :] = jnp.where(bit == 0, high, low).astype(BF)
                    kept_ref[pl.ds(aligned(t * out_slot), half), :] = jnp.where(bit == 0, low, high).astype(BF)

            for_tiles(tiles, one)


def sums(jobs):
    arrays, tasks, pack_rows = [], [], {}

    def at(array):
        for i, a in enumerate(arrays):
            if a is array:
                return i
        arrays.append(array)
        return len(arrays) - 1

    flops = 0
    for job in jobs:
        if job[0] == "weights":
            _, left, row, rows, right, right_sib, column, columns, bit, pack = job
            task = dict(kind="weights", ins=[at(left), at(right), at(right_sib)], row=row, column=column,
                        half=rows // 2, tiles=columns // TOK, bit=bit)
            flops += 4 * rows * columns * TOK
        elif job[0] == "along":
            _, left, right, pack = job
            task = dict(kind="along", ins=[at(left), at(right)], half=D // 2, tiles=right.shape[1] // TOK, bit="c")
            flops += 2 * D * right.shape[1] * 4 * TOK
        elif job[0] == "first":
            _, array, base, rows, tiles, bit, pack = job
            task = dict(kind="first", ins=[at(array)], came=base, half=rows // 2, tiles=tiles, bit=bit)
        else:
            _, member, bit, pack = job
            task = dict(kind="step", ins=[at(member.kept), at(member.got)], came=member.offset,
                        half=member.rows // 2, tiles=member.tiles, bit=bit)
        task["pack"], task["offset"] = pack, pack_rows.get(pack, 0)
        pack_rows[pack] = task["offset"] + task["tiles"] * slot(task["half"])
        tasks.append(task)
    names = sorted(pack_rows)
    shapes = [sds((pack_rows[n], TOK), BF) for n in names]
    for i, task in enumerate(tasks):
        task["kept"] = len(arrays) + len(names) + i
        task["pack"] = len(arrays) + names.index(task["pack"])
        shapes.append(sds((task["tiles"] * slot(task["half"]), TOK), BF))
    moved = sum(a.size for a in arrays) + sum(np.prod(s.shape) for s in shapes)
    outs = pl.pallas_call(
        lambda *refs: sums_kernel(tasks, *refs),
        out_shape=shapes,
        in_specs=[VMEM] * len(arrays),
        out_specs=[VMEM] * len(shapes),
        compiler_params=pltpu.CompilerParams(vmem_limit_bytes=10 * MIB),
        cost_estimate=pl.CostEstimate(flops=0, bytes_accessed=0, transcendentals=0),
        name="sums",
    )(*arrays)
    packs = dict(zip(names, outs))
    members = [
        Member(kept, task["half"], task["tiles"], task["offset"]) for kept, task in zip(outs[len(names) :], tasks)
    ]
    return packs, members


def came(members, got):
    for member in members:
        member.got = got


def finish_kernel(plan, places, *refs):
    back, arrays = refs[6], refs[7:-19]
    acts, gtok, gq, gk, gv, go, ggate, gup, gdown, gattn, gffn, by_x = refs[-19:-7]
    wq, wk, wv, wg, wu, gains = refs[-7:-1]
    copies = [
        pltpu.make_async_copy(source, buf, refs[-1].at[i]) for i, (source, buf) in enumerate(zip(refs[:6], refs[-7:-1]))
    ]
    for copy in copies:
        copy.start()
    gtok[...] = back[:TOK, :].astype(F32)
    acts[...] = back[TOK:, :]
    spot = here()
    mine = spot["x"]
    across, beside = 3 - mine, mine + 1 - 2 * lax.rem(mine, 2)
    first = jnp.where(spot["c"] == 0, beside, across)
    second = jnp.where(spot["c"] == 0, across, beside)
    opposite = lax.rem(mine + 2, 4)
    for m in range(2):
        (kept, got, offset), (kept_b, got_b, offset_b) = places[m]
        for group, array, base in (
            (mine, kept, 0), (first, kept_b, 0), (second, got, offset), (opposite, got_b, offset_b)
        ):
            by_x[4 * m + group] = arrays[array][base : base + 80, :]

    def total(name):
        kept, got, offset, tiles, rows = plan[name]
        parts = []
        for t in range(tiles):
            parts.append(
                arrays[kept][16 * t : 16 * t + rows, :].astype(F32)
                + arrays[got][offset + 16 * t : offset + 16 * t + rows, :].astype(F32)
            )
        return jnp.concatenate(parts, axis=1)

    lane = lax.broadcasted_iota(jnp.int32, (8, TOK), 1)
    result = jnp.zeros((8, TOK), F32)
    filler = jnp.zeros((2, 1), F32)
    both = jnp.concatenate([total("gate0"), total("up0")], axis=1), total("gu1")
    gates = [b[:, :FF] for b in both]
    ups = [b[:, FF:] for b in both]
    for layer in range(2):
        ggate[:, layer, :] = gates[layer]
        gup[:, layer, :] = ups[layer]
        go[:, layer, :] = total(f"out{layer}")
        gdown[layer] = total(f"down{layer}")
    for copy in copies:
        copy.wait()
    for layer in range(2):
        m = 1 - layer
        rows = [
            jnp.concatenate([by_x[4 * m + x, 16 * t : 16 * t + 6, :] for t in range(5)], axis=1) for x in range(4)
        ]
        acc = jnp.zeros((6, 1), F32)
        for i, (out, w) in enumerate(((gk, wk), (gv, wv), (gq, wq))):
            value = jnp.concatenate([r[:, GROUP * i : GROUP * i + GROUP] for r in rows], axis=1).astype(F32)
            out[:, layer, :] = value
            acc = acc + jnp.sum(value * w[layer][:6], axis=1, keepdims=True)
        result = jnp.where(lane == layer, jnp.concatenate([acc / gains[:6, layer : layer + 1], filler], axis=0), result)
        gate, up = gates[layer], ups[layer]
        acc = jnp.sum(gate * wg[layer][:6], axis=1, keepdims=True) + jnp.sum(
            up * wu[layer][:6], axis=1, keepdims=True
        )
        result = jnp.where(lane == 2 + layer, jnp.concatenate([acc / gains[:6, 2 + layer : 3 + layer], filler], axis=0), result)
    turned = result.T
    gattn[...] = turned[0:2, :6]
    gffn[...] = turned[2:4, :6]


def finish(rows_of, back, members, projections):
    arrays, plan = [], {}

    def at(array):
        for i, a in enumerate(arrays):
            if a is array:
                return i
        arrays.append(array)
        return len(arrays) - 1

    for name, m in members.items():
        plan[name] = (at(m.kept), at(m.got), m.offset, m.tiles, m.rows)
    places = [[(at(m.kept), at(m.got), m.offset) for m in pair] for pair in projections]
    return pl.pallas_call(
        lambda *refs: finish_kernel(plan, places, *refs),
        out_shape=[sds((TOK, D), BF), sds((TOK, D), F32)]
        + [sds((6, 2, D), F32)] * 4
        + [sds((6, 2, FF), F32)] * 2
        + [sds((2, 16, D), F32), sds((2, 6), F32), sds((2, 6), F32)],
        in_specs=[HBM] * 6 + [VMEM] * (1 + len(arrays)),
        out_specs=[VMEM] * 11,
        scratch_shapes=[pltpu.VMEM((8, 80, TOK), BF)]
        + [pltpu.VMEM((2, 8, D), F32)] * 3
        + [pltpu.VMEM((2, 8, FF), F32)] * 2
        + [pltpu.VMEM((8, TOK), F32), pltpu.SemaphoreType.DMA((6,))],
        compiler_params=pltpu.CompilerParams(vmem_limit_bytes=8 * MIB),
        cost_estimate=pl.CostEstimate(flops=0, bytes_accessed=0, transcendentals=0),
        name="finish",
    )(*map(at_rest, rows_of), back, *arrays)


def tie(value, *others):
    return lax.optimization_barrier((value,) + others)[0]


def per_device(
    tokens, seg_lengths, cotangent, norm_attn, w_query, w_key, w_value, w_out, norm_ffn, w_gate, w_up, w_down
):
    with jax.named_scope("S_setup"):
        _, early = first_norm(tokens[0], norm_attn, True)
        first_blocks = [send(early, GATHER[d]) for d in (1, 2, 3)]
        moved = send(tokens[0], RELOCATE)
        lengths = send(seg_lengths[0], RELOCATE)
        cot = send(cotangent[0], RELOCATE)
        x, normed = first_norm(moved, norm_attn)
        heads = own_heads(w_query, w_key, w_value)
        cos, sin, starts = tables(lengths)

    kept, carried, alongs = [], [], []
    for depth in range(2):
        with jax.named_scope(f"S_ahead{depth}"):
            blocks = exchange_x([normed] * 4) if depth else (normed, *first_blocks)
            if depth == 1:
                alongs.append(left_along(rows))
                cot = tie(cot, alongs[0])
                rows_of = own_rows(w_query, w_key, w_value, w_gate, w_up, norm_attn, norm_ffn)
                blocks = (tie(blocks[0], cot, *rows_of),) + tuple(blocks[1:])
            q, own, rows = project(depth, blocks, heads, cos, sin)
            sib = send(own, CORE)
            *blocks, q, kv, lse = attend(q, own, sib, starts)
            blocks = exchange_x(blocks)
            if depth == 1:
                alongs.append(left_along(rows))
                blocks = (tie(blocks[0], alongs[1]),) + tuple(blocks[1:])
            result, normed, acts, middle, slopes = feed(
                depth, x, norm_ffn, norm_attn, blocks, w_out, w_gate, w_up, w_down
            )
            kept.append((x, q, kv, lse, middle, slopes))
            carried.append(acts)
            x = result
    activations = x

    def step(members, bit, pack):
        return [("step", m, bit, pack) for m in members]

    half = D // 2
    x, q, kv, lse, middle, slopes = kept[1]
    with jax.named_scope("S_back1"):
        right, dmid, *blocks = feed_back(
            1, cot, middle, slopes, norm_ffn, w_down, w_gate, w_up, w_out, [carried[1], carried[0]]
        )
        blocks = exchange_x(blocks)
        right_sib = send(right, CORE)
    base1 = 2 * FF + 2 * D
    base0 = base1 + 2 * D + FF
    with jax.named_scope("S_back1"):
        left = left_sides(right, right_sib, [(base1, D, "yzx", "yz")])
        blocks = (tie(blocks[0], left),) + tuple(blocks[1:])
        dq, own, sib = attend_back(q, kv, starts, lse, blocks)
        right1, blocks = spread(1, dq, own, send(sib, CORE), cos, sin, heads)
        blocks = exchange_x(blocks)
    with jax.named_scope("S_sum1"):
        packs, (gu1,) = sums([("weights", left, 0, D // 2, tie(right, right1), right_sib, 0, 2 * FF, ("y", 0, "swapped"), "y")])
        came([gu1], send(packs["y"], PAIR["y", 1]))
        left = left_sides(
            right, right_sib,
            [
                (base0, D, "xzy", ""),
                (base0, D, "yzx", ""),
                (base0 + D, D, "xzy", ""),
                (base0 + 2 * D, FF, "zyx", ""),
                (base1 + D, D, "xzy", ""),
                (base1 + 2 * D, FF, "zyx", ""),
            ],
        )
        late, late_sib = right, right_sib
    with jax.named_scope("S_back1"):
        blocks = (tie(blocks[0], packs["y"]),) + tuple(blocks[1:])
        grad = project_back(dmid, x, norm_attn, blocks)

    x, q, kv, lse, middle, slopes = kept[0]
    with jax.named_scope("S_back0"):
        right, dmid, *blocks = feed_back(0, grad, middle, slopes, norm_ffn, w_down, w_gate, w_up, w_out, [])
        blocks = exchange_x(blocks)
        right_sib = send(right, CORE)
    with jax.named_scope("S_sum0"):
        packs, (gate0, up0, out0, down0, out1, down1, gu1) = sums(
            [
                ("weights", left, 0, D // 2, tie(right, *blocks), right_sib, 0, ALONG_X, ("x", 0), "x"),
                ("weights", left, half, D // 2, right, right_sib, ALONG_X, 2 * FF - ALONG_X, ("y", 0), "y"),
                ("weights", left, 2 * half, D // 2, right, right_sib, 2 * FF + D, D, ("x", 0), "x"),
                ("weights", left, 3 * half, FF // 2, right, right_sib, 2 * FF, D, ("z", 0), "z"),
                ("weights", left, 3 * half + FF // 2, D // 2, late, late_sib, 2 * FF + D, D, ("x", 0), "x"),
                ("weights", left, 4 * half + FF // 2, FF // 2, late, late_sib, 2 * FF, D, ("z", 0), "z"),
            ]
            + step([gu1], ("y", 1, "swapped"), "y")
        )
        came([gate0, out0, out1], send(packs["x"], PAIR["x", 0]))
        came([up0, gu1], send(packs["y"], PAIR["y", 0]))
        came([down0, down1], send(packs["z"], PAIR["z", 0]))
    with jax.named_scope("S_back0"):
        blocks = (tie(blocks[0], packs["x"], packs["y"], packs["z"]),) + tuple(blocks[1:])
        dq, own, sib = attend_back(q, kv, starts, lse, blocks)
        right0, (partial,) = spread(0, dq, own, send(sib, CORE), cos, sin, heads)

    with jax.named_scope("S_sum0"):
        packs, (qkv1, qkv0) = sums([("along", alongs[1], right1, "c"), ("along", alongs[0], right0, "c")])
        came([qkv1, qkv0], send(packs["c"], CORE))
        packs, (gate0, out0, out1, up0, down0, down1, gu1, qkv1, qkv0, da) = sums(
            step([gate0, out0, out1], ("x", 1), "x")
            + step([up0], ("y", 1), "y")
            + step([down0, down1], ("z", 1), "z")
            + step([gu1], ("z", 0, "swapped"), "z")
            + step([qkv1, qkv0], ("y", 0, "swapped"), "y")
            + [("first", partial, 0, 4 * TOK, 6, ("x", 0, "swapped"), "x")],
        )
        came([down0, down1, gu1], send(packs["z"], PAIR["z", 1]))
        came([gate0, out0, out1, da], send(packs["x"], PAIR["x", 1]))
        came([up0, qkv1, qkv0], send(packs["y"], PAIR["y", 1]))
        packs, (down0, down1, gate0, out0, out1, up0, gu1, qkv1, qkv0, da) = sums(
            step([down0, down1], ("y", 0), "y")
            + step([gate0, out0, out1, up0], ("z", 0), "z")
            + step([gu1], ("z", 1, "swapped"), "z")
            + step([qkv1, qkv0], ("y", 1, "swapped"), "y")
            + step([da], ("x", 1, "swapped"), "x"),
        )
        came([gate0, out0, out1, up0, gu1], send(packs["z"], PAIR["z", 0]))
        came([down0, down1, qkv1, qkv0], send(packs["y"], PAIR["y", 0]))
        came([da], send(packs["x"], PAIR["x", 0]))
        back = send(last_grad(da, dmid, x, norm_attn, activations), RESTORE)
        packs, (down0, down1, gate0, out0, out1, up0, qkv1, qkv0) = sums(
            step([down0, down1], ("y", 1), "y")
            + step([gate0, out0, out1, up0], ("z", 1), "z")
            + step([qkv1, qkv0], ("z", 0, "swapped"), "z"),
        )
        came([gate0, out0, out1, up0, qkv1, qkv0], send(packs["z"], PAIR["z", 1]))
        came([down0, down1], send(packs["y"], PAIR["y", 1]))
        packs, (gate0, out0, out1, qkv1, qkv0) = sums(
            step([gate0, out0, out1], ("y", 0), "y") + step([qkv1, qkv0], ("z", 1, "swapped"), "z")
        )
        came([gate0, out0, out1], send(packs["y"], PAIR["y", 0]))
        came([qkv1, qkv0], send(packs["z"], PAIR["z", 0]))
        packs, (gate0, out0, out1, up0, down0, down1, gu1, qkv1, qkv0) = sums(
            step([gate0, out0, out1], ("y", 1), "y")
            + step([up0, down0, down1, gu1, qkv1, qkv0], ("x", 0), "x"),
        )
        came([up0, down0, down1, gu1, qkv1, qkv0], send(packs["x"], PAIR["x", 0]))
        came([gate0, out0, out1], send(packs["y"], PAIR["y", 1]))
        gu1.kept = tie(gu1.kept, back)
        packs, (up0, down0, down1, gu1, mine1, first1, mine0, first0) = sums(
            step([up0, down0, down1, gu1], ("x", 1), "x")
            + [
                ("first", array, offset, 12, 5, ("x", 1), "x")
                for m in (qkv1, qkv0)
                for array, offset in ((m.kept, 0), (m.got, m.offset))
            ],
        )
        came([up0, down0, down1, gu1, mine1, first1, mine0, first0], send(packs["x"], PAIR["x", 1]))
        activations, grad_tokens, grad_q, grad_k, grad_v, grad_o, grad_gate, grad_up, grad_down, grad_attn, grad_ffn = finish(
            rows_of, back,
            dict(gate0=gate0, up0=up0, gu1=gu1, out0=out0, out1=out1, down0=down0, down1=down1),
            [(mine1, first1), (mine0, first0)],
        )
    return (
        activations[None],
        grad_tokens[None],
        grad_attn,
        jnp.swapaxes(grad_q, 0, 1),
        jnp.swapaxes(grad_k, 0, 1),
        jnp.swapaxes(grad_v, 0, 1),
        jnp.swapaxes(grad_o, 0, 1),
        grad_ffn,
        jnp.swapaxes(grad_gate, 0, 1),
        jnp.swapaxes(grad_up, 0, 1),
        grad_down,
    )


def solution(mesh):
    rows = P("batch", "seq", None)
    split = P(None, AXES)
    split3 = P(None, AXES, None)
    return jax.shard_map(
        per_device,
        mesh=mesh,
        in_specs=(rows, P("batch", None), rows) + (P(),) * 9,
        out_specs=(rows, rows, split, split3, split3, split3, split3, split, split3, split3, split3),
        check_vma=False,
    )
```

```python
import jax
import jax.numpy as jnp
import numpy as np
from jax import lax
from jax.experimental import pallas as pl
from jax.experimental.pallas import tpu as pltpu
from jax.sharding import PartitionSpec as P

D = 768
HEADS = 12
HEAD_DIM = 64
FF = 2048
ALONG_X = FF + 256
TOK = 128
ROW = 1024
GRID = 16
GROUP = 3 * HEAD_DIM
OFF = {"k": 0, "v": GROUP, "q": 2 * GROUP}
EPS = 1e-05
AXES = ("seq", "batch")
BF = jnp.bfloat16
F32 = jnp.float32
MIB = 1 << 20


def place(flat):
    seq, batch = divmod(flat, 16)
    z_lo, x = divmod(seq, 4)
    y, rest = divmod(batch, 4)
    z_hi, core = divmod(rest, 2)
    return dict(x=x, y=y, z=z_hi * 2 + z_lo, c=core)


def flat_of(p):
    z_hi, z_lo = divmod(p["z"], 2)
    return (z_lo * 4 + p["x"]) * 16 + p["y"] * 4 + z_hi * 2 + p["c"]


def permutation(move):
    pairs = []
    for flat in range(128):
        p = place(flat)
        move(p)
        pairs.append((flat, flat_of(p)))
    return pairs


def move_relocate(p):
    z_hi, z_lo = divmod(p["z"], 2)
    core = p["c"]
    p["z"] = z_hi * 2 + core
    p["c"] = z_lo ^ (1 if p["x"] >= 2 else 0)


RELOCATE = permutation(move_relocate)
RESTORE = sorted((dst, src) for src, dst in RELOCATE)


def move_core(p):
    p["c"] ^= 1


CORE = permutation(move_core)


def shift_x(by):
    def move(p):
        p["x"] = (p["x"] + by) % 4

    return permutation(move)


SHIFT_X = {d: shift_x(d) for d in (1, 2, 3)}


def pair_step(axis, step):
    def move(p):
        at = p[axis]
        p[axis] = at ^ 1 if (p["c"] == 0) == (step == 0) else 3 - at

    return permutation(move)


PAIR = {(axis, step): pair_step(axis, step) for axis in "xyz" for step in (0, 1)}


def relocate_and_shift(by):
    def move(p):
        move_relocate(p)
        p["x"] = (p["x"] + by) % 4

    return permutation(move)


GATHER = {d: relocate_and_shift(d) for d in (1, 2, 3)}


def send(value, pairs):
    return lax.ppermute(value, AXES, pairs)


RING_ORDER = {0: (0, 3, 1, 2), 1: (0, 1, 2, 3)}


def block_order(axes, swapped=""):
    order = []
    for core in (0, 1):
        first, second, third = (RING_ORDER[1 - core if axis in swapped else core] for axis in axes)
        for a in first:
            for b in second:
                for c in third:
                    order.append(flat_of({axes[0]: a, axes[1]: b, axes[2]: c, "c": core}))
    return np.array(order)


def one_hot(axes, core, swapped=""):
    row = lax.broadcasted_iota(jnp.int32, (D // 2, 1), 0)
    block = (row * 10923) >> 16
    within = row - 6 * block
    places = {}
    for i, axis in enumerate(axes):
        at = (block >> (4 - 2 * i)) & 3
        ring = jnp.where(at == 0, 0, jnp.where(at == 1, 3, at - 1))
        places[axis] = jnp.where(core == (1 if axis in swapped else 0), ring, at)
    z = places["z"]
    flat = ((z & 1) * 4 + places["x"]) * 16 + places["y"] * 4 + (z >> 1) * 2 + core
    lane = lax.broadcasted_iota(jnp.int32, (D // 2, D), 1)
    return jnp.where(lane == flat * 6 + within, 1.0, 0.0).astype(BF)


def mm(left, right):
    return jnp.dot(left, right, preferred_element_type=F32)


def mm_rt(left, right):
    return lax.dot_general(left, right, (((1,), (1,)), ((), ())), preferred_element_type=F32)


def mm_lt(left, right):
    return lax.dot_general(left, right, (((0,), (0,)), ((), ())), preferred_element_type=F32)


VMEM = pl.BlockSpec(memory_space=pltpu.VMEM)
SMEM = pl.BlockSpec(memory_space=pltpu.SMEM)
HBM = pl.BlockSpec(memory_space=pltpu.HBM)


def pinned(*weights):
    return tuple(pltpu.with_memory_space_constraint(w, pltpu.VMEM) for w in weights)


def at_rest(value):
    return pltpu.with_memory_space_constraint(value, pltpu.HBM)


def stored(shape, kind):
    return pltpu.HBM(shape, kind)


def sds(shape, kind):
    return jax.ShapeDtypeStruct(shape, kind)


def here():
    seq, batch = lax.axis_index("seq"), lax.axis_index("batch")
    return dict(
        x=lax.rem(seq, 4), y=batch // 4, z=lax.rem(batch // 2, 2) * 2 + seq // 4, c=lax.rem(batch, 2), flat=seq * 16 + batch
    )


def rank_of(core, at):
    return jnp.where(core == 0, jnp.where(at == 0, 0, jnp.where(at == 3, 1, at + 1)), at)


def ordered_by_x(mine, blocks, out):
    for d, b in enumerate(blocks):
        out[lax.rem(mine - d + 4, 4)] = b[...]


def norm_factor(values):
    return lax.rsqrt(jnp.mean(values * values, axis=-1, keepdims=True) + EPS)


def first_norm_kernel(tokens, gain, x, normed):
    values = tokens[...].astype(F32)
    x[...] = values
    normed[...] = (values * norm_factor(values) * gain[0:1, :]).astype(BF)


def first_norm(tokens, gain, first=False):
    return pl.pallas_call(
        first_norm_kernel,
        out_shape=[sds((TOK, D), F32), sds((TOK, D), BF)],
        in_specs=[VMEM] * 2,
        out_specs=[VMEM] * 2,
        compiler_params=pltpu.CompilerParams(vmem_limit_bytes=4 * MIB),
        cost_estimate=pl.CostEstimate(flops=0, bytes_accessed=0, transcendentals=0),
        name="first_norm",
    )(*map(at_rest, (tokens, gain)) if first else (tokens, gain))


def tables_kernel(lengths, freqs, cos, sin, starts):
    core = here()["c"]

    def places(shape, dim, base):
        r = lax.broadcasted_iota(jnp.int32, shape, dim) + base
        block = r >> 7
        block = jnp.where(core == 0, jnp.where(block < 2, block, block + 4), jnp.where(block < 2, block + 4, block))
        return (block << 7) + (r & 127)

    def begin(place):
        start = lengths[0] * 0
        result = jnp.zeros_like(place)
        for i in range(5):
            end = start + lengths[i]
            result = jnp.where((place >= start) & (place < end), start, result)
            start = end
        return result

    for half in range(2):
        starts[half : half + 1, :] = begin(places((1, 256), 1, 256 * half))
    place = places((4 * TOK, 1), 0, 0)
    inside = place - begin(place)
    offset = jnp.maximum(inside - 1, 0)
    lane = lax.broadcasted_iota(jnp.int32, (4 * TOK, TOK), 1)
    rows = (offset >> 4).astype(F32)
    columns = (offset & (GRID - 1)).astype(F32)
    angles = jnp.where((lane & 63) < 32, rows, columns) * freqs[...]
    angles = jnp.where(inside > 0, angles, 0.0)
    cos[...] = jnp.cos(angles)
    sin[...] = jnp.where((lane & 1) == 0, -1.0, 1.0) * jnp.sin(angles)


def tables(lengths):
    freqs = 10000.0 ** (-4.0 * np.arange(HEAD_DIM // 4, dtype=np.float32) / HEAD_DIM)
    freqs = np.tile(np.repeat(freqs.astype(np.float32), 2), 4)[None, :]
    return pl.pallas_call(
        tables_kernel,
        out_shape=[sds((4 * TOK, TOK), F32), sds((4 * TOK, TOK), F32), sds((2, 256), jnp.int32)],
        in_specs=[SMEM, VMEM],
        out_specs=[VMEM] * 3,
        compiler_params=pltpu.CompilerParams(vmem_limit_bytes=4 * MIB),
        cost_estimate=pl.CostEstimate(flops=0, bytes_accessed=0, transcendentals=0),
        name="tables",
    )(lengths, jnp.asarray(freqs))


def own_heads_kernel(wq, wk, wv, out, bq, bk, bv, sems):
    x = here()["x"]
    start = pl.multiple_of((x * GROUP // TOK) * TOK, TOK)
    copies = [
        pltpu.make_async_copy(w.at[:, :, pl.ds(start, 2 * TOK)], buf, sems.at[i])
        for i, (w, buf) in enumerate(((wk, bk), (wv, bv), (wq, bq)))
    ]
    for copy in copies:
        copy.start()
    for i, (copy, buf) in enumerate(zip(copies, (bk, bv, bq))):
        copy.wait()
        for layer in range(2):
            w = buf[layer]
            out[layer, :, GROUP * i : GROUP * i + GROUP] = jnp.where(lax.rem(x, 2) == 0, w[:, :GROUP], w[:, 64:])


def own_heads(wq, wk, wv):
    return pl.pallas_call(
        own_heads_kernel,
        out_shape=sds((2, D, 3 * GROUP), BF),
        in_specs=[HBM] * 3,
        out_specs=VMEM,
        scratch_shapes=[pltpu.VMEM((2, D, 2 * TOK), BF)] * 3 + [pltpu.SemaphoreType.DMA((3,))],
        compiler_params=pltpu.CompilerParams(vmem_limit_bytes=8 * MIB),
        cost_estimate=pl.CostEstimate(flops=0, bytes_accessed=0, transcendentals=0),
        name="own_heads",
    )(*map(at_rest, (wq, wk, wv)))


def turn_group(values, cos, sin):
    lane = lax.broadcasted_iota(jnp.int32, (values.shape[0], 128), 1)
    even = lane % 2 == 0
    tail = jnp.concatenate([values[:, 128:], jnp.zeros((values.shape[0], 64), F32)], axis=1)
    parts = []
    for v in (values[:, :128], tail):
        swapped = jnp.where(even, pltpu.roll(v, 127, 1), pltpu.roll(v, 1, 1))
        parts.append(v * cos + swapped * sin)
    return jnp.concatenate([parts[0], parts[1][:, :64]], axis=1)


def project_kernel(depth, n0, n1, n2, n3, w, cos, sin, q, own, rows_out, rows, sem):
    ordered_by_x(here()["x"], (n0, n1, n2, n3), rows)
    store = pltpu.make_async_copy(rows, rows_out, sem)
    store.start()
    normed = rows[...].reshape(4 * TOK, D)
    y = mm(normed, w[depth])
    own[:, :GROUP] = turn_group(y[:, :GROUP], cos[...], sin[...]).astype(BF)
    own[:, GROUP:] = y[:, GROUP : 2 * GROUP].astype(BF)
    q[...] = turn_group(y[:, 2 * GROUP :], cos[...], sin[...]).astype(BF)
    store.wait()


def project(depth, normed, w, cos, sin):
    return pl.pallas_call(
        lambda *refs: project_kernel(depth, *refs),
        out_shape=[sds((4 * TOK, GROUP), BF), sds((4 * TOK, 2 * GROUP), BF), stored((4, TOK, D), BF)],
        in_specs=[VMEM] * 7,
        out_specs=[VMEM] * 2 + [HBM],
        scratch_shapes=[pltpu.VMEM((4, TOK, D), BF), pltpu.SemaphoreType.DMA(())],
        compiler_params=pltpu.CompilerParams(vmem_limit_bytes=8 * MIB),
        cost_estimate=pl.CostEstimate(flops=0, bytes_accessed=0, transcendentals=0),
        name="project",
    )(*normed, w, cos, sin)


def tile_scores(q, k, start, place0, n):
    raw = mm_rt(k, q)
    keys = lax.broadcasted_iota(jnp.int32, (256, 256), 0)
    asks = lax.broadcasted_iota(jnp.int32, (256, 256), 1)
    parts = []
    for at in range(0, n, 256):
        allowed = keys >= start - at
        if at == place0:
            allowed = allowed & (keys <= asks)
        parts.append(jnp.where(allowed, raw[at : at + 256], -1e30))
    return parts[0] if len(parts) == 1 else jnp.concatenate(parts, axis=0)


def attend_kernel(depth, q, own, sib, starts, m0, m1, m2, m3, q_out, kv_out, lse_out, mixed, *rest):
    spot = here()
    core, mine = spot["c"], spot["x"]
    if depth == 0:
        kv, lse, sems = rest
        stores = [
            pltpu.make_async_copy(source, out, sems.at[i])
            for i, (source, out) in enumerate(((q, q_out), (kv, kv_out), (lse, lse_out)))
        ]
        stores[0].start()
    else:
        kv, lse, stores = kv_out, lse_out, []
        q_out[...] = q[...]

    @pl.when(core == 0)
    def _():
        kv[0:256, :] = own[0:256, :]
        kv[256:512, :] = sib[256:512, :]
        kv[512:768, :] = sib[0:256, :]
        kv[768:1024, :] = own[256:512, :]

    @pl.when(core == 1)
    def _():
        kv[0:256, :] = sib[0:256, :]
        kv[256:512, :] = own[256:512, :]
        kv[512:768, :] = own[0:256, :]
        kv[768:1024, :] = sib[256:512, :]

    if stores:
        stores[1].start()

    def tile(which, pos):
        n = 256 * (pos + 1)
        outs = []
        start = starts[which : which + 1, :]
        for h in range(3):
            qs = q[256 * which : 256 * which + 256, 64 * h : 64 * h + 64] * jnp.asarray(0.125, BF)
            s = tile_scores(qs, kv[0:n, 64 * h : 64 * h + 64], start, 256 * pos, n)
            top = jnp.max(s, axis=0, keepdims=True)
            e = jnp.exp(s - top)
            total = jnp.sum(e, axis=0, keepdims=True)
            probs = (e * (1.0 / total)).astype(BF)
            lse[3 * which + h : 3 * which + h + 1, :] = top + jnp.log(total)
            outs.append(mm_lt(kv[0:n, GROUP + 64 * h : GROUP + 64 * h + 64], probs))
        out = jnp.concatenate(outs, axis=0).T.astype(BF)
        mixed[2 * which] = out[:TOK]
        mixed[2 * which + 1] = out[TOK:]

    @pl.when(core == 0)
    def _():
        tile(0, 0)
        tile(1, 3)

    @pl.when(core == 1)
    def _():
        tile(0, 2)
        tile(1, 1)

    if stores:
        stores[2].start()
    for d, m in enumerate((m0, m1, m2, m3)):
        m[...] = mixed[lax.rem(mine + d, 4)]
    for store in stores:
        store.wait()


def attend(depth, q, own, sib, starts):
    keep = sds if depth else stored
    return pl.pallas_call(
        lambda *refs: attend_kernel(depth, *refs),
        out_shape=[sds((TOK, GROUP), BF)] * 4
        + [keep((4 * TOK, GROUP), BF), keep((ROW, 2 * GROUP), BF), keep((8, 256), F32)],
        in_specs=[VMEM] * 4,
        out_specs=[VMEM] * 4 + [VMEM if depth else HBM] * 3,
        scratch_shapes=[pltpu.VMEM((4, TOK, GROUP), BF)]
        + (
            []
            if depth
            else [pltpu.VMEM((ROW, 2 * GROUP), BF), pltpu.VMEM((8, 256), F32), pltpu.SemaphoreType.DMA((3,))]
        ),
        compiler_params=pltpu.CompilerParams(vmem_limit_bytes=8 * MIB),
        cost_estimate=pl.CostEstimate(flops=0, bytes_accessed=0, transcendentals=0),
        name="attend",
    )(q, own, sib, starts)


def feed_kernel(
    depth, x, gain, next_gain, b0, b1, b2, b3, wo, wg, wu, wd,
    result, normed_next, acts_out, middle_out, slopes_out,
    groups, acts, middle_b, slopes, sems, *own,
):
    if own:
        copies = [
            pltpu.make_async_copy(w.at[depth], buf, sems.at[3 + i]) for i, (w, buf) in enumerate(zip((wo, wd), own))
        ]
        for copy in copies:
            copy.start()
    stores = [pltpu.make_async_copy(acts, acts_out, sems.at[0])]
    if depth == 0:
        stores += [
            pltpu.make_async_copy(source, out, sems.at[i])
            for i, (source, out) in ((1, (middle_b, middle_out)), (2, (slopes, slopes_out)))
        ]
    else:
        middle_b, slopes = middle_out, slopes_out
    ordered_by_x(here()["x"], (b0, b1, b2, b3), groups)
    mixed = jnp.concatenate([groups[g] for g in range(4)], axis=1)
    acts[:, D : 2 * D] = mixed
    if own:
        copies[0].wait()
    middle = x[...] + mm(mixed, own[0][...] if own else wo[depth])
    middle_b[...] = middle
    if depth == 0:
        stores[1].start()
    normed2 = (middle * norm_factor(middle) * gain[depth : depth + 1, :]).astype(BF)
    acts[:, :D] = normed2
    gate = mm(normed2, wg[depth])
    sigma = 1.0 / (1.0 + jnp.exp(-gate))
    swish = gate * sigma
    up = mm(normed2, wu[depth])
    hidden = (swish * up).astype(BF)
    acts[:, 2 * D :] = hidden
    stores[0].start()
    slopes[:, :FF] = (up * sigma * (1.0 + gate * (1.0 - sigma))).astype(BF)
    slopes[:, FF:] = swish.astype(BF)
    if depth == 0:
        stores[2].start()
    if own:
        copies[1].wait()
    values = middle + mm(hidden, own[1][...] if own else wd[depth])
    if depth == 0:
        result[...] = values
        normed_next[...] = (values * norm_factor(values) * next_gain[1:2, :]).astype(BF)
    else:
        result[...] = values.astype(BF)
        normed_next[...] = jnp.zeros((TOK, D), BF)
    for store in stores:
        store.wait()


def feed(depth, x, gain, next_gain, blocks, wo, wg, wu, wd):
    keep = sds if depth else stored
    return pl.pallas_call(
        lambda *refs: feed_kernel(depth, *refs),
        out_shape=[
            sds((TOK, D), BF if depth else F32), sds((TOK, D), BF),
            stored((TOK, 2 * D + FF), BF), *(keep((TOK, D), F32), keep((TOK, 2 * FF), BF)),
        ],
        in_specs=[VMEM] * 7 + [VMEM if depth else HBM, VMEM, VMEM, VMEM if depth else HBM],
        out_specs=[VMEM] * 2 + [HBM] + [VMEM if depth else HBM] * 2,
        scratch_shapes=[
            pltpu.VMEM((4, TOK, GROUP), BF),
            pltpu.VMEM((TOK, 2 * D + FF), BF),
            pltpu.VMEM((TOK, D), F32),
            pltpu.VMEM((TOK, 2 * FF), BF),
            pltpu.SemaphoreType.DMA((5,)),
        ]
        + ([] if depth else [pltpu.VMEM((D, D), BF), pltpu.VMEM((FF, D), BF)]),
        compiler_params=pltpu.CompilerParams(vmem_limit_bytes=(12 if depth else 16) * MIB),
        cost_estimate=pl.CostEstimate(flops=0, bytes_accessed=0, transcendentals=0),
        name="feed",
    )(x, gain, next_gain, *blocks, *(pinned(wo, wg, wu, wd) if depth else (at_rest(wo), *pinned(wg, wu), at_rest(wd))))


def feed_back_kernel(
    depth, carried, grad, middle, slopes, gain, wd, wg, wu, wo, *refs,
):
    acts = refs[:carried]
    right_ref, dmid_ref, o0, o1, o2, o3, groups, sems = refs[carried:]
    width = 2 * FF + 2 * D
    carries = [
        pltpu.make_async_copy(source, right_ref.at[:, pl.ds(width + i * (2 * D + FF), 2 * D + FF)], sems.at[i])
        for i, source in enumerate(acts)
    ]
    slopes_b, middle_b = slopes, middle
    for carry in carries:
        carry.start()
    g = grad[...].astype(F32)
    gb = g.astype(BF)
    right_ref[:, 2 * FF : 2 * FF + D] = gb
    dhidden = mm_rt(gb, wd[depth])
    dgate = (dhidden * slopes_b[:, :FF]).astype(BF)
    dup = (dhidden * slopes_b[:, FF:]).astype(BF)
    right_ref[:, :FF] = dgate
    right_ref[:, FF : 2 * FF] = dup
    dn = mm_rt(dgate, wg[depth]) + mm_rt(dup, wu[depth])
    mid = middle_b[...]
    factor = norm_factor(mid)
    s = mid * factor
    inner = dn * gain[depth : depth + 1, :]
    dmid = g + factor * (inner - s * jnp.mean(inner * s, axis=-1, keepdims=True))
    dmid_ref[...] = dmid
    dmb = dmid.astype(BF)
    right_ref[:, 2 * FF + D : width] = dmb
    dmixed = mm_rt(dmb, wo[depth]).astype(BF)
    for j in range(4):
        groups[j] = dmixed[:, GROUP * j : GROUP * j + GROUP]
    mine = here()["x"]
    for d, o in enumerate((o0, o1, o2, o3)):
        o[...] = groups[lax.rem(mine + d, 4)]
    for carry in carries:
        carry.wait()


def feed_back(depth, grad, middle, slopes, gain, wd, wg, wu, wo, acts):
    width = 2 * FF + 2 * D + len(acts) * (2 * D + FF)
    return pl.pallas_call(
        lambda *refs: feed_back_kernel(depth, len(acts), *refs),
        out_shape=[sds((TOK, width), BF), sds((TOK, D), F32)] + [sds((TOK, GROUP), BF)] * 4,
        in_specs=[VMEM] * 8 + [HBM] * len(acts),
        out_specs=[VMEM] * 6,
        scratch_shapes=[
            pltpu.VMEM((4, TOK, GROUP), BF),
            pltpu.SemaphoreType.DMA((4,)),
        ],
        compiler_params=pltpu.CompilerParams(vmem_limit_bytes=12 * MIB),
        cost_estimate=pl.CostEstimate(flops=0, bytes_accessed=0, transcendentals=0),
        name="feed_back",
    )(grad, middle, slopes, gain, *pinned(wd, wg, wu, wo), *map(at_rest, acts))


def attend_back_kernel(q, kv, starts, lse, b0, b1, b2, b3, dq, own, sib, dout, dk, dv):
    spot = here()
    core, mine = spot["c"], spot["x"]
    for d, b in enumerate((b0, b1, b2, b3)):
        rows = pl.ds(pl.multiple_of(lax.rem(mine - d + 4, 4) * TOK, TOK), TOK)
        dout[rows, :] = b[...]

    def tile(which, pos, first):
        n = 256 * (pos + 1)
        start = starts[which : which + 1, :]
        dqs = []
        for h in range(3):
            lanes = slice(64 * h, 64 * h + 64)
            qs = q[256 * which : 256 * which + 256, lanes] * jnp.asarray(0.125, BF)
            do = dout[256 * which : 256 * which + 256, lanes]
            k = kv[0:n, lanes]
            v = kv[0:n, GROUP + 64 * h : GROUP + 64 * h + 64]
            s = tile_scores(qs, k, start, 256 * pos, n)
            p = jnp.exp(s - lse[3 * which + h : 3 * which + h + 1, :])
            dp = mm_rt(v, do)
            delta = jnp.sum(p * dp, axis=0, keepdims=True)
            ds = (p * (dp - delta)).astype(BF)
            dk_h = mm(ds, qs)
            dv_h = mm(p.astype(BF), do)
            if first:
                dk[0:n, lanes] = dk_h
                dv[0:n, lanes] = dv_h
            else:
                dk[0:n, lanes] += dk_h
                dv[0:n, lanes] += dv_h
            dqs.append(mm_lt(k, ds))
        out = jnp.concatenate(dqs, axis=0).T * 0.125
        dq[256 * which : 256 * which + 256, :] = out

    def put(target, rows, tile_no):
        target[rows : rows + 256, :GROUP] = dk[256 * tile_no : 256 * tile_no + 256, :].astype(target.dtype)
        target[rows : rows + 256, GROUP:] = dv[256 * tile_no : 256 * tile_no + 256, :].astype(target.dtype)

    @pl.when(core == 0)
    def _():
        tile(1, 3, True)
        tile(0, 0, False)
        put(own, 0, 0)
        put(sib, 256, 1)
        put(sib, 0, 2)
        put(own, 256, 3)

    @pl.when(core == 1)
    def _():
        tile(0, 2, True)
        tile(1, 1, False)
        dk[768:1024, :] = jnp.zeros((256, GROUP), F32)
        dv[768:1024, :] = jnp.zeros((256, GROUP), F32)
        put(sib, 0, 0)
        put(own, 256, 1)
        put(own, 0, 2)
        put(sib, 256, 3)


def attend_back(q, kv, starts, lse, blocks):
    return pl.pallas_call(
        attend_back_kernel,
        out_shape=[sds((4 * TOK, GROUP), F32), sds((4 * TOK, 2 * GROUP), F32), sds((4 * TOK, 2 * GROUP), BF)],
        in_specs=[VMEM] * 8,
        out_specs=[VMEM] * 3,
        scratch_shapes=[
            pltpu.VMEM((4 * TOK, GROUP), BF),
            pltpu.VMEM((ROW, GROUP), F32),
            pltpu.VMEM((ROW, GROUP), F32),
        ],
        compiler_params=pltpu.CompilerParams(vmem_limit_bytes=10 * MIB),
        cost_estimate=pl.CostEstimate(flops=0, bytes_accessed=0, transcendentals=0),
        name="attend_back",
    )(q, kv, starts, lse, *blocks)


def spread_kernel(depth, dq, own, got, cos, sin, w, right, *refs):
    right[:, : GROUP] = turn_group(own[:, :GROUP] + got[:, :GROUP].astype(F32), cos[...], -sin[...]).astype(BF)
    right[:, GROUP : 2 * GROUP] = (own[:, GROUP:] + got[:, GROUP:].astype(F32)).astype(BF)
    right[:, 2 * GROUP : 3 * GROUP] = turn_group(dq[...], cos[...], -sin[...]).astype(BF)
    right[:, 3 * GROUP :] = jnp.zeros((4 * TOK, 64), BF)
    da = mm_rt(right[:, : 3 * GROUP], w[depth]).astype(BF)
    spot = here()
    if depth == 1:
        groups = refs[-1]
        groups[...] = da.reshape(4, TOK, D)
        for d, o in enumerate(refs[:4]):
            o[...] = groups[lax.rem(spot["x"] + d, 4)]
    else:
        (stack,) = refs
        for x in range(4):
            rank = rank_of(1 - spot["c"], x)
            for t in range(6):
                rows = pl.ds(pl.multiple_of((4 * t + rank) * TOK, TOK), TOK)
                stack[rows, :] = da[TOK * x : TOK * x + TOK, TOK * t : TOK * t + TOK]


def spread(depth, dq, own, got, cos, sin, w):
    shapes = [sds((TOK, D), BF)] * 4 if depth == 1 else [sds((6 * 4 * TOK, TOK), BF)]
    right, *blocks = pl.pallas_call(
        lambda *refs: spread_kernel(depth, *refs),
        out_shape=[sds((4 * TOK, 3 * GROUP + 64), BF)] + shapes,
        in_specs=[VMEM] * 6,
        out_specs=[VMEM] * (1 + len(shapes)),
        scratch_shapes=[pltpu.VMEM((4, TOK, D), BF)] if depth == 1 else [],
        compiler_params=pltpu.CompilerParams(vmem_limit_bytes=8 * MIB),
        cost_estimate=pl.CostEstimate(flops=0, bytes_accessed=0, transcendentals=0),
        name="spread",
    )(dq, own, got, cos, sin, w)
    return right, blocks


def norm_back(da, dmid, x, gain):
    factor = norm_factor(x)
    s = x * factor
    inner = da * gain
    return dmid + factor * (inner - s * jnp.mean(inner * s, axis=-1, keepdims=True))


def project_back_kernel(dmid, x, gain, b0, b1, b2, b3, grad):
    da = b0[...].astype(F32) + b1[...].astype(F32) + b2[...].astype(F32) + b3[...].astype(F32)
    grad[...] = norm_back(da, dmid[...], x[...], gain[1:2, :])


def project_back(dmid, x, gain, blocks):
    return pl.pallas_call(
        project_back_kernel,
        out_shape=sds((TOK, D), F32),
        in_specs=[VMEM] * 7,
        out_specs=VMEM,
        compiler_params=pltpu.CompilerParams(vmem_limit_bytes=6 * MIB),
        cost_estimate=pl.CostEstimate(flops=0, bytes_accessed=0, transcendentals=0),
        name="project_back",
    )(dmid, x, gain, *blocks)


def last_grad_kernel(offset, kept, got, dmid, x, gain, activations, back):
    parts = []
    for t in range(6):
        rows = slice(TOK * t, TOK * t + TOK)
        parts.append(kept[rows, :].astype(F32) + got[offset + TOK * t : offset + TOK * t + TOK, :].astype(F32))
    da = jnp.concatenate(parts, axis=1)
    back[:TOK, :] = norm_back(da, dmid[...], x[...], gain[0:1, :]).astype(BF)
    back[TOK:, :] = activations[...]


def last_grad(member, dmid, x, gain, activations):
    return pl.pallas_call(
        lambda *refs: last_grad_kernel(member.offset, *refs),
        out_shape=sds((2 * TOK, D), BF),
        in_specs=[VMEM] * 6,
        out_specs=VMEM,
        compiler_params=pltpu.CompilerParams(vmem_limit_bytes=6 * MIB),
        cost_estimate=pl.CostEstimate(flops=0, bytes_accessed=0, transcendentals=0),
        name="last_grad",
    )(member.kept, member.got, dmid, x, gain, activations)


def exchange_x(blocks):
    return (blocks[0],) + tuple(send(blocks[d], SHIFT_X[d]) for d in (1, 2, 3))


def left_kernel(jobs, right, right_sib, both, turned):
    mine = here()["c"]
    row = 0
    for first, columns, axes, swapped in jobs:
        hot = one_hot(axes, mine, swapped) if columns == D else None
        for side, source in enumerate((right, right_sib)):
            lanes = slice(TOK * side, TOK * side + TOK)
            if hot is None:
                turned[...] = source[:, first : first + FF].T.reshape(FF // 16, 16, TOK)
                half = block_order(axes, swapped).reshape(2, 64)
                for i in range(64):
                    block = jnp.where(mine == 0, int(half[0, i]), int(half[1, i]))
                    both[row + 16 * i : row + 16 * i + 16, lanes] = turned[block]
            else:
                both[row : row + D // 2, lanes] = mm_rt(hot, source[:, first : first + D]).astype(BF)
        row += columns // 2


def left_sides(right, right_sib, jobs):
    rows = sum(columns // 2 for _, columns, _, _ in jobs)
    return pl.pallas_call(
        lambda *refs: left_kernel(jobs, *refs),
        out_shape=sds((rows, 2 * TOK), BF),
        in_specs=[VMEM] * 2,
        out_specs=VMEM,
        scratch_shapes=[pltpu.VMEM((FF // 16, 16, TOK), BF)],
        compiler_params=pltpu.CompilerParams(vmem_limit_bytes=8 * MIB),
        cost_estimate=pl.CostEstimate(flops=0, bytes_accessed=0, transcendentals=0),
        name="left_sides",
    )(right, right_sib)


def along_kernel(rows, along):
    normed = rows[...].reshape(4 * TOK, D)
    for side in range(2):
        along[D // 2 * side : D // 2 * side + D // 2, :] = mm_rt(one_hot("yzx", side, "yz"), normed).astype(BF)


def left_along(rows):
    return pl.pallas_call(
        along_kernel,
        out_shape=sds((D, 4 * TOK), BF),
        in_specs=[VMEM],
        out_specs=VMEM,
        compiler_params=pltpu.CompilerParams(vmem_limit_bytes=8 * MIB),
        cost_estimate=pl.CostEstimate(flops=0, bytes_accessed=0, transcendentals=0),
        name="left_along",
    )(rows)


def rows_kernel(wq, wk, wv, wg, wu, na, nf, rq, rk, rv, rg, ru, gains, bq, bk, bv, bg, bu, sems):
    first = here()["flat"] * 6
    start = pl.multiple_of(jnp.minimum((first >> 4) << 4, D - 32), 16)
    copies = [
        pltpu.make_async_copy(w.at[:, pl.ds(start, 32), :], buf, sems.at[i])
        for i, (w, buf) in enumerate(((wq, bq), (wk, bk), (wv, bv), (wg, bg), (wu, bu)))
    ]
    for copy in copies:
        copy.start()
    lane = lax.broadcasted_iota(jnp.int32, (8, D), 1)
    pick = lane == lax.broadcasted_iota(jnp.int32, (8, D), 0) + first
    column = lax.broadcasted_iota(jnp.int32, (8, TOK), 1)
    result = jnp.ones((8, TOK), F32)
    for i, row in enumerate((na[0:1, :], na[1:2, :], nf[0:1, :], nf[1:2, :])):
        value = jnp.sum(jnp.where(pick, row, 0.0), axis=1, keepdims=True)
        result = jnp.where(column == i, value, result)
    gains[...] = result
    place = lax.broadcasted_iota(jnp.int32, (8, 32), 1)
    hot = jnp.where(place == lax.broadcasted_iota(jnp.int32, (8, 32), 0) + (first - start), 1.0, 0.0).astype(BF)
    for copy, buf, out in zip(copies, (bq, bk, bv, bg, bu), (rq, rk, rv, rg, ru)):
        copy.wait()
        for layer in range(2):
            out[layer] = mm(hot, buf[layer])


def own_rows(wq, wk, wv, wg, wu, na, nf):
    return pl.pallas_call(
        rows_kernel,
        out_shape=[stored((2, 8, D), F32)] * 3 + [stored((2, 8, FF), F32)] * 2 + [stored((8, TOK), F32)],
        in_specs=[HBM] * 5 + [VMEM] * 2,
        out_specs=[VMEM] * 6,
        scratch_shapes=[pltpu.VMEM((2, 32, D), BF)] * 3
        + [pltpu.VMEM((2, 32, FF), BF)] * 2
        + [pltpu.SemaphoreType.DMA((5,))],
        compiler_params=pltpu.CompilerParams(vmem_limit_bytes=6 * MIB),
        cost_estimate=pl.CostEstimate(flops=0, bytes_accessed=0, transcendentals=0),
        name="own_rows",
    )(*map(at_rest, (wq, wk, wv, wg, wu)), na, nf)


def slot(rows):
    return -(-rows // 16) * 16


class Member:
    def __init__(self, kept, rows, tiles, offset):
        self.kept, self.rows, self.tiles, self.offset = kept, rows, tiles, offset
        self.got = None


def for_tiles(tiles, body):
    if tiles <= 6:
        for t in range(tiles):
            body(t)
    else:
        @pl.loop(0, tiles // 2)
        def _(i):
            body(2 * i)
            body(2 * i + 1)


def aligned(value):
    return value if isinstance(value, int) else pl.multiple_of(value, 16)


def bit_of(spot, which):
    if which == "c":
        return spot["c"]
    axis, step = which[0], which[1]
    rank = rank_of(1 - spot["c"] if len(which) > 2 else spot["c"], spot[axis])
    return rank // 2 if step == 0 else lax.rem(rank, 2)


def sums_kernel(tasks, *refs):
    spot = here()
    for task in tasks:
        kind, bit = task["kind"], bit_of(spot, task["bit"])
        pack, offset, kept_ref = refs[task["pack"]], task["offset"], refs[task["kept"]]
        half, tiles = task["half"], task["tiles"]
        out_slot = slot(half)
        if kind == "weights":
            left, right, right_sib = (refs[i] for i in task["ins"])
            lhs = jnp.concatenate(
                [left[pl.ds(pl.multiple_of(task["row"] + side * half, 64), half), :] for side in (1 - bit, bit)], axis=0
            )
            for t in range(0, tiles, 2):
                col = task["column"] + TOK * t
                rhs = jnp.concatenate([right[:, col : col + 2 * TOK], right_sib[:, col : col + 2 * TOK]], axis=0)
                part = mm(lhs, rhs).astype(BF)
                for out, base, rows in ((pack, offset, part[:half]), (kept_ref, 0, part[half:])):
                    out[base + t * half : base + (t + 1) * half, :] = rows[:, :TOK]
                    out[base + (t + 1) * half : base + (t + 2) * half, :] = rows[:, TOK:]
        elif kind == "along":
            left, right = (refs[i] for i in task["ins"])
            lhs = jnp.concatenate(
                [left[pl.ds(pl.multiple_of(side * half, 64), half), :] for side in (1 - bit, bit)], axis=0
            )
            part = mm(lhs, right[...]).astype(BF)
            for out, base, rows in ((pack, offset, part[:half]), (kept_ref, 0, part[half:])):
                for t in range(tiles):
                    out[base + t * half : base + (t + 1) * half, :] = rows[:, TOK * t : TOK * t + TOK]
        elif kind == "first":
            value, base, in_slot = refs[task["ins"][0]], task["came"], slot(2 * half)
            for t in range(tiles):
                at = base + t * in_slot
                if half % 16 == 0:
                    pack[offset + t * out_slot : offset + t * out_slot + half, :] = value[
                        pl.ds(pl.multiple_of(at + (1 - bit) * half, 16), half), :
                    ]
                    kept_ref[t * out_slot : t * out_slot + half, :] = value[
                        pl.ds(pl.multiple_of(at + bit * half, 16), half), :
                    ]
                else:
                    both = value[at : at + 2 * half, :].astype(F32)
                    low, high = both[:half], both[half:]
                    pack[offset + t * out_slot : offset + t * out_slot + half, :] = jnp.where(bit == 0, high, low).astype(BF)
                    kept_ref[t * out_slot : t * out_slot + half, :] = jnp.where(bit == 0, low, high).astype(BF)
        else:
            value, got = (refs[i] for i in task["ins"])
            came, in_slot = task["came"], slot(2 * half)

            def one(t, half=half, out_slot=out_slot, in_slot=in_slot, came=came, offset=offset, bit=bit,
                    value=value, got=got, pack=pack, kept_ref=kept_ref):
                if half % 16 == 0:
                    for out, base, side in ((pack, offset, 1 - bit), (kept_ref, 0, bit)):
                        at = t * in_slot + side * half
                        total = (
                            value[pl.ds(pl.multiple_of(at, 16), half), :].astype(F32)
                            + got[pl.ds(pl.multiple_of(came + at, 16), half), :].astype(F32)
                        )
                        out[pl.ds(aligned(base + t * out_slot), half), :] = total.astype(BF)
                else:
                    total = (
                        value[pl.ds(aligned(t * in_slot), 2 * half), :].astype(F32)
                        + got[pl.ds(aligned(came + t * in_slot), 2 * half), :].astype(F32)
                    )
                    low, high = total[:half], total[half:]
                    pack[pl.ds(aligned(offset + t * out_slot), half), :] = jnp.where(bit == 0, high, low).astype(BF)
                    kept_ref[pl.ds(aligned(t * out_slot), half), :] = jnp.where(bit == 0, low, high).astype(BF)

            for_tiles(tiles, one)


def sums(jobs):
    arrays, tasks, pack_rows = [], [], {}

    def at(array):
        for i, a in enumerate(arrays):
            if a is array:
                return i
        arrays.append(array)
        return len(arrays) - 1

    flops = 0
    for job in jobs:
        if job[0] == "weights":
            _, left, row, rows, right, right_sib, column, columns, bit, pack = job
            task = dict(kind="weights", ins=[at(left), at(right), at(right_sib)], row=row, column=column,
                        half=rows // 2, tiles=columns // TOK, bit=bit)
            flops += 4 * rows * columns * TOK
        elif job[0] == "along":
            _, left, right, pack = job
            task = dict(kind="along", ins=[at(left), at(right)], half=D // 2, tiles=right.shape[1] // TOK, bit="c")
            flops += 2 * D * right.shape[1] * 4 * TOK
        elif job[0] == "first":
            _, array, base, rows, tiles, bit, pack = job
            task = dict(kind="first", ins=[at(array)], came=base, half=rows // 2, tiles=tiles, bit=bit)
        else:
            _, member, bit, pack = job
            task = dict(kind="step", ins=[at(member.kept), at(member.got)], came=member.offset,
                        half=member.rows // 2, tiles=member.tiles, bit=bit)
        task["pack"], task["offset"] = pack, pack_rows.get(pack, 0)
        pack_rows[pack] = task["offset"] + task["tiles"] * slot(task["half"])
        tasks.append(task)
    names = sorted(pack_rows)
    shapes = [sds((pack_rows[n], TOK), BF) for n in names]
    for i, task in enumerate(tasks):
        task["kept"] = len(arrays) + len(names) + i
        task["pack"] = len(arrays) + names.index(task["pack"])
        shapes.append(sds((task["tiles"] * slot(task["half"]), TOK), BF))
    moved = sum(a.size for a in arrays) + sum(np.prod(s.shape) for s in shapes)
    outs = pl.pallas_call(
        lambda *refs: sums_kernel(tasks, *refs),
        out_shape=shapes,
        in_specs=[VMEM] * len(arrays),
        out_specs=[VMEM] * len(shapes),
        compiler_params=pltpu.CompilerParams(vmem_limit_bytes=10 * MIB),
        cost_estimate=pl.CostEstimate(flops=0, bytes_accessed=0, transcendentals=0),
        name="sums",
    )(*arrays)
    packs = dict(zip(names, outs))
    members = [
        Member(kept, task["half"], task["tiles"], task["offset"]) for kept, task in zip(outs[len(names) :], tasks)
    ]
    return packs, members


def came(members, got):
    for member in members:
        member.got = got


def finish_kernel(plan, places, *refs):
    back, arrays = refs[6], refs[7:-12]
    acts, gtok, gq, gk, gv, go, ggate, gup, gdown, gattn, gffn, by_x = refs[-12:]
    wq, wk, wv, wg, wu, gains = refs[:6]
    gtok[...] = back[:TOK, :].astype(F32)
    acts[...] = back[TOK:, :]
    spot = here()
    mine = spot["x"]
    across, beside = 3 - mine, mine + 1 - 2 * lax.rem(mine, 2)
    first = jnp.where(spot["c"] == 0, beside, across)
    second = jnp.where(spot["c"] == 0, across, beside)
    opposite = lax.rem(mine + 2, 4)
    for m in range(2):
        (kept, got, offset), (kept_b, got_b, offset_b) = places[m]
        for group, array, base in (
            (mine, kept, 0), (first, kept_b, 0), (second, got, offset), (opposite, got_b, offset_b)
        ):
            by_x[4 * m + group] = arrays[array][base : base + 80, :]

    def total(name):
        kept, got, offset, tiles, rows = plan[name]
        parts = []
        for t in range(tiles):
            parts.append(
                arrays[kept][16 * t : 16 * t + rows, :].astype(F32)
                + arrays[got][offset + 16 * t : offset + 16 * t + rows, :].astype(F32)
            )
        return jnp.concatenate(parts, axis=1)

    lane = lax.broadcasted_iota(jnp.int32, (8, TOK), 1)
    result = jnp.zeros((8, TOK), F32)
    filler = jnp.zeros((2, 1), F32)
    both = jnp.concatenate([total("gate0"), total("up0")], axis=1), total("gu1")
    gates = [b[:, :FF] for b in both]
    ups = [b[:, FF:] for b in both]
    for layer in range(2):
        ggate[:, layer, :] = gates[layer]
        gup[:, layer, :] = ups[layer]
        go[:, layer, :] = total(f"out{layer}")
        gdown[layer] = total(f"down{layer}")
    for layer in range(2):
        m = 1 - layer
        rows = [
            jnp.concatenate([by_x[4 * m + x, 16 * t : 16 * t + 6, :] for t in range(5)], axis=1) for x in range(4)
        ]
        acc = jnp.zeros((6, 1), F32)
        for i, (out, w) in enumerate(((gk, wk), (gv, wv), (gq, wq))):
            value = jnp.concatenate([r[:, GROUP * i : GROUP * i + GROUP] for r in rows], axis=1).astype(F32)
            out[:, layer, :] = value
            acc = acc + jnp.sum(value * w[layer][:6], axis=1, keepdims=True)
        result = jnp.where(lane == layer, jnp.concatenate([acc / gains[:6, layer : layer + 1], filler], axis=0), result)
        gate, up = gates[layer], ups[layer]
        acc = jnp.sum(gate * wg[layer][:6], axis=1, keepdims=True) + jnp.sum(
            up * wu[layer][:6], axis=1, keepdims=True
        )
        result = jnp.where(lane == 2 + layer, jnp.concatenate([acc / gains[:6, 2 + layer : 3 + layer], filler], axis=0), result)
    turned = result.T
    gattn[...] = turned[0:2, :6]
    gffn[...] = turned[2:4, :6]


def finish(rows_of, back, members, projections):
    arrays, plan = [], {}

    def at(array):
        for i, a in enumerate(arrays):
            if a is array:
                return i
        arrays.append(array)
        return len(arrays) - 1

    for name, m in members.items():
        plan[name] = (at(m.kept), at(m.got), m.offset, m.tiles, m.rows)
    places = [[(at(m.kept), at(m.got), m.offset) for m in pair] for pair in projections]
    return pl.pallas_call(
        lambda *refs: finish_kernel(plan, places, *refs),
        out_shape=[sds((TOK, D), BF), sds((TOK, D), F32)]
        + [sds((6, 2, D), F32)] * 4
        + [sds((6, 2, FF), F32)] * 2
        + [sds((2, 16, D), F32), sds((2, 6), F32), sds((2, 6), F32)],
        in_specs=[VMEM] * (7 + len(arrays)),
        out_specs=[VMEM] * 11,
        scratch_shapes=[pltpu.VMEM((8, 80, TOK), BF)],
        compiler_params=pltpu.CompilerParams(vmem_limit_bytes=8 * MIB),
        cost_estimate=pl.CostEstimate(flops=0, bytes_accessed=0, transcendentals=0),
        name="finish",
    )(*rows_of, back, *arrays)


def tie(value, *others):
    return lax.optimization_barrier((value,) + others)[0]


def per_device(
    tokens, seg_lengths, cotangent, norm_attn, w_query, w_key, w_value, w_out, norm_ffn, w_gate, w_up, w_down
):
    with jax.named_scope("S_setup"):
        _, early = first_norm(tokens[0], norm_attn, True)
        first_blocks = [send(early, GATHER[d]) for d in (1, 2, 3)]
        moved = send(tokens[0], RELOCATE)
        lengths = send(seg_lengths[0], RELOCATE)
        cot = send(cotangent[0], RELOCATE)
        x, normed = first_norm(moved, norm_attn)
        heads = own_heads(w_query, w_key, w_value)
        cos, sin, starts = tables(lengths)

    kept, carried, alongs = [], [], []
    for depth in range(2):
        with jax.named_scope(f"S_ahead{depth}"):
            blocks = exchange_x([normed] * 4) if depth else (normed, *first_blocks)
            if depth == 1:
                alongs.append(left_along(rows))
                cot = tie(cot, alongs[0])
                rows_of = own_rows(w_query, w_key, w_value, w_gate, w_up, norm_attn, norm_ffn)
                blocks = (tie(blocks[0], cot, *rows_of),) + tuple(blocks[1:])
            q, own, rows = project(depth, blocks, heads, cos, sin)
            sib = send(own, CORE)
            *blocks, q, kv, lse = attend(1, q, own, sib, starts)
            blocks = exchange_x(blocks)
            if depth == 1:
                alongs.append(left_along(rows))
                blocks = (tie(blocks[0], alongs[1]),) + tuple(blocks[1:])
            result, normed, acts, middle, slopes = feed(
                depth, x, norm_ffn, norm_attn, blocks, w_out, w_gate, w_up, w_down
            )
            kept.append((x, q, kv, lse, middle, slopes))
            carried.append(acts)
            x = result
    activations = x

    def step(members, bit, pack):
        return [("step", m, bit, pack) for m in members]

    half = D // 2
    x, q, kv, lse, middle, slopes = kept[1]
    with jax.named_scope("S_back1"):
        right, dmid, *blocks = feed_back(
            1, cot, middle, slopes, norm_ffn, w_down, w_gate, w_up, w_out, [carried[1], carried[0]]
        )
        blocks = exchange_x(blocks)
        right_sib = send(right, CORE)
    base1 = 2 * FF + 2 * D
    base0 = base1 + 2 * D + FF
    with jax.named_scope("S_back1"):
        left = left_sides(right, right_sib, [(base1, D, "yzx", "yz")])
        blocks = (tie(blocks[0], left),) + tuple(blocks[1:])
        dq, own, sib = attend_back(q, kv, starts, lse, blocks)
        right1, blocks = spread(1, dq, own, send(sib, CORE), cos, sin, heads)
        blocks = exchange_x(blocks)
    with jax.named_scope("S_sum1"):
        packs, (gu1,) = sums([("weights", left, 0, D // 2, tie(right, right1), right_sib, 0, 2 * FF, ("y", 0, "swapped"), "y")])
        came([gu1], send(packs["y"], PAIR["y", 1]))
        left = left_sides(
            right, right_sib,
            [
                (base0, D, "xzy", ""),
                (base0, D, "yzx", ""),
                (base0 + D, D, "xzy", ""),
                (base0 + 2 * D, FF, "zyx", ""),
                (base1 + D, D, "xzy", ""),
                (base1 + 2 * D, FF, "zyx", ""),
            ],
        )
        late, late_sib = right, right_sib
    with jax.named_scope("S_back1"):
        blocks = (tie(blocks[0], packs["y"]),) + tuple(blocks[1:])
        grad = project_back(dmid, x, norm_attn, blocks)

    x, q, kv, lse, middle, slopes = kept[0]
    with jax.named_scope("S_back0"):
        right, dmid, *blocks = feed_back(0, grad, middle, slopes, norm_ffn, w_down, w_gate, w_up, w_out, [])
        blocks = exchange_x(blocks)
        right_sib = send(right, CORE)
    with jax.named_scope("S_sum0"):
        packs, (gate0, up0, out0, down0, out1, down1, gu1) = sums(
            [
                ("weights", left, 0, D // 2, tie(right, *blocks), right_sib, 0, ALONG_X, ("x", 0), "x"),
                ("weights", left, half, D // 2, right, right_sib, ALONG_X, 2 * FF - ALONG_X, ("y", 0), "y"),
                ("weights", left, 2 * half, D // 2, right, right_sib, 2 * FF + D, D, ("x", 0), "x"),
                ("weights", left, 3 * half, FF // 2, right, right_sib, 2 * FF, D, ("z", 0), "z"),
                ("weights", left, 3 * half + FF // 2, D // 2, late, late_sib, 2 * FF + D, D, ("x", 0), "x"),
                ("weights", left, 4 * half + FF // 2, FF // 2, late, late_sib, 2 * FF, D, ("z", 0), "z"),
            ]
            + step([gu1], ("y", 1, "swapped"), "y")
        )
        came([gate0, out0, out1], send(packs["x"], PAIR["x", 0]))
        came([up0, gu1], send(packs["y"], PAIR["y", 0]))
        came([down0, down1], send(packs["z"], PAIR["z", 0]))
    with jax.named_scope("S_back0"):
        blocks = (tie(blocks[0], packs["x"], packs["y"], packs["z"]),) + tuple(blocks[1:])
        dq, own, sib = attend_back(q, kv, starts, lse, blocks)
        right0, (partial,) = spread(0, dq, own, send(sib, CORE), cos, sin, heads)

    with jax.named_scope("S_sum0"):
        packs, (qkv1, qkv0) = sums([("along", alongs[1], right1, "c"), ("along", alongs[0], right0, "c")])
        came([qkv1, qkv0], send(packs["c"], CORE))
        packs, (gate0, out0, out1, up0, down0, down1, gu1, qkv1, qkv0, da) = sums(
            step([gate0, out0, out1], ("x", 1), "x")
            + step([up0], ("y", 1), "y")
            + step([down0, down1], ("z", 1), "z")
            + step([gu1], ("z", 0, "swapped"), "z")
            + step([qkv1, qkv0], ("y", 0, "swapped"), "y")
            + [("first", partial, 0, 4 * TOK, 6, ("x", 0, "swapped"), "x")],
        )
        came([down0, down1, gu1], send(packs["z"], PAIR["z", 1]))
        came([gate0, out0, out1, da], send(packs["x"], PAIR["x", 1]))
        came([up0, qkv1, qkv0], send(packs["y"], PAIR["y", 1]))
        packs, (down0, down1, gate0, out0, out1, up0, gu1, qkv1, qkv0, da) = sums(
            step([down0, down1], ("y", 0), "y")
            + step([gate0, out0, out1, up0], ("z", 0), "z")
            + step([gu1], ("z", 1, "swapped"), "z")
            + step([qkv1, qkv0], ("y", 1, "swapped"), "y")
            + step([da], ("x", 1, "swapped"), "x"),
        )
        came([gate0, out0, out1, up0, gu1], send(packs["z"], PAIR["z", 0]))
        came([down0, down1, qkv1, qkv0], send(packs["y"], PAIR["y", 0]))
        came([da], send(packs["x"], PAIR["x", 0]))
        back = send(last_grad(da, dmid, x, norm_attn, activations), RESTORE)
        packs, (down0, down1, gate0, out0, out1, up0, qkv1, qkv0) = sums(
            step([down0, down1], ("y", 1), "y")
            + step([gate0, out0, out1, up0], ("z", 1), "z")
            + step([qkv1, qkv0], ("z", 0, "swapped"), "z"),
        )
        came([gate0, out0, out1, up0, qkv1, qkv0], send(packs["z"], PAIR["z", 1]))
        came([down0, down1], send(packs["y"], PAIR["y", 1]))
        packs, (gate0, out0, out1, qkv1, qkv0) = sums(
            step([gate0, out0, out1], ("y", 0), "y") + step([qkv1, qkv0], ("z", 1, "swapped"), "z")
        )
        came([gate0, out0, out1], send(packs["y"], PAIR["y", 0]))
        came([qkv1, qkv0], send(packs["z"], PAIR["z", 0]))
        packs, (gate0, out0, out1, up0, down0, down1, gu1, qkv1, qkv0) = sums(
            step([gate0, out0, out1], ("y", 1), "y")
            + step([up0, down0, down1, gu1, qkv1, qkv0], ("x", 0), "x"),
        )
        came([up0, down0, down1, gu1, qkv1, qkv0], send(packs["x"], PAIR["x", 0]))
        came([gate0, out0, out1], send(packs["y"], PAIR["y", 1]))
        gu1.kept = tie(gu1.kept, back)
        packs, (up0, down0, down1, gu1, mine1, first1, mine0, first0) = sums(
            step([up0, down0, down1, gu1], ("x", 1), "x")
            + [
                ("first", array, offset, 12, 5, ("x", 1), "x")
                for m in (qkv1, qkv0)
                for array, offset in ((m.kept, 0), (m.got, m.offset))
            ],
        )
        came([up0, down0, down1, gu1, mine1, first1, mine0, first0], send(packs["x"], PAIR["x", 1]))
        activations, grad_tokens, grad_q, grad_k, grad_v, grad_o, grad_gate, grad_up, grad_down, grad_attn, grad_ffn = finish(
            rows_of, back,
            dict(gate0=gate0, up0=up0, gu1=gu1, out0=out0, out1=out1, down0=down0, down1=down1),
            [(mine1, first1), (mine0, first0)],
        )
    return (
        activations[None],
        grad_tokens[None],
        grad_attn,
        jnp.swapaxes(grad_q, 0, 1),
        jnp.swapaxes(grad_k, 0, 1),
        jnp.swapaxes(grad_v, 0, 1),
        jnp.swapaxes(grad_o, 0, 1),
        grad_ffn,
        jnp.swapaxes(grad_gate, 0, 1),
        jnp.swapaxes(grad_up, 0, 1),
        grad_down,
    )


def solution(mesh):
    rows = P("batch", "seq", None)
    split = P(None, AXES)
    split3 = P(None, AXES, None)
    return jax.shard_map(
        per_device,
        mesh=mesh,
        in_specs=(rows, P("batch", None), rows) + (P(),) * 9,
        out_specs=(rows, rows, split, split3, split3, split3, split3, split, split3, split3, split3),
        check_vma=False,
    )
```
